32 devices in a mesh: shard: 2 (over y), ctx: 4 (over z), tp: 4 (over x, core).
Axes of the slice: x: 2, y: 2, z: 4, core: 2. Of those that a mesh axis runs over, the one named last changes fastest.
Arguments:
- tokens: bfloat16 [2, 1536, 2048], P('shard', 'ctx'), may hold values from -6 to 6
- segments: int32 [2, 1536], P('shard'), may hold values from 0 to 3, as said below
- routes: int32 [2, 1536, 8], P('shard', 'ctx'), may hold values from 0 to 15, all different within a row; in each aligned block of 384 rows (0 to 383, 384 to 767, ..., all dimensions but the last counted through in order) at most 240 rows name the same one
- cotangent: bfloat16 [2, 1536, 2048], P('shard', 'ctx'), may hold values from -6 to 6
- first_gain: bfloat16 [2048], P('shard'), may hold values from 0.099609375 to 1.8984375
- head_gain: bfloat16 [256], P('shard'), may hold values from 1 to 1.59375
- attention_in: bfloat16 [2048, 3, 2048], P('shard', None, 'tp'), may hold values from -0.125 to 0.125
- attention_out: bfloat16 [2048, 2048], P('shard', 'tp'), may hold values from -0.5 to 0.5
- second_gain: bfloat16 [2048], P('shard'), may hold values from 0.099609375 to 1.8984375
- router_weight: bfloat16 [2048, 16], P('shard'), may hold values from -0.0625 to 0.0625
- expert_in: bfloat16 [2048, 16, 2, 1024], P('shard', None, None, 'tp'), may hold values from -0.125 to 0.125
- expert_out: bfloat16 [2048, 16, 1024], P('shard', None, 'tp'), may hold values from -1.5 to 1.5
Outputs:
- layer_output: bfloat16 [2, 1536, 2048], P('shard', 'ctx')
- input_gradient: float32 [2, 1536, 2048], P('shard', 'ctx')
- first_gradient: float32 [2048], P('shard')
- head_gradient: float32 [256], P('shard')
- entry_gradient: float32 [2048, 3, 2048], P('shard', None, 'tp')
- exit_gradient: float32 [2048, 2048], P('shard', 'tp')
- second_gradient: float32 [2048], P('shard')
- router_gradient: float32 [2048, 16], P('shard')
- upward_gradient: float32 [2048, 16, 2, 1024], P('shard', None, None, 'tp')
- downward_gradient: float32 [2048, 16, 1024], P('shard', None, 'tp')
The draws below stay inside these ranges and needn't reach their ends.
Inputs may be any that keep to these rules, and one draw needn't show every extreme that they name: `segments`: within each pack the numbers never fall, each of 0 to 3 occurs, and one document, which one varies, starts among the pack's first 384 tokens and ends among its last 384. `routes`: each row names 8 different experts. Among the 384 rows of one index of ctx no expert is named by more than 240 rows, a bound that some block reaches.
All inputs are finite; a program needn't handle non-finite values.
Results may differ from the reference program's by a relative error of at most 0.017.
Values may be sent and summed in bfloat16 or wider, within the bound.
A program may use at most 576 MiB of HBM per device.

```python
import math
import jax
import jax.numpy as jnp
import numpy as np
from jax import lax

D = 2048
HEADS = 16
HEAD_DIM = 128
FF = 1024
EXPERTS = 16
TOPK = 8
DOCS = 4
TOK_DEV = 384
PACK = 1536
PACKS = 2
CAPACITY = 240


def one_pack_segments(key):
    key_long, key_short = jax.random.split(key)
    longest = jax.random.randint(key_long, (), 0, DOCS, dtype=jnp.int32)
    shorter = 1 + jax.random.randint(key_short, (DOCS - 1,), 0, TOK_DEV // 4 + 1, dtype=jnp.int32)
    places = jnp.arange(DOCS, dtype=jnp.int32)
    padded = jnp.concatenate([shorter, jnp.zeros((1,), jnp.int32)])
    shifted = jnp.concatenate([jnp.zeros((1,), jnp.int32), shorter])
    remain = PACK - jnp.sum(shorter)
    lengths = jnp.where(places < longest, padded, jnp.where(places > longest, shifted, remain))
    bounds = jnp.cumsum(lengths)[:DOCS - 1]
    spots = jnp.arange(PACK, dtype=jnp.int32)
    return jnp.sum((spots[:, None] >= bounds[None, :]).astype(jnp.int32), axis=1)


def draw_segments(key, part):
    key = jax.random.fold_in(key, 7)
    return jax.vmap(one_pack_segments)(jax.random.split(key, PACKS))


def block_levels(key, dims, cuts, low, top_value):
    def one(dim, shards_of):
        steps = jax.random.uniform(jax.random.fold_in(jax.random.fold_in(key, 6), dim), (shards_of,), jnp.float32, low / len(cuts), top_value / len(cuts))
        return jnp.repeat(jnp.exp(steps), dims[dim] // shards_of).reshape((-1,) + (1,) * (len(dims) - dim - 1))

    level = one(*cuts[0])
    for cut in cuts[1:]:
        level = level * one(*cut)
    return level


def assign_block(stream_key, own, number, rows, amount, top, bound, skew):
    ranking = jax.random.permutation(stream_key, amount)
    crowded, usual = shares(amount, rows * top, bound, skew, True), shares(amount, rows * top, bound, skew, False)
    places = jnp.arange(amount)

    def named(sizes, turn):
        used = int((sizes > 0).sum())
        fixed = max(1, used // 4)
        moved = fixed + (places - fixed + turn * (used - fixed)) % max(1, amount - fixed)
        return jnp.zeros((amount,), jnp.int32).at[ranking[jnp.where(places < fixed, places, moved)]].set(jnp.asarray(sizes, jnp.int32))

    sizes = jnp.where(number % 4 == 0, named(crowded, number // 4), named(usual, number - number // 4 - 1))
    mixed = jax.random.permutation(jax.random.fold_in(own, 3), amount)
    giver, taker = mixed[0:amount // 2 * 2:2], mixed[1:amount // 2 * 2:2]
    slack = jnp.minimum(sizes[giver] - 1, bound - sizes[taker]) // 2
    slack = jnp.where((giver == ranking[0]) | (taker == ranking[0]) | (sizes[taker] == 0), 0, jnp.maximum(slack, 0))
    moved = jax.random.randint(jax.random.fold_in(own, 4), (amount // 2,), 0, 1 << 20) % (slack + 1)
    sizes = sizes.at[giver].add(-moved).at[taker].add(moved)
    items = jnp.searchsorted(jnp.cumsum(sizes), jnp.arange(rows * top), side="right").astype(jnp.int32)
    listing = items.reshape(top, rows).T
    listing = listing[jax.random.permutation(jax.random.fold_in(own, 1), rows)]
    turn = jax.random.randint(jax.random.fold_in(own, 2), (rows, 1), 0, top)
    return jnp.take_along_axis(listing, (jnp.arange(top)[None, :] + turn) % top, axis=1)


def shares(amount, total, reach, slope, full):
    weights = [(1 << 20) // math.isqrt(rank ** slope) + 1 for rank in range(1, amount + 1)]
    largest = reach if full else min(reach, max(-(-total // amount), total * weights[0] // sum(weights)))
    least = 1 if total - largest >= amount - 1 else 0
    counts, rest = [largest] + [least] * (amount - 1), total - largest - least * (amount - 1)
    while rest > 0:
        free = [i for i in range(1, amount) if counts[i] < largest] or [i for i in range(1, amount) if counts[i] < reach]
        whole, remaining = sum([weights[i] for i in free]), rest
        for i in free:
            addition = min(reach - counts[i], max(1, remaining * weights[i] // whole), rest)
            counts[i] = counts[i] + addition
            rest = rest - addition
    return np.array(counts)


def scatter_about(own_key, dims, scale, reach, cuts=(), kind=jnp.bfloat16):
    loudness = block_levels(own_key, dims, cuts, -0.22, 0.18) if cuts else 1.0
    entries = jax.random.normal(own_key, dims, jnp.float32) * scale * loudness
    return jnp.minimum(jnp.maximum(entries, -reach), reach).astype(kind)


def setup_inputs(seed: int = 0) -> dict:
    arg_keys = jax.random.split(jax.random.key(seed), 13)
    tokens = scatter_about(arg_keys[0], (PACKS, PACK, D), 1.0, 6.0, ((0, 2), (1, 4)))
    segments = draw_segments(jax.random.fold_in(arg_keys[12], 71), 0)
    routes_keys = jax.random.split(jax.random.fold_in(arg_keys[2], 1), PACKS * PACK // TOK_DEV)
    routes_turns = jax.random.permutation(jax.random.fold_in(arg_keys[2], 3), PACKS * PACK // TOK_DEV)
    routes = jax.vmap(lambda own, number: assign_block(jax.random.fold_in(arg_keys[2], 2), own, number, TOK_DEV, EXPERTS, TOPK, CAPACITY, 1))(routes_keys, routes_turns).reshape((PACKS, PACK, TOPK))
    cotangent = scatter_about(arg_keys[3], (PACKS, PACK, D), 1.0, 6.0, ((0, 2), (1, 4)))
    first_gain = jnp.clip(1.0 + 0.18 * jax.random.normal(arg_keys[4], (D,), jnp.float32), 0.099609375, 1.8984375).astype(jnp.bfloat16)
    head_gain = jnp.clip(1.0 + 0.59375 * jax.random.uniform(arg_keys[5], (2 * HEAD_DIM,), jnp.float32) ** block_levels(arg_keys[5], (2 * HEAD_DIM,), ((0, 2),), -0.2, 0.2), 1.0, 1.59375).astype(jnp.bfloat16)
    attention_in = scatter_about(arg_keys[6], (D, 3, HEADS * HEAD_DIM), D ** -0.5, 0.125, ((0, 2), (2, 4)))
    attention_out = scatter_about(arg_keys[7], (D, HEADS * HEAD_DIM), (D // 16) ** -0.5, 0.5, ((0, 2), (1, 4)))
    second_gain = jnp.clip(1.0 + 0.18 * jax.random.normal(arg_keys[8], (D,), jnp.float32), 0.099609375, 1.8984375).astype(jnp.bfloat16)
    router_weight = scatter_about(arg_keys[9], (D, EXPERTS), (4 * D) ** -0.5, 0.0625, ((0, 2),))
    expert_in = scatter_about(arg_keys[10], (D, EXPERTS, 2, FF), D ** -0.5, 0.125, ((0, 2), (3, 4)))
    expert_out = scatter_about(arg_keys[11], (D, EXPERTS, FF), (FF // 64) ** -0.5, 1.5, ((0, 2), (2, 4)))
    return {"tokens": tokens, "segments": segments, "routes": routes, "cotangent": cotangent, "first_gain": first_gain, "head_gain": head_gain, "attention_in": attention_in, "attention_out": attention_out, "second_gain": second_gain, "router_weight": router_weight, "expert_in": expert_in, "expert_out": expert_out}


NORM_EPSILON = 1e-06
ROTARY_BASE = 50000.0
MASKED = -1e+30

@jax.custom_vjp
def low(v):
    return lax.optimization_barrier(v.astype(jnp.bfloat16)).astype(jnp.float32)

@jax.custom_vjp
def low_back(v):
    return v

def low_keep(v):
    return (low(v), None)

def low_pass(kept, grad):
    return (grad,)

def back_keep(v):
    return (v, None)

def back_low(kept, grad):
    return (low(grad),)
low.defvjp(low_keep, low_pass)
low_back.defvjp(back_keep, back_low)

def high_einsum(form, left, right):
    return jnp.einsum(form, left, right, precision=lax.Precision.HIGHEST)

def norm_scale(values, gain):
    return values * lax.rsqrt(lax.optimization_barrier(jnp.mean(values * values, axis=-1, keepdims=True)) + NORM_EPSILON) * gain

def rotate(values, positions):
    halfway = values.shape[-1] // 2
    steps = jnp.arange(halfway).astype(positions.dtype)
    frequency = ROTARY_BASE ** (-2.0 * steps / values.shape[-1])
    angles = positions[:, None] * frequency[None, :]
    cosine = jnp.cos(angles)[:, None, :]
    sine = jnp.sin(angles)[:, None, :]
    front = values[..., :halfway]
    back = values[..., halfway:]
    return jnp.concatenate([front * cosine - back * sine, back * cosine + front * sine], axis=-1)

def pack_forward(layer_in, segments, routes, weights):
    first_gain, head_gain, attention_in, attention_out, second_gain, router_weight, expert_in, expert_out = weights
    positions = jnp.arange(PACK).astype(jnp.float32)
    first_normed = low(norm_scale(layer_in, first_gain))
    projected = low_back(high_einsum('td,dsj->tsj', first_normed, attention_in))
    queries = projected[:, 0].reshape(PACK, HEADS, HEAD_DIM)
    keys = projected[:, 1].reshape(PACK, HEADS, HEAD_DIM)
    values = low(projected[:, 2].reshape(PACK, HEADS, HEAD_DIM))
    queries = low(rotate(norm_scale(queries, head_gain[:HEAD_DIM]), positions))
    keys = low(rotate(norm_scale(keys, head_gain[HEAD_DIM:]), positions))
    same_doc = segments[:, None] == segments[None, :]
    scale = HEAD_DIM ** (-0.5)

    def one_head(operands):
        query_head, key_head, value_head = operands
        scores = low_back(high_einsum('qd,kd->qk', query_head, key_head) * scale)
        chances = low(jax.nn.softmax(jnp.where(same_doc, scores, MASKED), axis=-1))
        return high_einsum('qk,kd->qd', chances, value_head)
    heads_out = lax.map(jax.checkpoint(one_head), (queries.transpose(1, 0, 2), keys.transpose(1, 0, 2), values.transpose(1, 0, 2)))
    mixed = low(low_back(heads_out.transpose(1, 0, 2).reshape(PACK, HEADS * HEAD_DIM)))
    residual = layer_in + low_back(high_einsum('tj,dj->td', mixed, attention_out))
    second_normed = low(norm_scale(residual, second_gain))
    logits = low_back(high_einsum('td,de->te', second_normed, router_weight))
    router_chances = jax.nn.softmax(logits, axis=-1)
    picked = lax.optimization_barrier(jnp.sum((routes[:, :, None] == jnp.arange(EXPERTS)[None, None, :]).astype(jnp.float32), axis=1))
    combine = picked * router_chances

    def one_expert(total, operands):
        inward, outward, column = operands
        gate_up = low_back(high_einsum('td,dxf->txf', second_normed, inward))
        hidden = low(jax.nn.silu(gate_up[:, 0]) * gate_up[:, 1])
        result = low_back(high_einsum('tf,df->td', hidden, outward))
        return (total + column[:, None] * result, None)
    start_total = jnp.zeros((PACK, D), jnp.float32)
    expert_total = lax.scan(jax.checkpoint(one_expert), start_total, (expert_in.transpose(1, 0, 2, 3), expert_out.transpose(1, 0, 2), combine.T))[0]
    return residual + expert_total

def reference(tokens, segments, routes, cotangent, first_gain, head_gain, attention_in, attention_out, second_gain, router_weight, expert_in, expert_out):
    weights = tuple((entry.astype(jnp.float32) for entry in (first_gain, head_gain, attention_in, attention_out, second_gain, router_weight, expert_in, expert_out)))
    inputs = tokens.astype(jnp.float32)

    def whole_layer(layer_in, layer_weights):

        def one_pack(operands):
            return pack_forward(operands[0], operands[1], operands[2], layer_weights)
        return lax.map(jax.checkpoint(one_pack), (layer_in, segments, routes))
    layer_output, pullback = jax.vjp(whole_layer, inputs, weights)
    input_gradient, weight_grads = pullback(cotangent.astype(jnp.float32))
    return (layer_output.astype(jnp.bfloat16), input_gradient, weight_grads[0], weight_grads[1], weight_grads[2], weight_grads[3], weight_grads[4], weight_grads[5], weight_grads[6], weight_grads[7])
```

```python
import jax
import jax.numpy as jnp
from jax import lax
from jax.sharding import PartitionSpec as P

HEAD_DIM = 128
NORM_EPSILON = 1e-06
ROTARY_BASE = 50000.0
MASKED = -1e30
F32 = jnp.float32
BF16 = jnp.bfloat16


def lower(values):
    return values.astype(BF16)


def dot(left, right, over, out=F32):
    result = lax.dot_general(left, right, (((over[0],), (over[1],)), ((), ())), preferred_element_type=F32)
    return result.astype(out)


def receive(values, axis, distance):
    size = lax.axis_size(axis)
    return lax.ppermute(values, axis, [((i + distance) % size, i) for i in range(size)])


def swap(values, axis, bit):
    size = lax.axis_size(axis)
    return lax.ppermute(values, axis, [(i, i ^ bit) for i in range(size)])


def bits(axis):
    size = lax.axis_size(axis)
    assert size & (size - 1) == 0
    found = [1 << i for i in range(size.bit_length() - 1)]
    return found


def masks(axis):
    order = [0]
    for bit in reversed(bits(axis)):
        order = order + [m ^ bit for m in order]
    return order


def gather_tp(values):
    for bit in reversed(bits("tp")):
        values = jnp.concatenate([values, swap(values, "tp", bit)], axis=0)
    return values


def scatter_tp(values):
    for bit in bits("tp"):
        half = values.shape[0] // 2
        values = values[:half].astype(F32) + swap(lower(values[half:]), "tp", bit).astype(F32)
    return values


def gather_rows(values):
    size = lax.axis_size("ctx")
    blocks = [[values] + [receive(values, "ctx", r) for r in range(1, size)]]
    for bit in reversed(bits("tp")[1:]):
        blocks = blocks + [[swap(v, "tp", bit) for v in part] for part in blocks]
    values = jnp.concatenate([v for part in blocks for v in part], axis=0)
    return jnp.concatenate([values, swap(values, "tp", 1)], axis=0)


def scatter_rows(values):
    size = lax.axis_size("ctx")
    half = values.shape[0] // 2
    values = values[:half].astype(F32) + swap(lower(values[half:]), "tp", 1).astype(F32)
    found = bits("tp")[1:]
    parts = 1 << len(found)
    blocks = values.reshape((parts, size, -1) + values.shape[1:])
    blocks = [[blocks[a, r] for r in range(size)] for a in range(parts)]
    for bit in found:
        near, far = blocks[: len(blocks) // 2], blocks[len(blocks) // 2 :]
        blocks = [
            [n + swap(lower(f), "tp", bit).astype(F32) for n, f in zip(one, other)]
            for one, other in zip(near, far)
        ]
    total = blocks[0][0]
    for r in range(1, size):
        total = total + receive(lower(blocks[0][r]), "ctx", size - r).astype(F32)
    return total


def sum_tokens(values):
    for axis in ("tp", "ctx"):
        for bit in bits(axis):
            values = values + swap(values, axis, bit)
    return values


def own_block(values, ahead=0, axis=0):
    size = lax.axis_size("shard")
    block = values.shape[axis] // size
    spot = lax.rem(lax.axis_index("shard") + ahead, size)
    return lax.dynamic_slice_in_dim(values, spot * block, block, axis=axis)


def sum_shard(values, axis):
    size = lax.axis_size("shard")
    total = own_block(values, 0, axis)
    for r in range(1, size):
        total = total + receive(own_block(values, r, axis), "shard", size - r)
    return total


def product_shard(lefts, right):
    size = lax.axis_size("shard")
    total = dot(lefts[0], right, (0, 0))
    for r in range(1, size):
        total = total + receive(dot(lefts[r], right, (0, 0), BF16), "shard", size - r).astype(F32)
    return total


def ahead_first(values, start, axis=0):
    return lax.dynamic_slice_in_dim(
        jnp.concatenate([values, values], axis=axis), start, values.shape[axis], axis=axis
    )


def gather_natural(values, axis_name, axis=0):
    return lax.all_gather(values, axis_name, axis=axis, tiled=True)


def row_order(values):
    values = ahead_first(values, lax.axis_index("ctx"))
    t = lax.axis_index("tp")
    return jnp.concatenate([lax.dynamic_index_in_dim(values, t ^ m, 1, False)[None] for m in masks("tp")], axis=0)


def natural_rows(values):
    t, order = lax.axis_index("tp"), masks("tp")
    part = values.shape[0] // len(order)
    found = []
    for q in range(len(order)):
        m, place = q ^ t, 0
        for i, bit in enumerate(reversed(bits("tp"))):
            place = place + jnp.where(m & bit, 1 << i, 0)
        found.append(lax.dynamic_slice_in_dim(values, place * part, part))
    return jnp.concatenate(found, axis=0)


def inverse_scale(values):
    return lax.rsqrt(jnp.mean(values * values, axis=-1, keepdims=True) + NORM_EPSILON)


def turn(values, cosine, sine):
    half = values.shape[-1] // 2
    front, back = values[..., :half], values[..., half:]
    return jnp.concatenate([front * cosine - back * sine, back * cosine + front * sine], axis=-1)


def norm_back(grad, values, gain):
    scale = inverse_scale(values)
    weighted = grad * gain
    middle = jnp.mean(values * weighted, axis=-1, keepdims=True)
    return scale * weighted - values * (scale * scale * scale) * middle, grad * values * scale


def local(
    tokens,
    segments,
    routes,
    cotangent,
    first_gain,
    head_gain,
    attention_in,
    attention_out,
    second_gain,
    router_weight,
    expert_in,
    expert_out,
):
    s, c, t = lax.axis_index("shard"), lax.axis_index("ctx"), lax.axis_index("tp")
    shards, ctxs, tps = lax.axis_size("shard"), lax.axis_size("ctx"), lax.axis_size("tp")
    rows, width = tokens.shape[1:]
    own = rows // tps
    block = width // shards
    every = rows * ctxs
    experts = router_weight.shape[1]
    group = experts // ctxs
    hidden_size = expert_out.shape[2]
    local_width = attention_out.shape[1]
    head_size = local_width // ctxs
    heads = head_size // HEAD_DIM

    gains = gather_natural(jnp.stack([first_gain, second_gain]), "shard", 1).astype(F32)
    gain_one, gain_two = gains[0], gains[1]
    head_gains = gather_natural(head_gain, "shard").astype(F32)
    head_in = lax.dynamic_slice_in_dim(attention_in, c * head_size, head_size, axis=2)
    head_in = gather_natural(head_in.reshape(block, 3 * head_size), "shard")
    exit_weight = gather_natural(ahead_first(attention_out, c * head_size, 1), "shard")
    router = gather_natural(router_weight, "shard")
    choices_all = gather_natural(routes[0], "ctx").reshape(ctxs, tps, own, -1)
    group_out = lax.dynamic_slice_in_dim(expert_out, c * group, group, axis=1)
    group_out = gather_natural(group_out.reshape(block, group * hidden_size), "shard")
    group_in = lax.dynamic_slice_in_dim(expert_in, c * group, group, axis=1)
    in_weights = [
        gather_natural(group_in[:, i].reshape(block, 2 * hidden_size), "shard") for i in range(group)
    ]

    first = t * own
    layer_in = lax.dynamic_slice_in_dim(tokens[0], first, own).astype(F32)
    cot_own = lax.dynamic_slice_in_dim(cotangent[0], first, own)
    upstream = cot_own.astype(F32)
    picks_all = jnp.any(row_order(choices_all)[..., None] == jnp.arange(experts), axis=3)
    picks = picks_all[0, 0]
    picks_all = picks_all.reshape(every, experts)

    normed_one = lower(layer_in * inverse_scale(layer_in) * gain_one)
    normed_one_all = gather_rows(normed_one)
    cot_own, _ = lax.optimization_barrier((cot_own, normed_one_all))
    cot_all = gather_rows(cot_own)
    spot = row_order(jnp.arange(every, dtype=jnp.int32).reshape(ctxs, tps, own)).reshape(-1)
    documents = row_order(segments[0].reshape(ctxs, tps, own)).reshape(-1)
    steps = jnp.arange(HEAD_DIM // 2).astype(F32)
    frequency = ROTARY_BASE ** (-2.0 * steps / HEAD_DIM)
    angles = spot.astype(F32)[:, None] * frequency[None, :]
    cosine, sine = jnp.cos(angles)[:, None], jnp.sin(angles)[:, None]
    projected = dot(normed_one_all, head_in, (1, 0)).reshape(every, 3, heads, HEAD_DIM)
    query_raw, key_raw = projected[:, 0], projected[:, 1]
    gain_q, gain_k = head_gains[:HEAD_DIM], head_gains[HEAD_DIM:]
    queries = lower(turn(query_raw * inverse_scale(query_raw) * gain_q, cosine, sine))
    keys = lower(turn(key_raw * inverse_scale(key_raw) * gain_k, cosine, sine))
    values = lower(projected[:, 2])
    scale = HEAD_DIM ** (-0.5)
    scores = jnp.einsum("qhd,khd->hqk", queries, keys, preferred_element_type=F32) * scale
    same = documents[:, None] == documents[None, :]
    chances = jax.nn.softmax(jnp.where(same[None], scores, MASKED), axis=-1)
    chances_low = lower(chances)
    mixed_head = lower(jnp.einsum("hqk,khd->qhd", chances_low, values, preferred_element_type=F32))
    blocks = mixed_head.reshape(tps, ctxs, own, head_size)
    mixed = [blocks[:, 0]] + [receive(blocks[:, ctxs - j], "ctx", j) for j in range(1, ctxs)]
    mixed = jnp.concatenate([m.reshape(rows, head_size) for m in mixed], axis=1)
    residual = layer_in + scatter_tp(dot(mixed, exit_weight, (1, 1)))

    normed_two = lower(residual * inverse_scale(residual) * gain_two)
    normed_two_all = gather_rows(normed_two)
    chances_all = jax.nn.softmax(dot(normed_two_all, router, (1, 0)), axis=-1)
    gates = jnp.where(picks_all, chances_all, 0.0)
    gates = lax.dynamic_slice_in_dim(gates, c * group, group, axis=1)
    out_weights = [group_out[:, i * hidden_size : (i + 1) * hidden_size] for i in range(group)]
    normed_blocks = [own_block(normed_two_all, r, 1) for r in range(shards)]
    cot_blocks = [own_block(cot_all, r, 1) for r in range(shards)]
    backs = dot(cot_all, group_out, (1, 0))
    scaled, gate_parts, inner_grads, chunks = [], [], [], []
    rows_now = normed_two_all
    for i in range(group):
        gate_up = dot(rows_now, in_weights[i], (1, 0))
        gate, up = gate_up[:, :hidden_size], gate_up[:, hidden_size:]
        back = backs[:, i * hidden_size : (i + 1) * hidden_size]
        sigmoid = jax.nn.sigmoid(gate)
        silu = gate * sigmoid
        hidden = lower(silu * up).astype(F32)
        weight = gates[:, i : i + 1]
        scaled.append(lower(hidden * weight))
        gate_parts.append(jnp.sum(hidden * back, axis=1))
        hidden_grad = back * weight
        inner_grads.append(
            lower(
                jnp.concatenate(
                    [hidden_grad * up * sigmoid * (1.0 + gate * (1.0 - sigmoid)), hidden_grad * silu], axis=1
                )
            )
        )
        upward = product_shard(normed_blocks, inner_grads[i])
        downward = product_shard(cot_blocks, scaled[i])
        chunks.append(
            lax.all_gather(lower(jnp.concatenate([upward, downward], axis=1)), "ctx", axis=0, tiled=False)
        )
        rows_now, _ = lax.optimization_barrier((normed_two_all, scaled[i]))

    normed_part = sum(dot(inner_grads[i], in_weights[i], (1, 1)) for i in range(group))
    gate_part = lax.dynamic_update_slice(
        jnp.zeros((every, 128), F32), jnp.stack(gate_parts, axis=1), (0, c * group)
    )
    normed_sum = scatter_rows(jnp.concatenate([normed_part, gate_part], axis=1))
    normed_sum, gate_grad = normed_sum[:, :width], normed_sum[:, width : width + experts]
    result_part = dot(jnp.concatenate(scaled, axis=1), group_out, (1, 1))
    result_part, _ = lax.optimization_barrier((result_part, normed_sum))
    result_sum = scatter_rows(result_part)
    layer_output = natural_rows(gather_tp(lower(residual + result_sum)))[None]

    router_chances = jax.nn.softmax(dot(normed_two, router, (1, 0)), axis=-1)
    chance_grad = jnp.where(picks, gate_grad, 0.0)
    logit_grad = lower(
        router_chances * (chance_grad - jnp.sum(router_chances * chance_grad, axis=-1, keepdims=True))
    )
    router_part = dot(logit_grad, normed_two, (0, 0))
    normed_grad = normed_sum + dot(logit_grad, router, (1, 1))
    residual_back, second_part = norm_back(normed_grad, residual, gain_two)
    residual_grad = upstream + residual_back

    attend_grad = gather_tp(lower(residual_grad))
    exit_part = product_shard([own_block(attend_grad, r, 1) for r in range(shards)], mixed)
    exit_head = exit_part[:, :head_size]
    for r in range(1, ctxs):
        exit_head = exit_head + receive(
            lower(exit_part[:, r * head_size : (r + 1) * head_size]), "ctx", ctxs - r
        ).astype(F32)
    mixed_grad = lower(dot(attend_grad, exit_weight, (1, 0))).reshape(tps, own, ctxs, head_size)
    parts = [mixed_grad[:, :, 0]] + [receive(mixed_grad[:, :, ctxs - j], "ctx", j) for j in range(1, ctxs)]
    mixed_grad = jnp.stack(parts, axis=1).reshape(every, heads, HEAD_DIM)
    weight_grad = jnp.einsum("qhd,khd->hqk", mixed_grad, values, preferred_element_type=F32)
    score_grad = lower(chances * (weight_grad - jnp.sum(chances * weight_grad, axis=-1, keepdims=True)))
    query_grad = jnp.einsum("hqk,khd->qhd", score_grad, keys, preferred_element_type=F32) * scale
    key_grad = jnp.einsum("hqk,qhd->khd", score_grad, queries, preferred_element_type=F32) * scale
    value_grad = jnp.einsum("hqk,qhd->khd", chances_low, mixed_grad, preferred_element_type=F32)
    query_raw_grad, gain_q_part = norm_back(turn(query_grad, cosine, -sine), query_raw, gain_q)
    key_raw_grad, gain_k_part = norm_back(turn(key_grad, cosine, -sine), key_raw, gain_k)
    projected_grad = lower(
        jnp.stack([query_raw_grad, key_raw_grad, value_grad], axis=1).reshape(every, 3 * head_size)
    )
    entry_head = product_shard([own_block(normed_one_all, r, 1) for r in range(shards)], projected_grad)
    attention_chunk = lax.all_gather(
        lower(jnp.concatenate([entry_head, exit_head], axis=1)), "ctx", axis=0, tiled=False
    )
    first_normed_grad = scatter_rows(dot(projected_grad, head_in, (1, 1)))
    input_back, first_part = norm_back(first_normed_grad, layer_in, gain_one)
    input_gradient = natural_rows(gather_tp(lower(residual_grad + input_back))).astype(F32)[None]

    early = jnp.concatenate([jnp.sum(second_part, axis=0)[None], router_part], axis=0)
    early = sum_shard(sum_tokens(early), 1)
    head_part = jnp.concatenate([jnp.sum(gain_q_part, axis=(0, 1)), jnp.sum(gain_k_part, axis=(0, 1))])
    late = sum_tokens(jnp.concatenate([jnp.sum(first_part, axis=0), head_part])[None])
    first_gradient = sum_shard(late[:, :width], 1)[0]
    head_gradient = sum_shard(late[:, width:], 1)[0]

    wide = jnp.moveaxis(attention_chunk, 0, 1).astype(F32)
    entry_gradient = jnp.moveaxis(
        wide[:, :, : 3 * head_size].reshape(block, ctxs, 3, head_size), 1, 2
    ).reshape(block, 3, local_width)
    exit_gradient = wide[:, :, 3 * head_size :].reshape(block, local_width)
    upward_gradient = jnp.stack([chunk[:, :, : 2 * hidden_size] for chunk in chunks], axis=1)
    upward_gradient = jnp.moveaxis(upward_gradient, 2, 0).astype(F32)
    upward_gradient = upward_gradient.reshape(block, experts, 2, hidden_size)
    downward_gradient = jnp.stack([chunk[:, :, 2 * hidden_size :] for chunk in chunks], axis=1)
    downward_gradient = jnp.moveaxis(downward_gradient, 2, 0).astype(F32)
    downward_gradient = downward_gradient.reshape(block, experts, hidden_size)
    return (
        layer_output,
        input_gradient,
        first_gradient,
        head_gradient,
        entry_gradient,
        exit_gradient,
        early[0],
        early[1:].T,
        upward_gradient,
        downward_gradient,
    )


def solution(mesh):
    return jax.shard_map(
        local,
        mesh=mesh,
        in_specs=(
            P("shard", "ctx", None),
            P("shard", None),
            P("shard", "ctx", None),
            P("shard", "ctx", None),
            P("shard"),
            P("shard"),
            P("shard", None, "tp"),
            P("shard", "tp"),
            P("shard"),
            P("shard", None),
            P("shard", None, None, "tp"),
            P("shard", None, "tp"),
        ),
        out_specs=(
            P("shard", "ctx", None),
            P("shard", "ctx", None),
            P("shard"),
            P("shard"),
            P("shard", None, "tp"),
            P("shard", "tp"),
            P("shard"),
            P("shard", None),
            P("shard", None, None, "tp"),
            P("shard", None, "tp"),
        ),
        check_vma=False,
    )
```

```python
import functools

import jax
import jax.numpy as jnp
from jax import lax
from jax.experimental import pallas as pl
from jax.experimental.pallas import tpu as pltpu
from jax.sharding import PartitionSpec as P

HEAD_DIM = 128
NORM_EPSILON = 1e-06
ROTARY_BASE = 50000.0
MASKED = -1e30
F32 = jnp.float32
BF16 = jnp.bfloat16


def lower(values):
    return values.astype(BF16)


def dot(left, right, over, out=F32):
    result = lax.dot_general(left, right, (((over[0],), (over[1],)), ((), ())), preferred_element_type=F32)
    return result.astype(out)


def receive(values, axis, distance):
    size = lax.axis_size(axis)
    return lax.ppermute(values, axis, [((i + distance) % size, i) for i in range(size)])


def swap(values, axis, bit):
    size = lax.axis_size(axis)
    return lax.ppermute(values, axis, [(i, i ^ bit) for i in range(size)])


def bits(axis):
    size = lax.axis_size(axis)
    assert size & (size - 1) == 0
    found = [1 << i for i in range(size.bit_length() - 1)]
    return found


def masks(axis):
    order = [0]
    for bit in reversed(bits(axis)):
        order = order + [m ^ bit for m in order]
    return order


def gather_tp(values):
    for bit in reversed(bits("tp")):
        values = jnp.concatenate([values, swap(values, "tp", bit)], axis=0)
    return values


def scatter_tp(values):
    for bit in bits("tp"):
        half = values.shape[0] // 2
        values = values[:half].astype(F32) + swap(lower(values[half:]), "tp", bit).astype(F32)
    return values


def spread_tp(block):
    parts = [block]
    for bit in reversed(bits("tp")[1:]):
        parts = parts + [swap(part, "tp", bit) for part in parts]
    return jnp.concatenate(parts + [swap(part, "tp", 1) for part in parts], axis=0)


def gather_ctx(values):
    size = lax.axis_size("ctx")
    whole = jnp.concatenate([values] + [receive(values, "ctx", r) for r in range(1, size)], axis=0)
    return ahead_first(whole, lax.rem(size - lax.axis_index("ctx"), size) * values.shape[0])


def greet(peers):
    barrier = pltpu.get_barrier_semaphore()
    for peer in peers:
        pl.semaphore_signal(barrier, inc=1, device_id=peer, device_id_type=pl.DeviceIdType.MESH)
    pl.semaphore_wait(barrier, len(peers))


def remote(source, target, sent, arrived, place, peer):
    return pltpu.make_async_remote_copy(
        src_ref=source,
        dst_ref=target,
        send_sem=sent.at[place],
        recv_sem=arrived.at[place],
        device_id=peer,
        device_id_type=pl.DeviceIdType.MESH,
    )


def far_first(size):
    return sorted(range(1, size), key=lambda r: min(r, size - r))


def gather_kernel(size, pieces, own, out, local, z_sent, z_here, x_sent, x_here, core_sent, core_here):
    c, t = lax.axis_index("ctx"), lax.axis_index("tp")
    x_peer, core_peer = {"tp": t ^ 2}, {"tp": t ^ 1}
    behind = {r: {"ctx": lax.rem(c + size - r, size)} for r in range(1, size)}
    greet([x_peer, core_peer] + [behind[r] for r in range(1, size)])
    step = own.shape[0] // pieces
    rows = [pl.ds(h * step, step) for h in range(pieces)]
    spot = [lax.rem(c + r, size) for r in range(size)]
    keep = pltpu.make_async_copy(own, out.at[0, c], local)
    keep.start()
    order = [(r, h) for r in far_first(size) for h in range(pieces)]
    mine = [(0, h) for h in range(pieces)]
    z = {
        (r, h): remote(own.at[rows[h]], out.at[0, c, rows[h]], z_sent, z_here, (r - 1) * pieces + h, behind[r])
        for r, h in order
    }
    x, core = {}, {}
    for r, h in mine + order:
        source = own.at[rows[h]] if r == 0 else out.at[0, spot[r], rows[h]]
        near, far = [out.at[1 + m, spot[r], rows[h]] for m in range(2)], out.at[3, spot[r], rows[h]]
        place = r * pieces + h
        x[r, h] = remote(source, near[0], x_sent, x_here, place, x_peer)
        core[0, r, h] = remote(source, near[1], core_sent, core_here, place, core_peer)
        core[1, r, h] = remote(near[0], far, core_sent, core_here, size * pieces + place, core_peer)
    for key in order:
        z[key].start()
    for key in mine:
        x[key].start()
        core[(0,) + key].start()
    for key in order:
        z[key].wait_recv()
        x[key].start()
        core[(0,) + key].start()
    for key in mine + order:
        x[key].wait_recv()
        core[(1,) + key].start()
    for copy in core.values():
        copy.wait()
    for copy in list(x.values()) + list(z.values()):
        copy.wait_send()
    keep.wait()


def gather_rows(values):
    size = lax.axis_size("ctx")
    assert lax.axis_size("tp") == 4
    pieces = 2
    count = size * pieces
    return pl.pallas_call(
        functools.partial(gather_kernel, size, pieces),
        out_shape=jax.ShapeDtypeStruct((4, size) + values.shape, values.dtype),
        in_specs=[pl.BlockSpec(memory_space=pl.ANY)],
        out_specs=pl.BlockSpec(memory_space=pl.ANY),
        scratch_shapes=[pltpu.SemaphoreType.DMA(())]
        + [pltpu.SemaphoreType.DMA((n,)) for n in (count - pieces, count - pieces, count, count, 2 * count, 2 * count)],
        compiler_params=pltpu.CompilerParams(collective_id=0, has_side_effects=True),
        name="gather_rows",
    )(values)


def scatter_kernel(size, parts, out, held, core_in, x_in, z_in, local, z_sent, z_here, x_sent, x_here, core_sent, core_here):
    c, t = lax.axis_index("ctx"), lax.axis_index("tp")
    x_peer, core_peer = {"tp": t ^ 2}, {"tp": t ^ 1}
    ahead = {r: {"ctx": lax.rem(c + r, size)} for r in range(1, size)}
    greet([x_peer, core_peer] + [ahead[r] for r in range(1, size)])
    spot = [lax.rem(c + r, size) for r in range(size)]
    keep = pltpu.make_async_copy(parts.at[pl.ds(0, 2)], held, local)
    keep.start()
    order = far_first(size) + [0]
    core = {
        (m, r): remote(parts.at[2 + m, spot[r]], core_in.at[m, r], core_sent, core_here, m * size + r, core_peer)
        for m in (1, 0)
        for r in order
    }
    x = {r: remote(held.at[1, spot[r]], x_in.at[r], x_sent, x_here, r, x_peer) for r in order}
    z = {r: remote(held.at[0, spot[r]], z_in.at[r - 1], z_sent, z_here, r - 1, ahead[r]) for r in order[:-1]}
    for copy in core.values():
        copy.start()
    keep.wait()
    tall = 16
    steps = out.shape[0] // tall

    for r in order:
        core[1, r].wait_recv()

        @pl.loop(0, steps)
        def _(i):
            rows = pl.ds(pl.multiple_of(i * tall, tall), tall)
            held[1, spot[r], rows] = (held[1, spot[r], rows].astype(F32) + core_in[1, r, rows].astype(F32)).astype(BF16)

        x[r].start()
    for r in order:
        core[0, r].wait_recv()
        x[r].wait_recv()

        @pl.loop(0, steps)
        def _(i):
            rows = pl.ds(pl.multiple_of(i * tall, tall), tall)
            total = held[0, spot[r], rows].astype(F32) + core_in[0, r, rows].astype(F32) + x_in[r, rows].astype(F32)
            if r == 0:
                out[rows] = total
            else:
                held[0, spot[r], rows] = total.astype(BF16)

        if r:
            z[r].start()
    for r in order[:-1]:
        z[r].wait_recv()

        @pl.loop(0, steps)
        def _(i):
            rows = pl.ds(pl.multiple_of(i * tall, tall), tall)
            out[rows] = out[rows] + z_in[r - 1, rows].astype(F32)

    for copy in list(core.values()) + list(x.values()) + list(z.values()):
        copy.wait_send()


def scatter_rows(parts, collective):
    size = lax.axis_size("ctx")
    rows, width = parts.shape[2:]
    return pl.pallas_call(
        functools.partial(scatter_kernel, size),
        out_shape=jax.ShapeDtypeStruct((rows, width), F32),
        in_specs=[pl.BlockSpec(memory_space=pl.ANY)],
        out_specs=pl.BlockSpec(memory_space=pltpu.VMEM),
        scratch_shapes=[
            pltpu.VMEM((2, size, rows, width), BF16),
            pltpu.VMEM((2, size, rows, width), BF16),
            pltpu.VMEM((size, rows, width), BF16),
            pltpu.VMEM((size - 1, rows, width), BF16),
            pltpu.SemaphoreType.DMA(()),
        ]
        + [pltpu.SemaphoreType.DMA((n,)) for n in (size - 1, size - 1, size, size, 2 * size, 2 * size)],
        compiler_params=pltpu.CompilerParams(
            collective_id=collective, has_side_effects=True, vmem_limit_bytes=32 * 1024 * 1024
        ),
        name="scatter_rows",
    )(parts)


def sum_tokens(values):
    for axis in ("tp", "ctx"):
        for bit in bits(axis):
            values = values + swap(values, axis, bit)
    return values


def own_block(values, ahead=0, axis=0):
    size = lax.axis_size("shard")
    block = values.shape[axis] // size
    spot = lax.rem(lax.axis_index("shard") + ahead, size)
    return lax.dynamic_slice_in_dim(values, spot * block, block, axis=axis)


def sum_shard(values, axis):
    size = lax.axis_size("shard")
    total = own_block(values, 0, axis)
    for r in range(1, size):
        total = total + receive(own_block(values, r, axis), "shard", size - r)
    return total


def product_parts(pairs):
    own = jnp.concatenate([dot(lefts[0], right, (0, 0)) for lefts, right in pairs], axis=1)
    others = tuple(
        jnp.concatenate([dot(lefts[r], right, (0, 0), BF16) for lefts, right in pairs], axis=1)
        for r in range(1, lax.axis_size("shard"))
    )
    return own, others


def product_sum(own, others):
    size = lax.axis_size("shard")
    for r in range(1, size):
        own = own + receive(others[r - 1], "shard", size - r).astype(F32)
    return own


def ahead_first(values, start, axis=0):
    return lax.dynamic_slice_in_dim(
        jnp.concatenate([values, values], axis=axis), start, values.shape[axis], axis=axis
    )


def gather_natural(values, axis_name, axis=0):
    return lax.all_gather(values, axis_name, axis=axis, tiled=True)


def gather_small(values, axis):
    size = lax.axis_size("shard")
    whole = jnp.concatenate([values] + [receive(values, "shard", r) for r in range(1, size)], axis=axis)
    return ahead_first(whole, lax.rem(size - lax.axis_index("shard"), size) * values.shape[axis], axis)


def after(values, *earlier):
    return lax.optimization_barrier((values,) + earlier)[0]


def part_order(values):
    t = lax.axis_index("tp")
    return jnp.concatenate([lax.dynamic_index_in_dim(values, t ^ m, 1, False)[None] for m in masks("tp")], axis=0)


def natural_rows(values):
    t, order = lax.axis_index("tp"), masks("tp")
    part = values.shape[0] // len(order)
    found = []
    for q in range(len(order)):
        m, place = q ^ t, 0
        for i, bit in enumerate(reversed(bits("tp"))):
            place = place + jnp.where(m & bit, 1 << i, 0)
        found.append(lax.dynamic_slice_in_dim(values, place * part, part))
    return jnp.concatenate(found, axis=0)


def inverse_scale(values):
    return lax.rsqrt(jnp.mean(values * values, axis=-1, keepdims=True) + NORM_EPSILON)


def turn(values, cosine, sine):
    half = values.shape[-1] // 2
    front, back = values[..., :half], values[..., half:]
    return jnp.concatenate([front * cosine - back * sine, back * cosine + front * sine], axis=-1)


def norm_back(grad, values, gain):
    scale = inverse_scale(values)
    weighted = grad * gain
    middle = jnp.mean(values * weighted, axis=-1, keepdims=True)
    return scale * weighted - values * (scale * scale * scale) * middle, grad * values * scale


def local(
    tokens,
    segments,
    routes,
    cotangent,
    first_gain,
    head_gain,
    attention_in,
    attention_out,
    second_gain,
    router_weight,
    expert_in,
    expert_out,
):
    s, c, t = lax.axis_index("shard"), lax.axis_index("ctx"), lax.axis_index("tp")
    shards, ctxs, tps = lax.axis_size("shard"), lax.axis_size("ctx"), lax.axis_size("tp")
    rows, width = tokens.shape[1:]
    own = rows // tps
    block = width // shards
    every = rows * ctxs
    experts = router_weight.shape[1]
    hidden_size = expert_out.shape[2]
    local_width = attention_out.shape[1]
    head_size = local_width // ctxs
    heads = head_size // HEAD_DIM

    group = experts // ctxs
    base = c * group

    gains = gather_small(jnp.stack([first_gain, second_gain]), 1).astype(F32)
    gain_one, gain_two = gains[0], gains[1]
    head_gains = gather_small(head_gain[None], 1)[0].astype(F32)
    head_in = lax.dynamic_slice_in_dim(attention_in, c * head_size, head_size, axis=2)
    head_in = head_in.reshape(block, 3 * head_size)
    first = t * own
    tokens_own = after(lax.dynamic_slice_in_dim(tokens[0], first, own), head_in)
    head_in = gather_natural(head_in, "shard")
    tokens_all = gather_rows(tokens_own).reshape(every, width)
    attention_out, expert_in, expert_out, cotangent, routes = lax.optimization_barrier(
        (attention_out, expert_in, expert_out, cotangent, routes, tokens_all)
    )[:-1]
    exit_weight = gather_natural(ahead_first(attention_out, c * head_size, 1), "shard")
    group_out = lax.dynamic_slice_in_dim(expert_out, base, group, axis=1)
    group_out = gather_natural(group_out.reshape(block, group * hidden_size), "shard")
    group_in = lax.dynamic_slice_in_dim(expert_in, base, group, axis=1)
    in_weights = [
        gather_natural(group_in[:, i].reshape(block, 2 * hidden_size), "shard") for i in range(group)
    ]

    layer_in = tokens_own.astype(F32)
    cot_own = lax.dynamic_slice_in_dim(cotangent[0], first, own)
    upstream = cot_own.astype(F32)
    cot_all = spread_tp(gather_ctx(cot_own))
    choices_all = gather_ctx(routes[0]).reshape(ctxs, tps, own, -1)
    picks_all = jnp.any(part_order(choices_all)[..., None] == jnp.arange(experts), axis=3)
    picks = lax.dynamic_index_in_dim(picks_all[0], c, 0, False)
    picks_all = picks_all.reshape(every, experts)
    router = gather_small(router_weight, 0)

    tokens_wide = tokens_all.astype(F32)
    normed_one_all = lower(tokens_wide * inverse_scale(tokens_wide) * gain_one)
    spot = part_order(jnp.arange(every, dtype=jnp.int32).reshape(ctxs, tps, own)).reshape(-1)
    documents = part_order(segments[0].reshape(ctxs, tps, own)).reshape(-1)
    steps = jnp.arange(HEAD_DIM // 2).astype(F32)
    frequency = ROTARY_BASE ** (-2.0 * steps / HEAD_DIM)
    angles = spot.astype(F32)[:, None] * frequency[None, :]
    cosine, sine = jnp.cos(angles)[:, None], jnp.sin(angles)[:, None]
    projected = dot(normed_one_all, head_in, (1, 0)).reshape(every, 3, heads, HEAD_DIM)
    query_raw, key_raw = projected[:, 0], projected[:, 1]
    gain_q, gain_k = head_gains[:HEAD_DIM], head_gains[HEAD_DIM:]
    queries = lower(turn(query_raw * inverse_scale(query_raw) * gain_q, cosine, sine))
    keys = lower(turn(key_raw * inverse_scale(key_raw) * gain_k, cosine, sine))
    values = lower(projected[:, 2])
    scale = HEAD_DIM ** (-0.5)
    scores = jnp.einsum("qhd,khd->hqk", queries, keys, preferred_element_type=F32) * scale
    same = documents[:, None] == documents[None, :]
    chances = jax.nn.softmax(jnp.where(same[None], scores, MASKED), axis=-1)
    chances_low = lower(chances)
    mixed_head = lower(jnp.einsum("hqk,khd->qhd", chances_low, values, preferred_element_type=F32))
    blocks = ahead_first(mixed_head.reshape(tps, ctxs, own, head_size), c, 1)
    mixed = [blocks[:, 0]] + [receive(blocks[:, ctxs - j], "ctx", j) for j in range(1, ctxs)]
    mixed = jnp.concatenate([m.reshape(rows, head_size) for m in mixed], axis=1)
    residual = layer_in + scatter_tp(dot(mixed, exit_weight, (1, 1)))

    normed_two = lower(residual * inverse_scale(residual) * gain_two)
    normed_two_all = gather_rows(normed_two).reshape(every, width)
    chances_all = jax.nn.softmax(dot(normed_two_all, router, (1, 0)), axis=-1)
    gates = jnp.where(picks_all, chances_all, 0.0)
    gates = lax.dynamic_slice_in_dim(gates, base, group, axis=1)
    normed_blocks = [own_block(normed_two_all, r, 1) for r in range(shards)]
    cot_blocks = [own_block(cot_all, r, 1) for r in range(shards)]
    backs = dot(cot_all, group_out, (1, 0))
    scaled, gate_parts, inner_grads, products = [], [], [], []
    rows_now = normed_two_all
    for i in range(group):
        gate_up = dot(rows_now, in_weights[i], (1, 0))
        gate, up = gate_up[:, :hidden_size], gate_up[:, hidden_size:]
        back = backs[:, i * hidden_size : (i + 1) * hidden_size]
        sigmoid = jax.nn.sigmoid(gate)
        silu = gate * sigmoid
        hidden = lower(silu * up).astype(F32)
        weight = gates[:, i : i + 1]
        scaled.append(lower(hidden * weight))
        gate_parts.append(jnp.sum(hidden * back, axis=1))
        hidden_grad = back * weight
        inner_grads.append(
            lower(
                jnp.concatenate(
                    [hidden_grad * up * sigmoid * (1.0 + gate * (1.0 - sigmoid)), hidden_grad * silu], axis=1
                )
            )
        )
        products.append(product_parts([(normed_blocks, inner_grads[i]), (cot_blocks, scaled[i])]))
        rows_now = after(rows_now, *products[i])

    normed_part = sum(dot(inner_grads[i], in_weights[i], (1, 1)) for i in range(group))
    gate_part = lax.dynamic_update_slice(
        jnp.zeros((every, 128), F32), jnp.stack(gate_parts, axis=1), (0, base)
    )
    normed_part = lower(jnp.concatenate([normed_part, gate_part], axis=1))
    normed_sum = scatter_rows(normed_part.reshape(tps, ctxs, own, -1), 1)
    normed_sum, gate_grad = normed_sum[:, :width], normed_sum[:, width : width + experts]
    chunks = [
        lax.all_gather(lower(product_sum(*products[i])), "ctx", axis=0, tiled=False) for i in range(group)
    ]

    router_chances = jax.nn.softmax(dot(normed_two, router, (1, 0)), axis=-1)
    chance_grad = jnp.where(picks, gate_grad, 0.0)
    logit_grad = lower(
        router_chances * (chance_grad - jnp.sum(router_chances * chance_grad, axis=-1, keepdims=True))
    )
    router_part = dot(logit_grad, normed_two, (0, 0))
    normed_grad = normed_sum + dot(logit_grad, router, (1, 1))
    residual_back, second_part = norm_back(normed_grad, residual, gain_two)
    residual_grad = upstream + residual_back

    attend_grad = gather_tp(lower(residual_grad))
    exit_part = product_sum(*product_parts([([own_block(attend_grad, r, 1) for r in range(shards)], mixed)]))
    exit_head = exit_part[:, :head_size]
    for r in range(1, ctxs):
        exit_head = exit_head + receive(
            lower(exit_part[:, r * head_size : (r + 1) * head_size]), "ctx", ctxs - r
        ).astype(F32)
    mixed_grad = lower(dot(attend_grad, exit_weight, (1, 0))).reshape(tps, own, ctxs, head_size)
    parts = [mixed_grad[:, :, 0]] + [receive(mixed_grad[:, :, ctxs - j], "ctx", j) for j in range(1, ctxs)]
    mixed_grad = ahead_first(jnp.stack(parts, axis=1), lax.rem(ctxs - c, ctxs), 1)
    mixed_grad = mixed_grad.reshape(every, heads, HEAD_DIM)
    weight_grad = jnp.einsum("qhd,khd->hqk", mixed_grad, values, preferred_element_type=F32)
    score_grad = lower(chances * (weight_grad - jnp.sum(chances * weight_grad, axis=-1, keepdims=True)))
    query_grad = jnp.einsum("hqk,khd->qhd", score_grad, keys, preferred_element_type=F32) * scale
    key_grad = jnp.einsum("hqk,qhd->khd", score_grad, queries, preferred_element_type=F32) * scale
    value_grad = jnp.einsum("hqk,qhd->khd", chances_low, mixed_grad, preferred_element_type=F32)
    query_raw_grad, gain_q_part = norm_back(turn(query_grad, cosine, -sine), query_raw, gain_q)
    key_raw_grad, gain_k_part = norm_back(turn(key_grad, cosine, -sine), key_raw, gain_k)
    projected_grad = lower(
        jnp.stack([query_raw_grad, key_raw_grad, value_grad], axis=1).reshape(every, 3 * head_size)
    )
    entry_blocks = [own_block(normed_one_all, r, 1) for r in range(shards)]
    entry_head = product_sum(*product_parts([(entry_blocks, projected_grad)]))
    attention_chunk = lax.all_gather(
        lower(jnp.concatenate([entry_head, exit_head], axis=1)), "ctx", axis=0, tiled=False
    )
    first_part = dot(projected_grad, head_in, (1, 1), BF16)
    first_normed_grad = scatter_rows(first_part.reshape(tps, ctxs, own, width), 2)

    result_part = dot(after(jnp.concatenate(scaled, axis=1), mixed_grad), group_out, (1, 1), BF16)
    result_sum = scatter_rows(result_part.reshape(tps, ctxs, own, width), 2)
    layer_output = natural_rows(gather_tp(lower(residual + result_sum)))[None]

    input_back, first_part = norm_back(first_normed_grad, layer_in, gain_one)
    input_gradient = natural_rows(gather_tp(lower(residual_grad + input_back))).astype(F32)[None]

    head_part = jnp.concatenate([jnp.sum(gain_q_part, axis=(0, 1)), jnp.sum(gain_k_part, axis=(0, 1))])
    small_part = jnp.concatenate(
        [jnp.sum(second_part, axis=0)[None], jnp.sum(first_part, axis=0)[None], router_part], axis=0
    )
    small_part = jnp.concatenate([small_part, jnp.pad(head_part, (0, width - head_part.shape[0]))[None]], axis=0)
    small_sum = sum_tokens(small_part)
    head_gradient = sum_shard(small_sum[-1:, : head_part.shape[0]], 1)[0]
    small_sum = sum_shard(small_sum[:-1], 1)

    wide = jnp.moveaxis(attention_chunk, 0, 1).astype(F32)
    entry_gradient = jnp.moveaxis(
        wide[:, :, : 3 * head_size].reshape(block, ctxs, 3, head_size), 1, 2
    ).reshape(block, 3, local_width)
    exit_gradient = wide[:, :, 3 * head_size :].reshape(block, local_width)
    upward_gradient = jnp.zeros((block, experts, 2, hidden_size), F32)
    downward_gradient = jnp.zeros((block, experts, hidden_size), F32)
    for i in range(group):
        for j in range(ctxs):
            up = chunks[i][j][:, : 2 * hidden_size].astype(F32).reshape(block, 1, 2, hidden_size)
            down = chunks[i][j][:, 2 * hidden_size :].astype(F32)[:, None]
            upward_gradient = lax.dynamic_update_slice(upward_gradient, up, (0, j * group + i, 0, 0))
            downward_gradient = lax.dynamic_update_slice(downward_gradient, down, (0, j * group + i, 0))
    return (
        layer_output,
        input_gradient,
        small_sum[1],
        head_gradient,
        entry_gradient,
        exit_gradient,
        small_sum[0],
        small_sum[2:].T,
        upward_gradient,
        downward_gradient,
    )


def solution(mesh):
    return jax.shard_map(
        local,
        mesh=mesh,
        in_specs=(
            P("shard", "ctx", None),
            P("shard", None),
            P("shard", "ctx", None),
            P("shard", "ctx", None),
            P("shard"),
            P("shard"),
            P("shard", None, "tp"),
            P("shard", "tp"),
            P("shard"),
            P("shard", None),
            P("shard", None, None, "tp"),
            P("shard", None, "tp"),
        ),
        out_specs=(
            P("shard", "ctx", None),
            P("shard", "ctx", None),
            P("shard"),
            P("shard"),
            P("shard", None, "tp"),
            P("shard", "tp"),
            P("shard"),
            P("shard", None),
            P("shard", None, None, "tp"),
            P("shard", None, "tp"),
        ),
        check_vma=False,
    )
```

```python
import functools

import jax
import jax.numpy as jnp
from jax import lax
from jax.experimental import pallas as pl
from jax.experimental.pallas import tpu as pltpu
from jax.sharding import PartitionSpec as P

HEAD_DIM = 128
NORM_EPSILON = 1e-06
ROTARY_BASE = 50000.0
MASKED = -1e30
F32 = jnp.float32
BF16 = jnp.bfloat16


def lower(values):
    return values.astype(BF16)


def dot(left, right, over, out=F32):
    result = lax.dot_general(left, right, (((over[0],), (over[1],)), ((), ())), preferred_element_type=F32)
    return result.astype(out)


def receive(values, axis, distance):
    size = lax.axis_size(axis)
    return lax.ppermute(values, axis, [((i + distance) % size, i) for i in range(size)])


def swap(values, axis, bit):
    size = lax.axis_size(axis)
    return lax.ppermute(values, axis, [(i, i ^ bit) for i in range(size)])


def bits(axis):
    size = lax.axis_size(axis)
    assert size & (size - 1) == 0
    found = [1 << i for i in range(size.bit_length() - 1)]
    return found


def masks(axis):
    order = [0]
    for bit in reversed(bits(axis)):
        order = order + [m ^ bit for m in order]
    return order


def gather_tp(values):
    for bit in reversed(bits("tp")):
        values = jnp.concatenate([values, swap(values, "tp", bit)], axis=0)
    return values


def scatter_tp(values):
    for bit in bits("tp"):
        half = values.shape[0] // 2
        values = values[:half].astype(F32) + swap(lower(values[half:]), "tp", bit).astype(F32)
    return values


def gather_ctx(values):
    size = lax.axis_size("ctx")
    whole = jnp.concatenate([values] + [receive(values, "ctx", r) for r in range(1, size)], axis=0)
    return ahead_first(whole, lax.rem(size - lax.axis_index("ctx"), size) * values.shape[0])


def greet(peers, neighbours):
    barrier = pltpu.get_barrier_semaphore()
    for peer in peers:
        pl.semaphore_signal(barrier, inc=1, device_id=peer, device_id_type=pl.DeviceIdType.MESH)
    for there, peer in neighbours:

        @pl.when(there)
        def _():
            pl.semaphore_signal(barrier, inc=1, device_id=peer, device_id_type=pl.DeviceIdType.MESH)

    pl.semaphore_wait(barrier, len(peers) + sum(jnp.where(there, 1, 0) for there, _ in neighbours))


def remote(source, target, sent, arrived, place, peer):
    return pltpu.make_async_remote_copy(
        src_ref=source,
        dst_ref=target,
        send_sem=sent.at[place],
        recv_sem=arrived.at[place],
        device_id=peer,
        device_id_type=pl.DeviceIdType.MESH,
    )


def far_first(size):
    return sorted(range(1, size), key=lambda r: min(r, size - r))


def gather_kernel(size, pieces, arrays, shared, earlier, *refs):
    owns, outs = refs[:arrays], refs[arrays + earlier : 2 * arrays + earlier]
    held = refs[2 * arrays + earlier : 3 * arrays + earlier]
    local, z_sent, z_here, x_sent, x_here, core_sent, core_here = refs[3 * arrays + earlier :]
    c, t = lax.axis_index("ctx"), lax.axis_index("tp")
    x_peer, core_peer = {"tp": t ^ 2}, {"tp": t ^ 1}
    before, behind = {"ctx": lax.max(c - 1, 0)}, {"ctx": lax.min(c + 1, size - 1)}
    greet([x_peer, core_peer], ((c > 0, before), (c < size - 1, behind)))
    rows = outs[0].shape[2]
    step = rows // pieces
    cuts = [pl.ds(h * step, step) for h in range(pieces)]
    loads, keeps, z, x, core, places = [], [], {}, {}, {}, {}
    for n in range(arrays):
        loads.append(pltpu.make_async_copy(owns[n], held[n], local.at[n * 5 + 4]))
        for m in range(4 if shared else 1):
            part = held[n].at[pl.ds(pl.multiple_of((t ^ masks("tp")[m]) * rows, rows), rows)] if shared else held[n]
            keeps.append(pltpu.make_async_copy(part, outs[n].at[m, c], local.at[n * 5 + m]))
    for n in range(arrays):
        for r in range(size):
            for side in range(2 if r else 1):
                spot = lax.rem((c + r if side else c + size - r), size)
                for h in range(pieces):
                    key = (n, r, side, h)
                    place = (n * size + r) * pieces + h
                    if r:
                        source = outs[n].at[0, spot, cuts[h]]
                    else:
                        source = owns[n].at[pl.ds(pl.multiple_of(t * rows + h * step, step) if shared else h * step, step)]
                    there = [outs[n].at[m, spot, cuts[h]] for m in range(4)]
                    count = arrays * size * pieces
                    if r < size - 1:
                        for way in (0, 1) if r == 0 else (side,):
                            z[key + (way,)] = remote(
                                source, there[0], z_sent, z_here, way * count + place, before if way else behind
                            )
                    near = (n * size + spot) * pieces + h
                    if shared and not r:
                        continue
                    x[key] = remote(source, there[1], x_sent, x_here, near, x_peer)
                    core[(0,) + key] = remote(source, there[2], core_sent, core_here, near, core_peer)
                    core[(1,) + key] = remote(there[1], there[3], core_sent, core_here, count + near, core_peer)
                    if r:
                        places[key] = remote(
                            source, there[0], z_sent, z_here, side * count + place - pieces, before if side else behind
                        )

    def go_on(way):
        return c > 0 if way else c < size - 1

    pieces_of = [(n, h) for n in range(arrays) for h in range(pieces)]
    for n, h in pieces_of:
        for way in range(2):

            @pl.when(go_on(way))
            def _():
                z[n, 0, 0, h, way].start()

    for load in loads:
        load.start()
    if not shared:
        for n, h in pieces_of:
            x[n, 0, 0, h].start()
            core[0, n, 0, 0, h].start()
    for load in loads:
        load.wait()
    for keep in keeps:
        keep.start()
    arrivals = [(n, r, side, h) for r in range(1, size) for n in range(arrays) for side in range(2) for h in range(pieces)]

    def there_is(key):
        return c + key[1] < size if key[2] else c >= key[1]

    for key in arrivals:

        @pl.when(there_is(key))
        def _():
            places[key].wait_recv()
            if key[1] < size - 1:

                @pl.when(go_on(key[2]))
                def _():
                    z[key + (key[2],)].start()

            x[key].start()
            core[(0,) + key].start()

    if not shared:
        for n, h in pieces_of:
            x[n, 0, 0, h].wait_recv()
            core[1, n, 0, 0, h].start()
    for key in arrivals:

        @pl.when(there_is(key))
        def _():
            x[key].wait_recv()
            core[(1,) + key].start()

    if not shared:
        for n, h in pieces_of:
            x[n, 0, 0, h].wait_send()
            core[0, n, 0, 0, h].wait()
            core[1, n, 0, 0, h].wait()
    for key in arrivals:

        @pl.when(there_is(key))
        def _():
            x[key].wait_send()
            core[(0,) + key].wait()
            core[(1,) + key].wait()
            if key[1] < size - 1:

                @pl.when(go_on(key[2]))
                def _():
                    z[key + (key[2],)].wait_send()

    for n, h in pieces_of:
        for way in range(2):

            @pl.when(go_on(way))
            def _():
                z[n, 0, 0, h, way].wait_send()

    for keep in keeps:
        keep.wait()


def gather_rows(values, collective, *earlier, shared=False):
    size, tps = lax.axis_size("ctx"), lax.axis_size("tp")
    assert tps == 4
    pieces, arrays = 2, len(values)
    rows = values[0].shape[0] // (tps if shared else 1)
    count = arrays * size * pieces
    anywhere = pl.BlockSpec(memory_space=pl.ANY)
    return pl.pallas_call(
        functools.partial(gather_kernel, size, pieces, arrays, shared, len(earlier)),
        out_shape=[jax.ShapeDtypeStruct((tps, size, rows, v.shape[1]), v.dtype) for v in values],
        in_specs=[anywhere] * (arrays + len(earlier)),
        out_specs=[anywhere] * arrays,
        scratch_shapes=[pltpu.VMEM(v.shape, v.dtype) for v in values]
        + [
            pltpu.SemaphoreType.DMA((n,))
            for n in (5 * arrays, 2 * count, 2 * count, count, count, 2 * count, 2 * count)
        ],
        compiler_params=pltpu.CompilerParams(collective_id=collective, has_side_effects=True),
        name="gather_rows",
    )(*values, *earlier)


def scatter_kernel(size, earlier, parts, *refs):
    out, held, core_in, x_in, z_in, local, z_sent, z_here, x_sent, x_here, core_sent, core_here = refs[earlier:]
    c, t = lax.axis_index("ctx"), lax.axis_index("tp")
    x_peer, core_peer = {"tp": t ^ 2}, {"tp": t ^ 1}
    first, last = c == 0, c == size - 1
    upper = c // (size // 2)
    spot = [size - 1 - k + upper * (2 * k - size + 1) for k in range(size)]
    before, behind = {"ctx": lax.max(c - 1, 0)}, {"ctx": lax.min(c + 1, size - 1)}
    greet([x_peer, core_peer], ((jnp.logical_not(first), before), (jnp.logical_not(last), behind)))
    keep = pltpu.make_async_copy(parts.at[pl.ds(0, 2)], held, local)
    keep.start()
    core = {
        (m, k): remote(parts.at[2 + m, spot[k]], core_in.at[m, k], core_sent, core_here, m * size + k, core_peer)
        for m in (1, 0)
        for k in range(size)
    }
    x = [remote(held.at[1, spot[k]], x_in.at[k], x_sent, x_here, k, x_peer) for k in range(size)]
    rising = [remote(held.at[0, spot[k]], z_in.at[0, spot[k]], z_sent, z_here, spot[k], behind) for k in range(size)]
    falling = [
        remote(held.at[0, spot[k]], z_in.at[1, spot[k]], z_sent, z_here, size + spot[k], before) for k in range(size)
    ]
    for copy in core.values():
        copy.start()
    keep.wait()
    tall = 16

    def each(body):
        @pl.loop(0, out.shape[0] // tall)
        def _(i):
            body(pl.ds(pl.multiple_of(i * tall, tall), tall))

    for k in range(size):
        a = spot[k]
        core[1, k].wait_recv()

        def add_core(rows):
            held[1, a, rows] = (held[1, a, rows].astype(F32) + core_in[1, k, rows].astype(F32)).astype(BF16)

        each(add_core)
        x[k].start()
    for k in range(size):
        a = spot[k]
        core[0, k].wait_recv()
        x[k].wait_recv()

        def total(rows):
            return held[0, a, rows].astype(F32) + core_in[0, k, rows].astype(F32) + x_in[k, rows].astype(F32)

        def add(rows):
            held[0, a, rows] = total(rows).astype(BF16)

        def add_rising(rows):
            held[0, a, rows] = (total(rows) + z_in[0, a, rows].astype(F32)).astype(BF16)

        def add_falling(rows):
            held[0, a, rows] = (total(rows) + z_in[1, a, rows].astype(F32)).astype(BF16)

        def keep_total(rows):
            out[rows] = total(rows)

        @pl.when(a == c)
        def _():
            each(keep_total)

        @pl.when(a > c)
        def _():
            @pl.when(first)
            def _():
                each(add)

            @pl.when(jnp.logical_not(first))
            def _():
                rising[k].wait_recv()
                each(add_rising)

            rising[k].start()

        @pl.when(a < c)
        def _():
            @pl.when(last)
            def _():
                each(add)

            @pl.when(jnp.logical_not(last))
            def _():
                falling[k].wait_recv()
                each(add_falling)

            falling[k].start()

    for side, edge in enumerate((first, last)):

        @pl.when(jnp.logical_not(edge))
        def _():
            remote(
                held.at[0, c], z_in.at[side, c], z_sent, z_here, side * size + c, before if side else behind
            ).wait_recv()

            def add_side(rows):
                out[rows] = out[rows] + z_in[side, c, rows].astype(F32)

            each(add_side)

    for copy in list(core.values()) + x:
        copy.wait_send()
    for k in range(size):

        @pl.when(spot[k] > c)
        def _():
            rising[k].wait_send()

        @pl.when(spot[k] < c)
        def _():
            falling[k].wait_send()


def scatter_rows(parts, collective, *earlier):
    size = lax.axis_size("ctx")
    rows, width = parts.shape[2:]
    return pl.pallas_call(
        functools.partial(scatter_kernel, size, len(earlier)),
        out_shape=jax.ShapeDtypeStruct((rows, width), F32),
        in_specs=[pl.BlockSpec(memory_space=pl.ANY)] * (1 + len(earlier)),
        out_specs=pl.BlockSpec(memory_space=pltpu.VMEM),
        scratch_shapes=[
            pltpu.VMEM((2, size, rows, width), BF16),
            pltpu.VMEM((2, size, rows, width), BF16),
            pltpu.VMEM((size, rows, width), BF16),
            pltpu.VMEM((2, size, rows, width), BF16),
            pltpu.SemaphoreType.DMA(()),
        ]
        + [pltpu.SemaphoreType.DMA((n,)) for n in (2 * size, 2 * size, size, size, 2 * size, 2 * size)],
        compiler_params=pltpu.CompilerParams(
            collective_id=collective, has_side_effects=True, vmem_limit_bytes=40 * 1024 * 1024
        ),
        name="scatter_rows",
    )(parts, *earlier)


def sum_tokens(values):
    size = lax.axis_size("ctx")
    for bit in bits("tp"):
        values = values + swap(values, "tp", bit)
    found = jnp.stack([values] + [receive(values, "ctx", r) for r in range(1, size)])
    return jnp.sum(ahead_first(found, lax.rem(size - lax.axis_index("ctx"), size)), axis=0)


def own_block(values, ahead=0, axis=0):
    size = lax.axis_size("shard")
    block = values.shape[axis] // size
    spot = lax.rem(lax.axis_index("shard") + ahead, size)
    return lax.dynamic_slice_in_dim(values, spot * block, block, axis=axis)


def sum_shard(values, axis):
    size = lax.axis_size("shard")
    total = own_block(values, 0, axis)
    for r in range(1, size):
        total = total + receive(own_block(values, r, axis), "shard", size - r)
    return total


def product_parts(pairs):
    own = jnp.concatenate([dot(lefts[0], right, (0, 0)) for lefts, right in pairs], axis=1)
    others = tuple(
        jnp.concatenate([dot(lefts[r], right, (0, 0), BF16) for lefts, right in pairs], axis=1)
        for r in range(1, lax.axis_size("shard"))
    )
    return own, others


def product_sum(own, others):
    size = lax.axis_size("shard")
    for r in range(1, size):
        own = own + receive(others[r - 1], "shard", size - r).astype(F32)
    return own


def ahead_first(values, start, axis=0):
    return lax.dynamic_slice_in_dim(
        jnp.concatenate([values, values], axis=axis), start, values.shape[axis], axis=axis
    )


def gather_natural(values, axis_name, axis=0):
    return lax.all_gather(values, axis_name, axis=axis, tiled=True)


def gather_small(values, axis):
    size = lax.axis_size("shard")
    whole = jnp.concatenate([values] + [receive(values, "shard", r) for r in range(1, size)], axis=axis)
    return ahead_first(whole, lax.rem(size - lax.axis_index("shard"), size) * values.shape[axis], axis)


def corner(values):
    return values[(0,) * values.ndim]


def start_after(values):
    first = corner(values)
    return (first != first).astype(jnp.int32)


def tie(values, earlier):
    return values + (corner(earlier).astype(F32) * 0.0).astype(values.dtype)


def part_order(values):
    t = lax.axis_index("tp")
    return jnp.concatenate([lax.dynamic_index_in_dim(values, t ^ m, 1, False)[None] for m in masks("tp")], axis=0)


def natural_rows(values):
    t, order = lax.axis_index("tp"), masks("tp")
    part = values.shape[0] // len(order)
    found = []
    for q in range(len(order)):
        m, place = q ^ t, 0
        for i, bit in enumerate(reversed(bits("tp"))):
            place = place + jnp.where(m & bit, 1 << i, 0)
        found.append(lax.dynamic_slice_in_dim(values, place * part, part))
    return jnp.concatenate(found, axis=0)


def inverse_scale(values):
    return lax.rsqrt(jnp.mean(values * values, axis=-1, keepdims=True) + NORM_EPSILON)


def turn(values, cosine, sine):
    half = values.shape[-1] // 2
    front, back = values[..., :half], values[..., half:]
    return jnp.concatenate([front * cosine - back * sine, back * cosine + front * sine], axis=-1)


def norm_back(grad, values, gain):
    scale = inverse_scale(values)
    weighted = grad * gain
    middle = jnp.mean(values * weighted, axis=-1, keepdims=True)
    return scale * weighted - values * (scale * scale * scale) * middle, grad * values * scale


def expert_kernel(group, tall, hidden, *refs):
    chunks, up, down, up_rows, down_rows = refs[:group], *refs[group:]
    pieces = hidden // 128
    ctxs = chunks[0].shape[0]
    experts = group * ctxs
    for i in range(group):
        for j in range(ctxs):
            e = j * group + i
            for p in range(2 * pieces):
                side, piece = p // pieces, p % pieces
                value = chunks[i][j, :, p * 128 : p * 128 + 128].astype(F32)
                up_rows[pl.ds((e * pieces + piece) * 2 + side, tall, stride=experts * pieces * 2), :] = value
            for piece in range(pieces):
                value = chunks[i][j, :, (2 * pieces + piece) * 128 : (2 * pieces + piece) * 128 + 128].astype(F32)
                row = (e // 8 * pieces + piece) * 8 + e % 8
                down_rows[pl.ds(row, tall, stride=experts * pieces), :] = value
    up[...] = up_rows[...].reshape(up.shape)
    down[...] = down_rows[...].reshape(down.shape)


def expert_gradients(chunks):
    group = len(chunks)
    ctxs, rows, width = chunks[0].shape
    hidden, experts = width // 3, group * ctxs
    pieces = hidden // 128
    assert experts % 8 == 0 and hidden % 128 == 0
    tall = 32
    up, down = pl.pallas_call(
        functools.partial(expert_kernel, group, tall, hidden),
        grid=(rows // tall,),
        in_specs=[pl.BlockSpec((ctxs, tall, width), lambda b: (0, b, 0))] * group,
        out_specs=[
            pl.BlockSpec((tall, experts * pieces * 2, 128), lambda b: (b, 0, 0)),
            pl.BlockSpec((tall, experts * pieces, 128), lambda b: (b, 0, 0)),
        ],
        out_shape=[
            jax.ShapeDtypeStruct((rows, experts * pieces * 2, 128), F32),
            jax.ShapeDtypeStruct((rows, experts * pieces, 128), F32),
        ],
        scratch_shapes=[
            pltpu.VMEM((tall * experts * pieces * 2, 128), F32),
            pltpu.VMEM((tall * experts * pieces, 128), F32),
        ],
        compiler_params=pltpu.CompilerParams(vmem_limit_bytes=32 * 1024 * 1024),
        name="expert_gradients",
    )(*chunks)
    up = up.reshape(rows, experts, pieces, 2, 128).transpose(0, 1, 3, 2, 4).reshape(rows, experts, 2, hidden)
    down = down.reshape(rows, experts // 8, pieces, 8, 128).transpose(0, 1, 3, 2, 4).reshape(rows, experts, hidden)
    return up, down


def attention_kernel(chunk, entry, exit_out):
    ctxs, _, width = chunk.shape
    head = width // 4
    for j in range(ctxs):
        for k in range(3):
            entry[k, :, j * head : (j + 1) * head] = chunk[j, :, k * head : (k + 1) * head].astype(F32)
        exit_out[:, j * head : (j + 1) * head] = chunk[j, :, 3 * head :].astype(F32)


def attention_gradients(chunk):
    ctxs, rows, width = chunk.shape
    wide = ctxs * width // 4
    tall = 128
    entry, exit_out = pl.pallas_call(
        attention_kernel,
        grid=(rows // tall,),
        in_specs=[pl.BlockSpec((ctxs, tall, width), lambda b: (0, b, 0))],
        out_specs=[pl.BlockSpec((3, tall, wide), lambda b: (0, b, 0)), pl.BlockSpec((tall, wide), lambda b: (b, 0))],
        out_shape=[jax.ShapeDtypeStruct((3, rows, wide), F32), jax.ShapeDtypeStruct((rows, wide), F32)],
        name="attention_gradients",
    )(chunk)
    return entry.transpose(1, 0, 2), exit_out


def local(
    tokens,
    segments,
    routes,
    cotangent,
    first_gain,
    head_gain,
    attention_in,
    attention_out,
    second_gain,
    router_weight,
    expert_in,
    expert_out,
):
    s, c, t = lax.axis_index("shard"), lax.axis_index("ctx"), lax.axis_index("tp")
    shards, ctxs, tps = lax.axis_size("shard"), lax.axis_size("ctx"), lax.axis_size("tp")
    rows, width = tokens.shape[1:]
    own = rows // tps
    block = width // shards
    every = rows * ctxs
    experts = router_weight.shape[1]
    hidden_size = expert_out.shape[2]
    local_width = attention_out.shape[1]
    head_size = local_width // ctxs
    heads = head_size // HEAD_DIM

    group = experts // ctxs
    base = c * group

    gains = gather_small(jnp.stack([first_gain, second_gain]), 1).astype(F32)
    gain_one, gain_two = gains[0], gains[1]
    head_gains = gather_small(head_gain[None], 1)[0].astype(F32)
    head_in = lax.dynamic_slice_in_dim(attention_in, c * head_size, head_size, axis=2)
    head_in = gather_natural(head_in.reshape(block, 3 * head_size), "shard")
    exit_weight = gather_natural(ahead_first(attention_out, c * head_size, 1), "shard")

    def expert_weights(start, count):
        inward = lax.dynamic_slice_in_dim(expert_in, start, count, axis=1)
        outward = lax.dynamic_slice_in_dim(expert_out, start, count, axis=1)
        inward = [inward[:, i].reshape(block, 2 * hidden_size) for i in range(count)]
        outward = outward.reshape(block, count * hidden_size)
        return inward, outward

    first = t * own
    tokens_own = lax.dynamic_slice_in_dim(tokens[0], first, own)
    cot_own = lax.dynamic_slice_in_dim(cotangent[0], first, own)
    inward, outward = expert_weights(base, 1)
    tokens_all, cot_all = gather_rows([tokens[0], cotangent[0]], 3, inward[0], outward, shared=True)
    tokens_all, cot_all = tokens_all.reshape(every, width), cot_all.reshape(every, width)
    in_weights = [gather_natural(inward[0], "shard")]
    out_weights = [gather_natural(outward, "shard")]

    layer_in = tokens_own.astype(F32)
    upstream = cot_own.astype(F32)
    choices_all = gather_ctx(routes[0]).reshape(ctxs, tps, own, -1)
    picks_all = jnp.any(part_order(choices_all)[..., None] == jnp.arange(experts), axis=3)
    picks = lax.dynamic_index_in_dim(picks_all[0], c, 0, False)
    picks_all = picks_all.reshape(every, experts)
    router = gather_small(router_weight, 0)

    tokens_wide = tokens_all.astype(F32)
    normed_one_all = lower(tokens_wide * inverse_scale(tokens_wide) * gain_one)
    spot = part_order(jnp.arange(every, dtype=jnp.int32).reshape(ctxs, tps, own)).reshape(-1)
    documents = part_order(segments[0].reshape(ctxs, tps, own)).reshape(-1)
    steps = jnp.arange(HEAD_DIM // 2).astype(F32)
    frequency = ROTARY_BASE ** (-2.0 * steps / HEAD_DIM)
    angles = spot.astype(F32)[:, None] * frequency[None, :]
    cosine, sine = jnp.cos(angles)[:, None], jnp.sin(angles)[:, None]
    projected = dot(normed_one_all, head_in, (1, 0)).reshape(every, 3, heads, HEAD_DIM)
    query_raw, key_raw = projected[:, 0], projected[:, 1]
    gain_q, gain_k = head_gains[:HEAD_DIM], head_gains[HEAD_DIM:]
    queries = lower(turn(query_raw * inverse_scale(query_raw) * gain_q, cosine, sine))
    keys = lower(turn(key_raw * inverse_scale(key_raw) * gain_k, cosine, sine))
    values = lower(projected[:, 2])
    scale = HEAD_DIM ** (-0.5)
    scores = jnp.einsum("qhd,khd->hqk", queries, keys, preferred_element_type=F32) * scale
    same = documents[:, None] == documents[None, :]
    chances = jax.nn.softmax(jnp.where(same[None], scores, MASKED), axis=-1)
    chances_low = lower(chances)
    mixed_head = lower(jnp.einsum("hqk,khd->qhd", chances_low, values, preferred_element_type=F32))
    blocks = ahead_first(mixed_head.reshape(tps, ctxs, own, head_size), c, 1)
    mixed = [blocks[:, 0]] + [receive(blocks[:, ctxs - j], "ctx", j) for j in range(1, ctxs)]
    mixed = jnp.concatenate([m.reshape(rows, head_size) for m in mixed], axis=1)
    inward, outward = expert_weights(base + 1 + start_after(mixed), group - 1)
    in_weights.append(gather_natural(inward[0], "shard"))
    outward = gather_natural(outward, "shard")
    out_weights += [outward[:, i * hidden_size : (i + 1) * hidden_size] for i in range(group - 1)]
    in_weights += [gather_natural(inward[i], "shard") for i in range(1, group - 1)]
    residual = layer_in + scatter_tp(dot(mixed, exit_weight, (1, 1)))

    normed_two = lower(residual * inverse_scale(residual) * gain_two)
    normed_two_all = gather_rows([normed_two], 0)[0].reshape(every, width)
    chances_all = jax.nn.softmax(dot(normed_two_all, router, (1, 0)), axis=-1)
    gates = jnp.where(picks_all, chances_all, 0.0)
    gates = lax.dynamic_slice_in_dim(gates, base, group, axis=1)
    normed_blocks = [own_block(normed_two_all, r, 1) for r in range(shards)]
    cot_blocks = [own_block(cot_all, r, 1) for r in range(shards)]
    scaled, gate_parts, inner_grads, products, chunks, gathered = [], [], [], [], [], []

    def finish(i):
        own_part, others = products[i]
        chunks.append(lower(product_sum(tie(own_part, products[-1][1][0]), others)))
        chunk = chunks[i] if i < 2 else tie(chunks[i], gathered[i - 2])
        gathered.append(lax.all_gather(chunk, "ctx", axis=0, tiled=False))

    for i in range(group):
        gate_up = dot(normed_two_all, in_weights[i], (1, 0))
        gate, up = gate_up[:, :hidden_size], gate_up[:, hidden_size:]
        back = dot(cot_all, out_weights[i], (1, 0))
        sigmoid = jax.nn.sigmoid(gate)
        silu = gate * sigmoid
        hidden = lower(silu * up).astype(F32)
        weight = gates[:, i : i + 1]
        if i >= 2:
            weight = tie(weight, chunks[max(i - 3, 0)])
        scaled.append(lower(hidden * weight))
        gate_parts.append(jnp.sum(hidden * back, axis=1))
        hidden_grad = back * weight
        inner_grads.append(
            lower(
                jnp.concatenate(
                    [hidden_grad * up * sigmoid * (1.0 + gate * (1.0 - sigmoid)), hidden_grad * silu], axis=1
                )
            )
        )
        products.append(product_parts([(normed_blocks, inner_grads[i]), (cot_blocks, scaled[i])]))
        if i != 1:
            finish(max(i - 1, 0))
    finish(group - 1)

    normed_part = sum(dot(inner_grads[i], in_weights[i], (1, 1)) for i in range(group))
    gate_part = lax.dynamic_update_slice(
        jnp.zeros((every, 128), F32), jnp.stack(gate_parts, axis=1), (0, base)
    )
    normed_part = lower(jnp.concatenate([normed_part, gate_part], axis=1))
    normed_sum = scatter_rows(normed_part.reshape(tps, ctxs, own, -1), 1, chunks[-2])
    result_part = lower(sum(dot(scaled[i], out_weights[i], (1, 1)) for i in range(group)))
    result_sum = scatter_rows(result_part.reshape(tps, ctxs, own, width), 2, normed_sum)
    normed_sum, gate_grad = normed_sum[:, :width], normed_sum[:, width : width + experts]

    router_chances = jax.nn.softmax(dot(normed_two, router, (1, 0)), axis=-1)
    chance_grad = jnp.where(picks, gate_grad, 0.0)
    logit_grad = lower(
        router_chances * (chance_grad - jnp.sum(router_chances * chance_grad, axis=-1, keepdims=True))
    )
    router_part = dot(logit_grad, normed_two, (0, 0))
    normed_grad = normed_sum + dot(logit_grad, router, (1, 1))
    residual_back, second_part = norm_back(normed_grad, residual, gain_two)
    residual_grad = upstream + residual_back

    attend_grad = gather_tp(lower(residual_grad))
    exit_part = product_sum(*product_parts([([own_block(attend_grad, r, 1) for r in range(shards)], mixed)]))
    exit_head = exit_part[:, :head_size]
    for r in range(1, ctxs):
        exit_head = exit_head + receive(
            lower(exit_part[:, r * head_size : (r + 1) * head_size]), "ctx", ctxs - r
        ).astype(F32)
    mixed_grad = lower(dot(attend_grad, exit_weight, (1, 0))).reshape(tps, own, ctxs, head_size)
    parts = [mixed_grad[:, :, 0]] + [receive(mixed_grad[:, :, ctxs - j], "ctx", j) for j in range(1, ctxs)]
    mixed_grad = ahead_first(jnp.stack(parts, axis=1), lax.rem(ctxs - c, ctxs), 1)
    mixed_grad = mixed_grad.reshape(every, heads, HEAD_DIM)
    weight_grad = jnp.einsum("qhd,khd->hqk", mixed_grad, values, preferred_element_type=F32)
    score_grad = lower(chances * (weight_grad - jnp.sum(chances * weight_grad, axis=-1, keepdims=True)))
    query_grad = jnp.einsum("hqk,khd->qhd", score_grad, keys, preferred_element_type=F32) * scale
    key_grad = jnp.einsum("hqk,qhd->khd", score_grad, queries, preferred_element_type=F32) * scale
    value_grad = jnp.einsum("hqk,qhd->khd", chances_low, mixed_grad, preferred_element_type=F32)
    query_raw_grad, gain_q_part = norm_back(turn(query_grad, cosine, -sine), query_raw, gain_q)
    key_raw_grad, gain_k_part = norm_back(turn(key_grad, cosine, -sine), key_raw, gain_k)
    projected_grad = lower(
        jnp.stack([query_raw_grad, key_raw_grad, value_grad], axis=1).reshape(every, 3 * head_size)
    )
    entry_blocks = [own_block(normed_one_all, r, 1) for r in range(shards)]
    entry_head = product_sum(*product_parts([(entry_blocks, projected_grad)]))
    attention_chunk = tie(lower(jnp.concatenate([entry_head, exit_head], axis=1)), gathered[-2])
    attention_chunk = lax.all_gather(attention_chunk, "ctx", axis=0, tiled=False)
    first_part = dot(projected_grad, head_in, (1, 1), BF16)
    first_normed_grad = scatter_rows(first_part.reshape(tps, ctxs, own, width), 4, chunks[-1])

    layer_output = natural_rows(gather_tp(lower(residual + result_sum)))[None]

    input_back, first_part = norm_back(first_normed_grad, layer_in, gain_one)
    input_gradient = natural_rows(gather_tp(lower(residual_grad + input_back))).astype(F32)[None]

    head_part = jnp.concatenate([jnp.sum(gain_q_part, axis=(0, 1)), jnp.sum(gain_k_part, axis=(0, 1))])
    small_part = jnp.concatenate(
        [jnp.sum(second_part, axis=0)[None], jnp.sum(first_part, axis=0)[None], router_part], axis=0
    )
    small_part = jnp.concatenate([small_part, jnp.pad(head_part, (0, width - head_part.shape[0]))[None]], axis=0)
    small_sum = sum_tokens(small_part)
    head_gradient = sum_shard(small_sum[-1:, : head_part.shape[0]], 1)[0]
    small_sum = sum_shard(small_sum[:-1], 1)

    upward_gradient, downward_gradient = expert_gradients(gathered)
    entry_gradient, exit_gradient = attention_gradients(attention_chunk)
    return (
        layer_output,
        input_gradient,
        small_sum[1],
        head_gradient,
        entry_gradient,
        exit_gradient,
        small_sum[0],
        small_sum[2:].T,
        upward_gradient,
        downward_gradient,
    )


def solution(mesh):
    return jax.shard_map(
        local,
        mesh=mesh,
        in_specs=(
            P("shard", "ctx", None),
            P("shard", None),
            P("shard", "ctx", None),
            P("shard", "ctx", None),
            P("shard"),
            P("shard"),
            P("shard", None, "tp"),
            P("shard", "tp"),
            P("shard"),
            P("shard", None),
            P("shard", None, None, "tp"),
            P("shard", None, "tp"),
        ),
        out_specs=(
            P("shard", "ctx", None),
            P("shard", "ctx", None),
            P("shard"),
            P("shard"),
            P("shard", None, "tp"),
            P("shard", "tp"),
            P("shard"),
            P("shard", None),
            P("shard", None, None, "tp"),
            P("shard", None, "tp"),
        ),
        check_vma=False,
    )
```

```python
import functools

import jax
import jax.numpy as jnp
from jax import lax
from jax.experimental import pallas as pl
from jax.experimental.pallas import tpu as pltpu
from jax.sharding import PartitionSpec as P

HEAD_DIM = 128
NORM_EPSILON = 1e-06
ROTARY_BASE = 50000.0
MASKED = -1e30
F32 = jnp.float32
BF16 = jnp.bfloat16


def lower(values):
    return values.astype(BF16)


def dot(left, right, over, out=F32):
    result = lax.dot_general(left, right, (((over[0],), (over[1],)), ((), ())), preferred_element_type=F32)
    return result.astype(out)


def receive(values, axis, distance):
    size = lax.axis_size(axis)
    return lax.ppermute(values, axis, [((i + distance) % size, i) for i in range(size)])


def swap(values, axis, bit):
    size = lax.axis_size(axis)
    return lax.ppermute(values, axis, [(i, i ^ bit) for i in range(size)])


def bits(axis):
    size = lax.axis_size(axis)
    assert size & (size - 1) == 0
    found = [1 << i for i in range(size.bit_length() - 1)]
    return found


def masks(axis):
    order = [0]
    for bit in reversed(bits(axis)):
        order = order + [m ^ bit for m in order]
    return order


def gather_tp(values):
    for bit in reversed(bits("tp")):
        values = jnp.concatenate([values, swap(values, "tp", bit)], axis=0)
    return values


def scatter_tp(values):
    for bit in bits("tp"):
        half = values.shape[0] // 2
        values = values[:half].astype(F32) + swap(lower(values[half:]), "tp", bit).astype(F32)
    return values


def gather_ctx(values):
    size = lax.axis_size("ctx")
    whole = jnp.concatenate([values] + [receive(values, "ctx", r) for r in range(1, size)], axis=0)
    return ahead_first(whole, lax.rem(size - lax.axis_index("ctx"), size) * values.shape[0])


def greet(peers, neighbours):
    barrier = pltpu.get_barrier_semaphore()
    for peer in peers:
        pl.semaphore_signal(barrier, inc=1, device_id=peer, device_id_type=pl.DeviceIdType.MESH)
    for there, peer in neighbours:

        @pl.when(there)
        def _():
            pl.semaphore_signal(barrier, inc=1, device_id=peer, device_id_type=pl.DeviceIdType.MESH)

    pl.semaphore_wait(barrier, len(peers) + sum(jnp.where(there, 1, 0) for there, _ in neighbours))


def remote(source, target, sent, arrived, place, peer):
    return pltpu.make_async_remote_copy(
        src_ref=source,
        dst_ref=target,
        send_sem=sent.at[place],
        recv_sem=arrived.at[place],
        device_id=peer,
        device_id_type=pl.DeviceIdType.MESH,
    )


def far_first(size):
    return sorted(range(1, size), key=lambda r: min(r, size - r))


def gather_kernel(size, pieces, arrays, shared, earlier, *refs):
    owns, outs = refs[:arrays], refs[arrays + earlier : 2 * arrays + earlier]
    held = refs[2 * arrays + earlier : 3 * arrays + earlier]
    local, z_sent, z_here, x_sent, x_here, core_sent, core_here = refs[3 * arrays + earlier :]
    c, t = lax.axis_index("ctx"), lax.axis_index("tp")
    x_peer, core_peer = {"tp": t ^ 2}, {"tp": t ^ 1}
    before, behind = {"ctx": lax.max(c - 1, 0)}, {"ctx": lax.min(c + 1, size - 1)}
    greet([x_peer, core_peer], ((c > 0, before), (c < size - 1, behind)))
    rows = outs[0].shape[2]
    step = rows // pieces
    cuts = [pl.ds(h * step, step) for h in range(pieces)]
    loads, keeps, z, x, core, places = [], [], {}, {}, {}, {}
    for n in range(arrays):
        loads.append(pltpu.make_async_copy(owns[n], held[n], local.at[n * 5 + 4]))
        for m in range(4 if shared else 1):
            part = held[n].at[pl.ds(pl.multiple_of((t ^ masks("tp")[m]) * rows, rows), rows)] if shared else held[n]
            keeps.append(pltpu.make_async_copy(part, outs[n].at[m, c], local.at[n * 5 + m]))
    for n in range(arrays):
        for r in range(size):
            for side in range(2 if r else 1):
                spot = lax.rem((c + r if side else c + size - r), size)
                for h in range(pieces):
                    key = (n, r, side, h)
                    place = (n * size + r) * pieces + h
                    if r:
                        source = outs[n].at[0, spot, cuts[h]]
                    else:
                        source = owns[n].at[pl.ds(pl.multiple_of(t * rows + h * step, step) if shared else h * step, step)]
                    there = [outs[n].at[m, spot, cuts[h]] for m in range(4)]
                    count = arrays * size * pieces
                    if r < size - 1:
                        for way in (0, 1) if r == 0 else (side,):
                            z[key + (way,)] = remote(
                                source, there[0], z_sent, z_here, way * count + place, before if way else behind
                            )
                    near = (n * size + spot) * pieces + h
                    if shared and not r:
                        continue
                    x[key] = remote(source, there[1], x_sent, x_here, near, x_peer)
                    core[(0,) + key] = remote(source, there[2], core_sent, core_here, near, core_peer)
                    core[(1,) + key] = remote(there[1], there[3], core_sent, core_here, count + near, core_peer)
                    if r:
                        places[key] = remote(
                            source, there[0], z_sent, z_here, side * count + place - pieces, before if side else behind
                        )

    def go_on(way):
        return c > 0 if way else c < size - 1

    pieces_of = [(n, h) for n in range(arrays) for h in range(pieces)]
    for n, h in pieces_of:
        for way in range(2):

            @pl.when(go_on(way))
            def _():
                z[n, 0, 0, h, way].start()

    for load in loads:
        load.start()
    if not shared:
        for n, h in pieces_of:
            x[n, 0, 0, h].start()
            core[0, n, 0, 0, h].start()
    for load in loads:
        load.wait()
    for keep in keeps:
        keep.start()
    arrivals = [(n, r, side, h) for r in range(1, size) for n in range(arrays) for side in range(2) for h in range(pieces)]

    def there_is(key):
        return c + key[1] < size if key[2] else c >= key[1]

    for key in arrivals:

        @pl.when(there_is(key))
        def _():
            places[key].wait_recv()
            if key[1] < size - 1:

                @pl.when(go_on(key[2]))
                def _():
                    z[key + (key[2],)].start()

            x[key].start()
            core[(0,) + key].start()

    if not shared:
        for n, h in pieces_of:
            x[n, 0, 0, h].wait_recv()
            core[1, n, 0, 0, h].start()
    for key in arrivals:

        @pl.when(there_is(key))
        def _():
            x[key].wait_recv()
            core[(1,) + key].start()

    if not shared:
        for n, h in pieces_of:
            x[n, 0, 0, h].wait_send()
            core[0, n, 0, 0, h].wait()
            core[1, n, 0, 0, h].wait()
    for key in arrivals:

        @pl.when(there_is(key))
        def _():
            x[key].wait_send()
            core[(0,) + key].wait()
            core[(1,) + key].wait()
            if key[1] < size - 1:

                @pl.when(go_on(key[2]))
                def _():
                    z[key + (key[2],)].wait_send()

    for n, h in pieces_of:
        for way in range(2):

            @pl.when(go_on(way))
            def _():
                z[n, 0, 0, h, way].wait_send()

    for keep in keeps:
        keep.wait()


def gather_rows(values, collective, *earlier, shared=False):
    size, tps = lax.axis_size("ctx"), lax.axis_size("tp")
    assert tps == 4
    pieces, arrays = 2, len(values)
    rows = values[0].shape[0] // (tps if shared else 1)
    count = arrays * size * pieces
    anywhere = pl.BlockSpec(memory_space=pl.ANY)
    return pl.pallas_call(
        functools.partial(gather_kernel, size, pieces, arrays, shared, len(earlier)),
        out_shape=[jax.ShapeDtypeStruct((tps, size, rows, v.shape[1]), v.dtype) for v in values],
        in_specs=[anywhere] * (arrays + len(earlier)),
        out_specs=[anywhere] * arrays,
        scratch_shapes=[pltpu.VMEM(v.shape, v.dtype) for v in values]
        + [
            pltpu.SemaphoreType.DMA((n,))
            for n in (5 * arrays, 2 * count, 2 * count, count, count, 2 * count, 2 * count)
        ],
        compiler_params=pltpu.CompilerParams(collective_id=collective, has_side_effects=True),
        name="gather_rows",
    )(*values, *earlier)


def scatter_kernel(size, arrays, earlier, *refs):
    parts = refs[:arrays]
    outs, refs = refs[arrays + earlier : 2 * arrays + earlier], refs[2 * arrays + earlier :]
    helds, core_ins, x_ins, z_ins = [refs[k * arrays : (k + 1) * arrays] for k in range(4)]
    local, z_sent, z_here, x_sent, x_here, core_sent, core_here = refs[4 * arrays :]
    c, t = lax.axis_index("ctx"), lax.axis_index("tp")
    x_peer, core_peer = {"tp": t ^ 2}, {"tp": t ^ 1}
    first, last = c == 0, c == size - 1
    upper = c // (size // 2)
    spot = [size - 1 - k + upper * (2 * k - size + 1) for k in range(size)]
    before, behind = {"ctx": lax.max(c - 1, 0)}, {"ctx": lax.min(c + 1, size - 1)}
    greet([x_peer, core_peer], ((jnp.logical_not(first), before), (jnp.logical_not(last), behind)))
    keeps, core, x, rising, falling, finals = [], {}, {}, {}, {}, {}
    for n in range(arrays):
        part, held, core_in, x_in, z_in = parts[n], helds[n], core_ins[n], x_ins[n], z_ins[n]
        keeps.append(pltpu.make_async_copy(part.at[pl.ds(0, 2)], held, local.at[n]))
        for m in (1, 0):
            for k in range(size):
                core[n, m, k] = remote(
                    part.at[2 + m, spot[k]], core_in.at[m, k], core_sent, core_here, (n * 2 + m) * size + k, core_peer
                )
        for k in range(size):
            a = spot[k]
            x[n, k] = remote(held.at[1, a], x_in.at[k], x_sent, x_here, n * size + k, x_peer)
            rising[n, k] = remote(held.at[0, a], z_in.at[0, a], z_sent, z_here, 2 * n * size + a, behind)
            falling[n, k] = remote(held.at[0, a], z_in.at[1, a], z_sent, z_here, (2 * n + 1) * size + a, before)
        finals[n] = [
            remote(held.at[0, c], z_in.at[0, c], z_sent, z_here, 2 * n * size + c, behind),
            remote(held.at[0, c], z_in.at[1, c], z_sent, z_here, (2 * n + 1) * size + c, before),
        ]
    for copy in core.values():
        copy.start()
    for keep in keeps:
        keep.start()
    for keep in keeps:
        keep.wait()
    tall = 16

    def each(body):
        @pl.loop(0, outs[0].shape[0] // tall)
        def _(i):
            body(pl.ds(pl.multiple_of(i * tall, tall), tall))

    order = [(n, k) for n in range(arrays) for k in range(size)]
    for n, k in order:
        a, held, core_in = spot[k], helds[n], core_ins[n]
        core[n, 1, k].wait_recv()

        def add_core(rows):
            held[1, a, rows] = (held[1, a, rows].astype(F32) + core_in[1, k, rows].astype(F32)).astype(BF16)

        each(add_core)
        x[n, k].start()
    for n, k in order:
        a, held, core_in, x_in, z_in, out = spot[k], helds[n], core_ins[n], x_ins[n], z_ins[n], outs[n]
        core[n, 0, k].wait_recv()
        x[n, k].wait_recv()

        def total(rows):
            return held[0, a, rows].astype(F32) + core_in[0, k, rows].astype(F32) + x_in[k, rows].astype(F32)

        def add(rows):
            held[0, a, rows] = total(rows).astype(BF16)

        def add_rising(rows):
            held[0, a, rows] = (total(rows) + z_in[0, a, rows].astype(F32)).astype(BF16)

        def add_falling(rows):
            held[0, a, rows] = (total(rows) + z_in[1, a, rows].astype(F32)).astype(BF16)

        def keep_total(rows):
            out[rows] = total(rows)

        @pl.when(a == c)
        def _():
            each(keep_total)

        @pl.when(a > c)
        def _():
            @pl.when(first)
            def _():
                each(add)

            @pl.when(jnp.logical_not(first))
            def _():
                rising[n, k].wait_recv()
                each(add_rising)

            rising[n, k].start()

        @pl.when(a < c)
        def _():
            @pl.when(last)
            def _():
                each(add)

            @pl.when(jnp.logical_not(last))
            def _():
                falling[n, k].wait_recv()
                each(add_falling)

            falling[n, k].start()

    for n in range(arrays):
        for side, edge in enumerate((first, last)):
            z_in, out = z_ins[n], outs[n]

            @pl.when(jnp.logical_not(edge))
            def _():
                finals[n][side].wait_recv()

                def add_side(rows):
                    out[rows] = out[rows] + z_in[side, c, rows].astype(F32)

                each(add_side)

    for copy in list(core.values()) + list(x.values()):
        copy.wait_send()
    for n, k in order:

        @pl.when(spot[k] > c)
        def _():
            rising[n, k].wait_send()

        @pl.when(spot[k] < c)
        def _():
            falling[n, k].wait_send()


def scatter_rows(parts, collective, *earlier):
    size, arrays = lax.axis_size("ctx"), len(parts)
    rows, width = parts[0].shape[2:]
    return pl.pallas_call(
        functools.partial(scatter_kernel, size, arrays, len(earlier)),
        out_shape=[jax.ShapeDtypeStruct((rows, width), F32)] * arrays,
        in_specs=[pl.BlockSpec(memory_space=pl.ANY)] * (arrays + len(earlier)),
        out_specs=[pl.BlockSpec(memory_space=pltpu.VMEM)] * arrays,
        scratch_shapes=[pltpu.VMEM((2, size, rows, width), BF16)] * (2 * arrays)
        + [pltpu.VMEM((size, rows, width), BF16)] * arrays
        + [pltpu.VMEM((2, size, rows, width), BF16)] * arrays
        + [
            pltpu.SemaphoreType.DMA((arrays * n,))
            for n in (1, 2 * size, 2 * size, size, size, 2 * size, 2 * size)
        ],
        compiler_params=pltpu.CompilerParams(
            collective_id=collective, has_side_effects=True, vmem_limit_bytes=48 * 1024 * 1024
        ),
        name="scatter_rows",
    )(*parts, *earlier)


def sum_tokens(values):
    size = lax.axis_size("ctx")
    for bit in bits("tp"):
        values = values + swap(values, "tp", bit)
    found = jnp.stack([values] + [receive(values, "ctx", r) for r in range(1, size)])
    return jnp.sum(ahead_first(found, lax.rem(size - lax.axis_index("ctx"), size)), axis=0)


def own_block(values, ahead=0, axis=0):
    size = lax.axis_size("shard")
    block = values.shape[axis] // size
    spot = lax.rem(lax.axis_index("shard") + ahead, size)
    return lax.dynamic_slice_in_dim(values, spot * block, block, axis=axis)


def sum_shard(values, axis):
    size = lax.axis_size("shard")
    total = own_block(values, 0, axis)
    for r in range(1, size):
        total = total + receive(own_block(values, r, axis), "shard", size - r)
    return total


def product_parts(pairs):
    own = jnp.concatenate([dot(lefts[0], right, (0, 0)) for lefts, right in pairs], axis=1)
    others = tuple(
        jnp.concatenate([dot(lefts[r], right, (0, 0), BF16) for lefts, right in pairs], axis=1)
        for r in range(1, lax.axis_size("shard"))
    )
    return own, others


def product_sum(own, others):
    size = lax.axis_size("shard")
    for r in range(1, size):
        own = own + receive(others[r - 1], "shard", size - r).astype(F32)
    return own


def ahead_first(values, start, axis=0):
    return lax.dynamic_slice_in_dim(
        jnp.concatenate([values, values], axis=axis), start, values.shape[axis], axis=axis
    )


def gather_natural(values, axis_name, axis=0):
    return lax.all_gather(values, axis_name, axis=axis, tiled=True)


def gather_small(values, axis):
    size = lax.axis_size("shard")
    whole = jnp.concatenate([values] + [receive(values, "shard", r) for r in range(1, size)], axis=axis)
    return ahead_first(whole, lax.rem(size - lax.axis_index("shard"), size) * values.shape[axis], axis)


def corner(values):
    return values[(0,) * values.ndim]


def start_after(values):
    first = corner(values)
    return (first != first).astype(jnp.int32)


def tie(values, earlier):
    return values + (corner(earlier).astype(F32) * 0.0).astype(values.dtype)


def part_order(values):
    t = lax.axis_index("tp")
    return jnp.concatenate([lax.dynamic_index_in_dim(values, t ^ m, 1, False)[None] for m in masks("tp")], axis=0)


def natural_rows(values):
    t, order = lax.axis_index("tp"), masks("tp")
    part = values.shape[0] // len(order)
    found = []
    for q in range(len(order)):
        m, place = q ^ t, 0
        for i, bit in enumerate(reversed(bits("tp"))):
            place = place + jnp.where(m & bit, 1 << i, 0)
        found.append(lax.dynamic_slice_in_dim(values, place * part, part))
    return jnp.concatenate(found, axis=0)


def inverse_scale(values):
    return lax.rsqrt(jnp.mean(values * values, axis=-1, keepdims=True) + NORM_EPSILON)


def norm_back(grad, values, gain):
    scale = inverse_scale(values)
    weighted = grad * gain
    middle = jnp.mean(values * weighted, axis=-1, keepdims=True)
    return scale * weighted - values * (scale * scale * scale) * middle, grad * values * scale


def weights_kernel(ctxs, group, pieces, index, inward, outward, entry, *refs):
    exits, (first, others, head, leave) = refs[:ctxs], refs[ctxs:]
    c = index[0]
    tall = first.shape[0]
    deep = 16
    in_rows, out_rows = inward.shape[1], outward.shape[1]
    out_experts = 8
    half = lax.rem(c, out_experts // group) * group

    def picker(rows, kept, place):
        count = kept * deep
        to = lax.broadcasted_iota(jnp.int32, (count, rows * deep), 0)
        source = lax.broadcasted_iota(jnp.int32, (count, rows * deep), 1)
        return (source == to % deep * rows + place(to // deep)).astype(BF16)

    in_pick = picker(in_rows, in_rows, lambda row: row)
    kept = group * pieces
    out_pick = picker(out_rows, kept, lambda row: row // group * out_experts + half + row % group)

    def put(i, column, rows, value):
        if i:
            column = column + (i - 1) * 3 * pieces * 128
        (others if i else first)[rows, column : column + 128] = value

    for step in range(tall // deep):
        rows = slice(step * deep, (step + 1) * deep)
        moved = matmul(in_pick, inward[rows].reshape(deep * in_rows, 128)).astype(BF16)
        for row in range(in_rows):
            i, piece, side = row // (2 * pieces), row // 2 % pieces, row % 2
            put(i, (side * pieces + piece) * 128, rows, moved[row * deep : (row + 1) * deep])
        moved = matmul(out_pick, outward[rows].reshape(deep * out_rows, 128)).astype(BF16)
        for row in range(kept):
            i, piece = row % group, row // group
            put(i, (2 * pieces + piece) * 128, rows, moved[row * deep : (row + 1) * deep])
    for k in range(3):
        head[:, k * HEAD_DIM : (k + 1) * HEAD_DIM] = entry[k]
    for j in range(ctxs):
        leave[:, j * HEAD_DIM : (j + 1) * HEAD_DIM] = exits[j][...]


def own_weights(expert_in, expert_out, attention_in, attention_out):
    c, ctxs = lax.axis_index("ctx"), lax.axis_size("ctx")
    rows, experts, _, hidden = expert_in.shape
    group, pieces = experts // ctxs, hidden // 128
    assert group in (1, 2, 4, 8) and group * 2 * pieces % 16 == 0 and 8 * pieces % 16 == 0
    inward = expert_in.reshape(rows, experts, 2, pieces, 128).transpose(0, 1, 3, 2, 4).reshape(rows, -1, 128)
    outward = expert_out.reshape(rows, experts // 8, 8, pieces, 128).transpose(0, 1, 3, 2, 4).reshape(rows, -1, 128)
    entry = attention_in.transpose(1, 0, 2)
    tall = 64
    wide = 3 * hidden
    grid_spec = pltpu.PrefetchScalarGridSpec(
        num_scalar_prefetch=1,
        grid=(rows // tall,),
        in_specs=[
            pl.BlockSpec((tall, group * 2 * pieces, 128), lambda b, c: (b, c[0], 0)),
            pl.BlockSpec((tall, 8 * pieces, 128), lambda b, c: (b, c[0] * group // 8, 0)),
            pl.BlockSpec((3, tall, HEAD_DIM), lambda b, c: (0, b, c[0])),
        ]
        + [
            pl.BlockSpec((tall, HEAD_DIM), functools.partial(lambda j, b, c: (b, lax.rem(c[0] + j, ctxs)), j))
            for j in range(ctxs)
        ],
        out_specs=[
            pl.BlockSpec((tall, n), lambda b, c: (b, 0))
            for n in (wide, (group - 1) * wide, 3 * HEAD_DIM, ctxs * HEAD_DIM)
        ],
    )
    return pl.pallas_call(
        functools.partial(weights_kernel, ctxs, group, pieces),
        grid_spec=grid_spec,
        out_shape=[
            jax.ShapeDtypeStruct((rows, n), BF16)
            for n in (wide, (group - 1) * wide, 3 * HEAD_DIM, ctxs * HEAD_DIM)
        ],
        compiler_params=pltpu.CompilerParams(vmem_limit_bytes=48 * 1024 * 1024),
        name="own_weights",
    )(c.astype(jnp.int32)[None], inward, outward, entry, *([attention_out] * ctxs))


def matmul(left, right, over=(1, 0)):
    return lax.dot_general(left, right, (((over[0],), (over[1],)), ((), ())), preferred_element_type=F32)


def head_norm(values):
    return lax.rsqrt(jnp.mean(values * values, axis=-1, keepdims=True) + NORM_EPSILON)


def turned(values, cosine, sine):
    return values * cosine + pltpu.roll(values, values.shape[-1] // 2, 1) * sine


def project_kernel(tokens, gain, weight, gains, cosine, sine, normed, raw, query, key, value):
    values = tokens[...].astype(F32)
    low = (values * head_norm(values) * gain[...]).astype(BF16)
    normed[...] = low
    projected = matmul(low, weight[...])
    raw[...] = projected[:, : 2 * HEAD_DIM]
    for k, out in enumerate((query, key)):
        part = projected[:, k * HEAD_DIM : (k + 1) * HEAD_DIM]
        part = part * head_norm(part) * gains[k : k + 1, :]
        out[...] = turned(part, cosine[...], sine[...]).astype(BF16)
    value[...] = projected[:, 2 * HEAD_DIM :].astype(BF16)


def project(tokens, gain, weight, gains, cosine, sine):
    rows, width = tokens.shape
    tall = 256
    block = lambda n: pl.BlockSpec((tall, n), lambda b: (b, 0))
    whole = lambda v: pl.BlockSpec(v.shape, lambda b: (0, 0))
    head = jax.ShapeDtypeStruct((rows, HEAD_DIM), BF16)
    return pl.pallas_call(
        project_kernel,
        grid=(rows // tall,),
        in_specs=[block(width), whole(gain), whole(weight), whole(gains), block(HEAD_DIM), block(HEAD_DIM)],
        out_specs=[block(width), block(2 * HEAD_DIM)] + [block(HEAD_DIM)] * 3,
        out_shape=[
            jax.ShapeDtypeStruct((rows, width), BF16),
            jax.ShapeDtypeStruct((rows, 2 * HEAD_DIM), F32),
            head,
            head,
            head,
        ],
        compiler_params=pltpu.CompilerParams(vmem_limit_bytes=48 * 1024 * 1024),
        name="project",
    )(tokens, gain, weight, gains, cosine, sine)


def chances_of(query, key, row_doc, column_doc):
    scores = matmul(query, key, (1, 1)) * (HEAD_DIM**-0.5)
    scores = jnp.where(row_doc == column_doc, scores, MASKED)
    grown = jnp.exp(scores - jnp.max(scores, axis=-1, keepdims=True))
    return grown / jnp.sum(grown, axis=-1, keepdims=True)


def attend_kernel(query, key, value, row_doc, column_doc, mixed):
    chances = chances_of(query[...], key[...], row_doc[...], column_doc[...])
    mixed[...] = matmul(chances.astype(BF16), value[...]).astype(BF16)


def attend(query, key, value, row_doc, column_doc):
    rows = query.shape[0]
    tall = 256
    block = pl.BlockSpec((tall, HEAD_DIM), lambda b: (b, 0))
    whole = pl.BlockSpec((rows, HEAD_DIM), lambda b: (0, 0))
    return pl.pallas_call(
        attend_kernel,
        grid=(rows // tall,),
        in_specs=[
            block,
            whole,
            whole,
            pl.BlockSpec((tall, 1), lambda b: (b, 0)),
            pl.BlockSpec((1, rows), lambda b: (0, 0)),
        ],
        out_specs=block,
        out_shape=jax.ShapeDtypeStruct((rows, HEAD_DIM), BF16),
        compiler_params=pltpu.CompilerParams(vmem_limit_bytes=48 * 1024 * 1024),
        name="attend",
    )(query, key, value, row_doc, column_doc)


def attend_back_kernel(
    tall, query, key, value, raw, cosine, sine, gains, row_doc, column_doc, mixed_grad, grad, gain_grad, key_grad, value_grad
):
    step = pl.program_id(0)
    rows = pl.ds(pl.multiple_of(step * tall, tall), tall)

    def projected_back(turned_grad, k, where):
        values = raw[where, k * HEAD_DIM : (k + 1) * HEAD_DIM]
        grown = turned(turned_grad, cosine[where], -sine[where])
        scale = head_norm(values)
        weighted = grown * gains[k : k + 1, :]
        middle = jnp.mean(values * weighted, axis=-1, keepdims=True)
        part = jnp.sum(grown * values * scale, axis=0, keepdims=True)
        return scale * weighted - values * (scale * scale * scale) * middle, part

    @pl.when(step == 0)
    def _():
        key_grad[...] = jnp.zeros_like(key_grad)
        value_grad[...] = jnp.zeros_like(value_grad)
        gain_grad[...] = jnp.zeros_like(gain_grad)

    here = query[...]
    chances = chances_of(here, key[...], row_doc[...], column_doc[...])
    upstream = mixed_grad[...]
    weight_grad = matmul(upstream, value[...], (1, 1))
    score_grad = chances * (weight_grad - jnp.sum(chances * weight_grad, axis=-1, keepdims=True))
    score_grad = score_grad.astype(BF16)
    scale = HEAD_DIM**-0.5
    query_grad, part = projected_back(matmul(score_grad, key[...]) * scale, 0, rows)
    grad[rows, :HEAD_DIM] = query_grad.astype(BF16)
    gain_grad[0:1, :] += part
    key_grad[...] += matmul(score_grad, here, (0, 0)) * scale
    value_grad[...] += matmul(chances.astype(BF16), upstream, (0, 0))

    @pl.when(step == pl.num_programs(0) - 1)
    def _():
        back, part = projected_back(key_grad[...], 1, slice(None))
        grad[:, HEAD_DIM : 2 * HEAD_DIM] = back.astype(BF16)
        gain_grad[1:2, :] += part
        grad[:, 2 * HEAD_DIM :] = value_grad[...].astype(BF16)


def attend_back(query, key, value, raw, cosine, sine, gains, row_doc, column_doc, mixed_grad):
    rows = query.shape[0]
    tall = 256
    block = pl.BlockSpec((tall, HEAD_DIM), lambda b: (b, 0))
    whole = lambda v: pl.BlockSpec(v.shape, lambda b: (0, 0))
    return pl.pallas_call(
        functools.partial(attend_back_kernel, tall),
        grid=(rows // tall,),
        in_specs=[
            block,
            whole(key),
            whole(value),
            whole(raw),
            whole(cosine),
            whole(sine),
            whole(gains),
            pl.BlockSpec((tall, 1), lambda b: (b, 0)),
            whole(column_doc),
            block,
        ],
        out_specs=[
            pl.BlockSpec((rows, 3 * HEAD_DIM), lambda b: (0, 0)),
            pl.BlockSpec((8, HEAD_DIM), lambda b: (0, 0)),
        ],
        out_shape=[
            jax.ShapeDtypeStruct((rows, 3 * HEAD_DIM), BF16),
            jax.ShapeDtypeStruct((8, HEAD_DIM), F32),
        ],
        scratch_shapes=[pltpu.VMEM((rows, HEAD_DIM), F32)] * 2,
        compiler_params=pltpu.CompilerParams(vmem_limit_bytes=48 * 1024 * 1024),
        name="attend_back",
    )(query, key, value, raw, cosine, sine, gains, row_doc, column_doc, mixed_grad)


def expert_step_kernel(index, earlier, rows, upstream, gate_in, up_in, outward, gates, *refs):
    scaled, inner_grad, gate_part = refs[earlier:]
    hidden_size = outward.shape[1]
    gate, up = matmul(rows[...], gate_in[...]), matmul(rows[...], up_in[...])
    back = matmul(upstream[...], outward[...])
    sigmoid = 1.0 / (1.0 + jnp.exp(-gate))
    silu = gate * sigmoid
    hidden = (silu * up).astype(BF16).astype(F32)
    weight = gates[:, index : index + 1]
    scaled[...] = (hidden * weight).astype(BF16)
    lane = lax.broadcasted_iota(jnp.int32, gate_part.shape, 1)
    gate_part[...] = jnp.where(lane == index, jnp.sum(hidden * back, axis=1, keepdims=True), 0.0)
    hidden_grad = back * weight
    inner_grad[:, :hidden_size] = (hidden_grad * up * sigmoid * (1.0 + gate * (1.0 - sigmoid))).astype(BF16)
    inner_grad[:, hidden_size:] = (hidden_grad * silu).astype(BF16)


def expert_step(index, place, rows, upstream, weights, hidden_size, gates, *earlier):
    count, width = rows.shape
    tall = 256
    block = lambda n: pl.BlockSpec((tall, n), lambda b: (b, 0))
    column = lambda k: pl.BlockSpec((width, hidden_size), lambda b: (0, 3 * place + k))
    return pl.pallas_call(
        functools.partial(expert_step_kernel, index, len(earlier)),
        grid=(count // tall,),
        in_specs=[block(width), block(width), column(0), column(1), column(2), block(gates.shape[1])]
        + [pl.BlockSpec(memory_space=pl.ANY)] * len(earlier),
        out_specs=[block(hidden_size), block(2 * hidden_size), block(128)],
        out_shape=[
            jax.ShapeDtypeStruct((count, hidden_size), BF16),
            jax.ShapeDtypeStruct((count, 2 * hidden_size), BF16),
            jax.ShapeDtypeStruct((count, 128), F32),
        ],
        compiler_params=pltpu.CompilerParams(vmem_limit_bytes=48 * 1024 * 1024),
        name="expert_step",
    )(rows, upstream, weights, weights, weights, gates, *earlier)


def expert_kernel(group, tall, hidden, *refs):
    chunks, up, down, up_rows, down_rows = refs[:group], *refs[group:]
    pieces = hidden // 128
    ctxs = chunks[0].shape[0]
    experts = group * ctxs
    for i in range(group):
        for j in range(ctxs):
            e = j * group + i
            for p in range(2 * pieces):
                side, piece = p // pieces, p % pieces
                value = chunks[i][j, :, p * 128 : p * 128 + 128].astype(F32)
                up_rows[pl.ds((e * pieces + piece) * 2 + side, tall, stride=experts * pieces * 2), :] = value
            for piece in range(pieces):
                value = chunks[i][j, :, (2 * pieces + piece) * 128 : (2 * pieces + piece) * 128 + 128].astype(F32)
                row = (e // 8 * pieces + piece) * 8 + e % 8
                down_rows[pl.ds(row, tall, stride=experts * pieces), :] = value
    up[...] = up_rows[...].reshape(up.shape)
    down[...] = down_rows[...].reshape(down.shape)


def expert_gradients(chunks):
    group = len(chunks)
    ctxs, rows, width = chunks[0].shape
    hidden, experts = width // 3, group * ctxs
    pieces = hidden // 128
    assert experts % 8 == 0 and hidden % 128 == 0
    tall = 32
    up, down = pl.pallas_call(
        functools.partial(expert_kernel, group, tall, hidden),
        grid=(rows // tall,),
        in_specs=[pl.BlockSpec((ctxs, tall, width), lambda b: (0, b, 0))] * group,
        out_specs=[
            pl.BlockSpec((tall, experts * pieces * 2, 128), lambda b: (b, 0, 0)),
            pl.BlockSpec((tall, experts * pieces, 128), lambda b: (b, 0, 0)),
        ],
        out_shape=[
            jax.ShapeDtypeStruct((rows, experts * pieces * 2, 128), F32),
            jax.ShapeDtypeStruct((rows, experts * pieces, 128), F32),
        ],
        scratch_shapes=[
            pltpu.VMEM((tall * experts * pieces * 2, 128), F32),
            pltpu.VMEM((tall * experts * pieces, 128), F32),
        ],
        compiler_params=pltpu.CompilerParams(vmem_limit_bytes=32 * 1024 * 1024),
        name="expert_gradients",
    )(*chunks)
    up = up.reshape(rows, experts, pieces, 2, 128).transpose(0, 1, 3, 2, 4).reshape(rows, experts, 2, hidden)
    down = down.reshape(rows, experts // 8, pieces, 8, 128).transpose(0, 1, 3, 2, 4).reshape(rows, experts, hidden)
    return up, down


def attention_kernel(chunk, entry, exit_out):
    ctxs, _, width = chunk.shape
    head = width // 4
    for j in range(ctxs):
        for k in range(3):
            entry[k, :, j * head : (j + 1) * head] = chunk[j, :, k * head : (k + 1) * head].astype(F32)
        exit_out[:, j * head : (j + 1) * head] = chunk[j, :, 3 * head :].astype(F32)


def attention_gradients(chunk):
    ctxs, rows, width = chunk.shape
    wide = ctxs * width // 4
    tall = 128
    entry, exit_out = pl.pallas_call(
        attention_kernel,
        grid=(rows // tall,),
        in_specs=[pl.BlockSpec((ctxs, tall, width), lambda b: (0, b, 0))],
        out_specs=[pl.BlockSpec((3, tall, wide), lambda b: (0, b, 0)), pl.BlockSpec((tall, wide), lambda b: (b, 0))],
        out_shape=[jax.ShapeDtypeStruct((3, rows, wide), F32), jax.ShapeDtypeStruct((rows, wide), F32)],
        name="attention_gradients",
    )(chunk)
    return entry.transpose(1, 0, 2), exit_out


def local(
    tokens,
    segments,
    routes,
    cotangent,
    first_gain,
    head_gain,
    attention_in,
    attention_out,
    second_gain,
    router_weight,
    expert_in,
    expert_out,
):
    s, c, t = lax.axis_index("shard"), lax.axis_index("ctx"), lax.axis_index("tp")
    shards, ctxs, tps = lax.axis_size("shard"), lax.axis_size("ctx"), lax.axis_size("tp")
    rows, width = tokens.shape[1:]
    own = rows // tps
    block = width // shards
    every = rows * ctxs
    experts = router_weight.shape[1]
    hidden_size = expert_out.shape[2]
    local_width = attention_out.shape[1]
    head_size = local_width // ctxs

    group = experts // ctxs
    base = c * group

    gains = gather_small(jnp.stack([first_gain, second_gain]), 1).astype(F32)
    gain_one, gain_two = gains[0], gains[1]
    head_gains = gather_small(head_gain[None], 1)[0].astype(F32)
    first_weights, others, head_in, exit_weight = own_weights(expert_in, expert_out, attention_in, attention_out)
    tokens_all, cot_all = gather_rows([tokens[0], cotangent[0]], 3, head_in, shared=True)
    tokens_all, cot_all = tokens_all.reshape(every, width), cot_all.reshape(every, width)
    head_in = gather_natural(head_in, "shard")
    first_weights, others = gather_natural(first_weights, "shard"), gather_natural(others, "shard")
    exit_weight = gather_small(exit_weight, 0)
    columns = lambda i, start, count: (others if i else first_weights)[
        :, (3 * max(i - 1, 0) + start) * hidden_size : (3 * max(i - 1, 0) + start + count) * hidden_size
    ]
    in_weights = [columns(i, 0, 2) for i in range(group)]
    out_weights = [columns(i, 2, 1) for i in range(group)]
    first = t * own
    tokens_own = lax.dynamic_slice_in_dim(tokens[0], first, own)
    cot_own = lax.dynamic_slice_in_dim(cotangent[0], first, own)

    layer_in = tokens_own.astype(F32)
    upstream = cot_own.astype(F32)
    choices_all = gather_ctx(routes[0]).reshape(ctxs, tps, own, -1)
    picks_all = jnp.any(part_order(choices_all)[..., None] == jnp.arange(experts), axis=3)
    picks = lax.dynamic_index_in_dim(picks_all[0], c, 0, False)
    picks_all = picks_all.reshape(every, experts)
    router = gather_small(router_weight, 0)

    assert head_size == HEAD_DIM
    spot = part_order(jnp.arange(every, dtype=jnp.int32).reshape(ctxs, tps, own)).reshape(-1)
    documents = part_order(segments[0].reshape(ctxs, tps, own)).reshape(-1)
    row_doc, column_doc = documents[:, None], documents[None, :]
    steps = jnp.arange(HEAD_DIM // 2).astype(F32)
    frequency = ROTARY_BASE ** (-2.0 * steps / HEAD_DIM)
    angles = spot.astype(F32)[:, None] * frequency[None, :]
    cosine, sine = jnp.cos(angles), jnp.sin(angles)
    cosine, sine = jnp.concatenate([cosine, cosine], axis=1), jnp.concatenate([-sine, sine], axis=1)
    head_gains = head_gains.reshape(2, HEAD_DIM)
    normed_one_all, raw, queries, keys, values = project(
        tokens_all, gain_one[None], head_in, head_gains, cosine, sine
    )
    mixed_head = attend(queries, keys, values, row_doc, column_doc)
    blocks = ahead_first(mixed_head.reshape(tps, ctxs, own, head_size), c, 1)
    mixed = [blocks[:, 0]] + [receive(blocks[:, ctxs - j], "ctx", j) for j in range(1, ctxs)]
    mixed = jnp.concatenate([m.reshape(rows, head_size) for m in mixed], axis=1)
    residual = layer_in + scatter_tp(dot(mixed, exit_weight, (1, 1)))

    normed_two = lower(residual * inverse_scale(residual) * gain_two)
    normed_two_all = gather_rows([normed_two], 0)[0].reshape(every, width)
    chances_all = jax.nn.softmax(dot(normed_two_all, router, (1, 0)), axis=-1)
    gates = jnp.where(picks_all, chances_all, 0.0)
    gates = lax.dynamic_slice_in_dim(gates, base, group, axis=1)
    normed_blocks = [own_block(normed_two_all, r, 1) for r in range(shards)]
    cot_blocks = [own_block(cot_all, r, 1) for r in range(shards)]
    scaled, gate_parts, inner_grads, products, chunks, gathered = [], [], [], [], [], []

    def finish(i, later):
        own_part, others = products[i]
        chunks.append(lower(product_sum(tie(own_part, later), others)))
        chunk = chunks[i] if i < 2 else tie(chunks[i], gathered[i - 2])
        gathered.append(lax.all_gather(chunk, "ctx", axis=0, tiled=False))

    for i in range(group):
        before = [] if i == 0 else list(products[i - 1][1])
        step = expert_step(
            i, max(i - 1, 0), normed_two_all, cot_all, others if i else first_weights, hidden_size, gates, *before
        )
        scaled.append(step[0])
        inner_grads.append(step[1])
        gate_parts.append(step[2])
        products.append(product_parts([(normed_blocks, inner_grads[i]), (cot_blocks, scaled[i])]))
    early = min(2, group)
    for i in range(early):
        finish(i, products[min(2 * i + 1, group - 1)][1][0])
    normed_part = sum(dot(inner_grads[i], in_weights[i], (1, 1)) for i in range(group))
    gate_part = lax.dynamic_update_slice(
        jnp.zeros((every, 128), F32), sum(gate_parts)[:, :group], (0, base)
    )
    normed_part = lower(jnp.concatenate([normed_part, gate_part], axis=1))
    (normed_sum,) = scatter_rows([normed_part.reshape(tps, ctxs, own, -1)], 1, *chunks)
    for i in range(early, group):
        finish(i, normed_sum)
    normed_sum, gate_grad = normed_sum[:, :width], normed_sum[:, width : width + experts]

    router_chances = jax.nn.softmax(dot(normed_two, router, (1, 0)), axis=-1)
    chance_grad = jnp.where(picks, gate_grad, 0.0)
    logit_grad = lower(
        router_chances * (chance_grad - jnp.sum(router_chances * chance_grad, axis=-1, keepdims=True))
    )
    router_part = dot(logit_grad, normed_two, (0, 0))
    normed_grad = normed_sum + dot(logit_grad, router, (1, 1))
    residual_back, second_part = norm_back(normed_grad, residual, gain_two)
    residual_grad = upstream + residual_back

    attend_grad = gather_tp(lower(residual_grad))
    exit_part = product_sum(*product_parts([([own_block(attend_grad, r, 1) for r in range(shards)], mixed)]))
    exit_head = exit_part[:, :head_size]
    for r in range(1, ctxs):
        exit_head = exit_head + receive(
            lower(exit_part[:, r * head_size : (r + 1) * head_size]), "ctx", ctxs - r
        ).astype(F32)
    mixed_grad = lower(dot(attend_grad, exit_weight, (1, 0))).reshape(tps, own, ctxs, head_size)
    parts = [mixed_grad[:, :, 0]] + [receive(mixed_grad[:, :, ctxs - j], "ctx", j) for j in range(1, ctxs)]
    mixed_grad = ahead_first(jnp.stack(parts, axis=1), lax.rem(ctxs - c, ctxs), 1)
    mixed_grad = mixed_grad.reshape(every, HEAD_DIM)
    projected_grad, gain_part = attend_back(
        queries, keys, values, raw, cosine, sine, head_gains, row_doc, column_doc, mixed_grad
    )
    entry_blocks = [own_block(normed_one_all, r, 1) for r in range(shards)]
    entry_head = product_sum(*product_parts([(entry_blocks, projected_grad)]))
    attention_chunk = lower(jnp.concatenate([entry_head, exit_head], axis=1))
    attention_gathered = lax.all_gather(tie(attention_chunk, gathered[-2]), "ctx", axis=0, tiled=False)

    result_part = lower(sum(dot(tie(scaled[i], projected_grad), out_weights[i], (1, 1)) for i in range(group)))
    first_part = dot(projected_grad, head_in, (1, 1), BF16)
    first_normed_grad, result_sum = scatter_rows(
        [part.reshape(tps, ctxs, own, width) for part in (first_part, result_part)], 2, attention_chunk
    )
    layer_output = natural_rows(gather_tp(lower(residual + result_sum)))[None]

    input_back, first_part = norm_back(first_normed_grad, layer_in, gain_one)
    input_gradient = natural_rows(gather_tp(lower(residual_grad + input_back))).astype(F32)[None]

    head_part = gain_part[:2].reshape(-1)
    small_part = jnp.concatenate(
        [jnp.sum(second_part, axis=0)[None], jnp.sum(first_part, axis=0)[None], router_part], axis=0
    )
    small_part = jnp.concatenate([small_part, jnp.pad(head_part, (0, width - head_part.shape[0]))[None]], axis=0)
    small_sum = sum_tokens(small_part)
    head_gradient = sum_shard(small_sum[-1:, : head_part.shape[0]], 1)[0]
    small_sum = sum_shard(small_sum[:-1], 1)

    upward_gradient, downward_gradient = expert_gradients(gathered)
    entry_gradient, exit_gradient = attention_gradients(attention_gathered)
    return (
        layer_output,
        input_gradient,
        small_sum[1],
        head_gradient,
        entry_gradient,
        exit_gradient,
        small_sum[0],
        small_sum[2:].T,
        upward_gradient,
        downward_gradient,
    )


def solution(mesh):
    return jax.shard_map(
        local,
        mesh=mesh,
        in_specs=(
            P("shard", "ctx", None),
            P("shard", None),
            P("shard", "ctx", None),
            P("shard", "ctx", None),
            P("shard"),
            P("shard"),
            P("shard", None, "tp"),
            P("shard", "tp"),
            P("shard"),
            P("shard", None),
            P("shard", None, None, "tp"),
            P("shard", None, "tp"),
        ),
        out_specs=(
            P("shard", "ctx", None),
            P("shard", "ctx", None),
            P("shard"),
            P("shard"),
            P("shard", None, "tp"),
            P("shard", "tp"),
            P("shard"),
            P("shard", None),
            P("shard", None, None, "tp"),
            P("shard", None, "tp"),
        ),
        check_vma=False,
    )
```

```python
import functools

import jax
import jax.numpy as jnp
from jax import lax
from jax.experimental import pallas as pl
from jax.experimental.pallas import tpu as pltpu
from jax.sharding import PartitionSpec as P

HEAD_DIM = 128
NORM_EPSILON = 1e-06
ROTARY_BASE = 50000.0
MASKED = -1e30
F32 = jnp.float32
BF16 = jnp.bfloat16
COST = pl.CostEstimate(flops=1024, bytes_accessed=1024, transcendentals=0)


def lower(values):
    return values.astype(BF16)


def dot(left, right, over, out=F32):
    result = lax.dot_general(left, right, (((over[0],), (over[1],)), ((), ())), preferred_element_type=F32)
    return result.astype(out)


def receive(values, axis, distance):
    size = lax.axis_size(axis)
    return lax.ppermute(values, axis, [((i + distance) % size, i) for i in range(size)])


def swap(values, axis, bit):
    size = lax.axis_size(axis)
    return lax.ppermute(values, axis, [(i, i ^ bit) for i in range(size)])


def bits(axis):
    size = lax.axis_size(axis)
    assert size & (size - 1) == 0
    found = [1 << i for i in range(size.bit_length() - 1)]
    return found


def masks(axis):
    order = [0]
    for bit in reversed(bits(axis)):
        order = order + [m ^ bit for m in order]
    return order


def gather_tp(values, beside=()):
    for k, bit in enumerate(reversed(bits("tp"))):
        far = swap(values, "tp", bit)
        values = jnp.concatenate([tie(values, beside[k]) if beside else values, far], axis=0)
    return values


def scatter_tp(values):
    for bit in bits("tp"):
        half = values.shape[0] // 2
        values = values[:half].astype(F32) + swap(lower(values[half:]), "tp", bit).astype(F32)
    return values


def gather_ctx(values):
    size = lax.axis_size("ctx")
    whole = jnp.concatenate([values] + [receive(values, "ctx", r) for r in range(1, size)], axis=0)
    return ahead_first(whole, lax.rem(size - lax.axis_index("ctx"), size) * values.shape[0])


def greet(peers, neighbours):
    barrier = pltpu.get_barrier_semaphore()
    for peer in peers:
        pl.semaphore_signal(barrier, inc=1, device_id=peer, device_id_type=pl.DeviceIdType.MESH)
    for there, peer in neighbours:

        @pl.when(there)
        def _():
            pl.semaphore_signal(barrier, inc=1, device_id=peer, device_id_type=pl.DeviceIdType.MESH)

    pl.semaphore_wait(barrier, len(peers) + sum(jnp.where(there, 1, 0) for there, _ in neighbours))


def remote(source, target, sent, arrived, place, peer):
    return pltpu.make_async_remote_copy(
        src_ref=source,
        dst_ref=target,
        send_sem=sent.at[place],
        recv_sem=arrived.at[place],
        device_id=peer,
        device_id_type=pl.DeviceIdType.MESH,
    )


def far_first(size):
    return sorted(range(1, size), key=lambda r: min(r, size - r))


def gather_kernel(size, pieces, arrays, shared, earlier, *refs):
    owns, outs = refs[:arrays], refs[arrays + earlier : 2 * arrays + earlier]
    held = refs[2 * arrays + earlier : 3 * arrays + earlier]
    local, z_sent, z_here, x_sent, x_here, core_sent, core_here = refs[3 * arrays + earlier :]
    c, t = lax.axis_index("ctx"), lax.axis_index("tp")
    x_peer, core_peer = {"tp": t ^ 2}, {"tp": t ^ 1}
    before, behind = {"ctx": lax.max(c - 1, 0)}, {"ctx": lax.min(c + 1, size - 1)}
    greet([x_peer, core_peer], ((c > 0, before), (c < size - 1, behind)))
    rows = outs[0].shape[2]
    step = rows // pieces
    cuts = [pl.ds(h * step, step) for h in range(pieces)]
    loads, keeps, z, x, core, places = [], [], {}, {}, {}, {}
    for n in range(arrays):
        loads.append(pltpu.make_async_copy(owns[n], held[n], local.at[n * 5 + 4]))
        for m in range(4 if shared else 1):
            part = held[n].at[pl.ds(pl.multiple_of((t ^ masks("tp")[m]) * rows, rows), rows)] if shared else held[n]
            keeps.append(pltpu.make_async_copy(part, outs[n].at[m, c], local.at[n * 5 + m]))
    for n in range(arrays):
        for r in range(size):
            for side in range(2 if r else 1):
                spot = lax.rem((c + r if side else c + size - r), size)
                for h in range(pieces):
                    key = (n, r, side, h)
                    place = (n * size + r) * pieces + h
                    if r:
                        source = outs[n].at[0, spot, cuts[h]]
                    else:
                        source = owns[n].at[pl.ds(pl.multiple_of(t * rows + h * step, step) if shared else h * step, step)]
                    there = [outs[n].at[m, spot, cuts[h]] for m in range(4)]
                    count = arrays * size * pieces
                    if r < size - 1:
                        for way in (0, 1) if r == 0 else (side,):
                            z[key + (way,)] = remote(
                                source, there[0], z_sent, z_here, way * count + place, before if way else behind
                            )
                    near = (n * size + spot) * pieces + h
                    if shared and not r:
                        continue
                    x[key] = remote(source, there[1], x_sent, x_here, near, x_peer)
                    core[(0,) + key] = remote(source, there[2], core_sent, core_here, near, core_peer)
                    core[(1,) + key] = remote(there[1], there[3], core_sent, core_here, count + near, core_peer)
                    if r:
                        places[key] = remote(
                            source, there[0], z_sent, z_here, side * count + place - pieces, before if side else behind
                        )

    def go_on(way):
        return c > 0 if way else c < size - 1

    pieces_of = [(n, h) for n in range(arrays) for h in range(pieces)]
    for n, h in pieces_of:
        for way in range(2):

            @pl.when(go_on(way))
            def _():
                z[n, 0, 0, h, way].start()

    for load in loads:
        load.start()
    if not shared:
        for n, h in pieces_of:
            x[n, 0, 0, h].start()
            core[0, n, 0, 0, h].start()
    for load in loads:
        load.wait()
    for keep in keeps:
        keep.start()
    arrivals = [(n, r, side, h) for r in range(1, size) for n in range(arrays) for side in range(2) for h in range(pieces)]

    def there_is(key):
        return c + key[1] < size if key[2] else c >= key[1]

    for key in arrivals:

        @pl.when(there_is(key))
        def _():
            places[key].wait_recv()
            if key[1] < size - 1:

                @pl.when(go_on(key[2]))
                def _():
                    z[key + (key[2],)].start()

            x[key].start()
            core[(0,) + key].start()

    if not shared:
        for n, h in pieces_of:
            x[n, 0, 0, h].wait_recv()
            core[1, n, 0, 0, h].start()
    for key in arrivals:

        @pl.when(there_is(key))
        def _():
            x[key].wait_recv()
            core[(1,) + key].start()

    if not shared:
        for n, h in pieces_of:
            x[n, 0, 0, h].wait_send()
            core[0, n, 0, 0, h].wait()
            core[1, n, 0, 0, h].wait()
    for key in arrivals:

        @pl.when(there_is(key))
        def _():
            x[key].wait_send()
            core[(0,) + key].wait()
            core[(1,) + key].wait()
            if key[1] < size - 1:

                @pl.when(go_on(key[2]))
                def _():
                    z[key + (key[2],)].wait_send()

    for n, h in pieces_of:
        for way in range(2):

            @pl.when(go_on(way))
            def _():
                z[n, 0, 0, h, way].wait_send()

    for keep in keeps:
        keep.wait()


def gather_rows(values, collective, *earlier, shared=False):
    size, tps = lax.axis_size("ctx"), lax.axis_size("tp")
    assert tps == 4
    pieces, arrays = 2, len(values)
    rows = values[0].shape[0] // (tps if shared else 1)
    count = arrays * size * pieces
    anywhere = pl.BlockSpec(memory_space=pl.ANY)
    return pl.pallas_call(
        functools.partial(gather_kernel, size, pieces, arrays, shared, len(earlier)),
        out_shape=[jax.ShapeDtypeStruct((tps, size, rows, v.shape[1]), v.dtype) for v in values],
        in_specs=[anywhere] * (arrays + len(earlier)),
        out_specs=[anywhere] * arrays,
        scratch_shapes=[pltpu.VMEM(v.shape, v.dtype) for v in values]
        + [
            pltpu.SemaphoreType.DMA((n,))
            for n in (5 * arrays, 2 * count, 2 * count, count, count, 2 * count, 2 * count)
        ],
        compiler_params=pltpu.CompilerParams(collective_id=collective, has_side_effects=True),
        name="gather_rows",
        cost_estimate=COST,
    )(*values, *earlier)


def scatter_kernel(size, arrays, aheads, small, earlier, *refs):
    parts, swaps = refs[:arrays], refs[arrays : arrays + len(aheads)]
    given, refs = refs[arrays + len(aheads) :][:small], refs[arrays + len(aheads) + small + earlier :]
    outs, swapped, refs = refs[:arrays], refs[arrays : arrays + len(aheads)], refs[arrays + len(aheads) :]
    summed, refs = refs[:small], refs[small:]
    if small:
        (given,), (summed,), (near, pair, blocks, small_sent, small_here) = given, summed, refs[-5:]
        refs = refs[:-5]
    helds, core_ins, x_ins, z_ins = [refs[k * arrays : (k + 1) * arrays] for k in range(4)]
    local, z_sent, z_here, x_sent, x_here, core_sent, core_here, y_sent, y_here = refs[4 * arrays :]
    c, t, s = lax.axis_index("ctx"), lax.axis_index("tp"), lax.axis_index("shard")
    shards = lax.axis_size("shard")
    rings = [{"shard": lax.rem(s + r, shards)} for r in range(1, shards)] if aheads else []
    x_peer, core_peer = {"tp": t ^ 2}, {"tp": t ^ 1}
    first, last = c == 0, c == size - 1
    upper = c // (size // 2)
    spot = [size - 1 - k + upper * (2 * k - size + 1) for k in range(size)]
    before, behind = {"ctx": lax.max(c - 1, 0)}, {"ctx": lax.min(c + 1, size - 1)}
    line = ((jnp.logical_not(first), before), (jnp.logical_not(last), behind))
    around = [{"ctx": lax.rem(c + r, size)} for r in range(1, size)] if small else []
    greet([x_peer, core_peer] + rings + around, () if small else line)
    if small:
        small_core = remote(given, near.at[0], small_sent, small_here, 0, core_peer)
        small_x = remote(pair, near.at[1], small_sent, small_here, 1, x_peer)
        small_ctx = [
            remote(blocks.at[c], blocks.at[c], small_sent, small_here, 1 + r, around[r - 1]) for r in range(1, size)
        ]
        small_from = [
            remote(blocks.at[b], blocks.at[b], small_sent, small_here, 1 + r, around[r - 1])
            for r, b in [(r, lax.rem(c + size - r, size)) for r in range(1, size)]
        ]
        small_core.start()
    keeps, core, x, rising, falling, finals = [], {}, {}, {}, {}, {}
    y = [remote(swaps[k], swapped[k], y_sent, y_here, k, rings[ahead - 1]) for k, ahead in enumerate(aheads)]
    for n in range(arrays):
        part, held, core_in, x_in, z_in = parts[n], helds[n], core_ins[n], x_ins[n], z_ins[n]
        keeps.append(pltpu.make_async_copy(part.at[pl.ds(0, 2)], held, local.at[n]))
        for m in (1, 0):
            for k in range(size):
                core[n, m, k] = remote(
                    part.at[2 + m, spot[k]], core_in.at[m, k], core_sent, core_here, (n * 2 + m) * size + k, core_peer
                )
        for k in range(size):
            a = spot[k]
            x[n, k] = remote(held.at[1, a], x_in.at[k], x_sent, x_here, n * size + k, x_peer)
            rising[n, k] = remote(held.at[0, a], z_in.at[0, a], z_sent, z_here, 2 * n * size + a, behind)
            falling[n, k] = remote(held.at[0, a], z_in.at[1, a], z_sent, z_here, (2 * n + 1) * size + a, before)
        finals[n] = [
            remote(held.at[0, c], z_in.at[0, c], z_sent, z_here, 2 * n * size + c, behind),
            remote(held.at[0, c], z_in.at[1, c], z_sent, z_here, (2 * n + 1) * size + c, before),
        ]
    for copy in list(core.values()) + y:
        copy.start()
    for keep in keeps:
        keep.start()
    for keep in keeps:
        keep.wait()
    tall = 16

    def each(body):
        @pl.loop(0, outs[0].shape[0] // tall)
        def _(i):
            body(pl.ds(pl.multiple_of(i * tall, tall), tall))

    order = [(n, k) for n in range(arrays) for k in range(size)]
    for n, k in order:
        a, held, core_in = spot[k], helds[n], core_ins[n]
        core[n, 1, k].wait_recv()

        def add_core(rows):
            held[1, a, rows] = (held[1, a, rows].astype(F32) + core_in[1, k, rows].astype(F32)).astype(BF16)

        each(add_core)
        x[n, k].start()
    if small:
        small_core.wait_recv()
        pair[...] = given[...] + near[0]
        small_x.start()
    for n, k in order:
        a, held, core_in, x_in, z_in, out = spot[k], helds[n], core_ins[n], x_ins[n], z_ins[n], outs[n]
        core[n, 0, k].wait_recv()
        x[n, k].wait_recv()

        def total(rows):
            return held[0, a, rows].astype(F32) + core_in[0, k, rows].astype(F32) + x_in[k, rows].astype(F32)

        def add(rows):
            held[0, a, rows] = total(rows).astype(BF16)

        def add_rising(rows):
            held[0, a, rows] = (total(rows) + z_in[0, a, rows].astype(F32)).astype(BF16)

        def add_falling(rows):
            held[0, a, rows] = (total(rows) + z_in[1, a, rows].astype(F32)).astype(BF16)

        def keep_total(rows):
            out[rows] = total(rows)

        @pl.when(a == c)
        def _():
            each(keep_total)

        @pl.when(a > c)
        def _():
            @pl.when(first)
            def _():
                each(add)

            @pl.when(jnp.logical_not(first))
            def _():
                rising[n, k].wait_recv()
                each(add_rising)

            rising[n, k].start()

        @pl.when(a < c)
        def _():
            @pl.when(last)
            def _():
                each(add)

            @pl.when(jnp.logical_not(last))
            def _():
                falling[n, k].wait_recv()
                each(add_falling)

            falling[n, k].start()

    if small:
        small_x.wait_recv()
        blocks[c] = pair[...] + near[1]
        for copy in small_ctx:
            copy.start()
    for n in range(arrays):
        for side, edge in enumerate((first, last)):
            z_in, out = z_ins[n], outs[n]

            @pl.when(jnp.logical_not(edge))
            def _():
                finals[n][side].wait_recv()

                def add_side(rows):
                    out[rows] = out[rows] + z_in[side, c, rows].astype(F32)

                each(add_side)

    for copy in y:
        copy.wait()
    if small:
        for copy in small_from:
            copy.wait_recv()
        summed[...] = sum(blocks[b] for b in range(1, size)) + blocks[0]
        for copy in [small_core, small_x] + small_ctx:
            copy.wait_send()
    for copy in list(core.values()) + list(x.values()):
        copy.wait_send()
    for n, k in order:

        @pl.when(spot[k] > c)
        def _():
            rising[n, k].wait_send()

        @pl.when(spot[k] < c)
        def _():
            falling[n, k].wait_send()


def scatter_rows(parts, collective, swaps, *earlier, small=None):
    size, arrays = lax.axis_size("ctx"), len(parts)
    rows, width = parts[0].shape[2:]
    moved = [v for v, _ in swaps]
    smalls = [] if small is None else [small]
    anywhere, held = pl.BlockSpec(memory_space=pl.ANY), pl.BlockSpec(memory_space=pltpu.VMEM)
    found = pl.pallas_call(
        functools.partial(
            scatter_kernel, size, arrays, tuple(ahead for _, ahead in swaps), len(smalls), len(earlier)
        ),
        out_shape=[jax.ShapeDtypeStruct((rows, width), F32)] * arrays
        + [jax.ShapeDtypeStruct(v.shape, v.dtype) for v in moved + smalls],
        in_specs=[anywhere] * (arrays + len(moved)) + [held] * len(smalls) + [anywhere] * len(earlier),
        out_specs=[held] * arrays + [anywhere] * len(moved) + [held] * len(smalls),
        scratch_shapes=[pltpu.VMEM((2, size, rows, width), BF16)] * (2 * arrays)
        + [pltpu.VMEM((size, rows, width), BF16)] * arrays
        + [pltpu.VMEM((2, size, rows, width), BF16)] * arrays
        + [
            pltpu.SemaphoreType.DMA((arrays * n,))
            for n in (1, 2 * size, 2 * size, size, size, 2 * size, 2 * size)
        ]
        + [pltpu.SemaphoreType.DMA((max(len(moved), 1),))] * 2
        + [pltpu.VMEM((n,) + v.shape, F32) if n else pltpu.VMEM(v.shape, F32) for v in smalls for n in (2, 0, size)]
        + [pltpu.SemaphoreType.DMA((1 + size,))] * (2 * len(smalls)),
        compiler_params=pltpu.CompilerParams(
            collective_id=collective, has_side_effects=True, vmem_limit_bytes=48 * 1024 * 1024
        ),
        name="scatter_rows",
        cost_estimate=COST,
    )(*parts, *moved, *smalls, *earlier)
    return found[:arrays], found[arrays:]


def own_block(values, ahead=0, axis=0):
    size = lax.axis_size("shard")
    block = values.shape[axis] // size
    spot = lax.rem(lax.axis_index("shard") + ahead, size)
    return lax.dynamic_slice_in_dim(values, spot * block, block, axis=axis)


def sum_shard(values, axis):
    size = lax.axis_size("shard")
    total = own_block(values, 0, axis)
    for r in range(1, size):
        total = total + receive(own_block(values, r, axis), "shard", size - r)
    return total


def product_parts(pairs):
    own = jnp.concatenate([dot(lefts[0], right, (0, 0)) for lefts, right in pairs], axis=1)
    others = tuple(
        jnp.concatenate([dot(lefts[r], right, (0, 0), BF16) for lefts, right in pairs], axis=1)
        for r in range(1, lax.axis_size("shard"))
    )
    return own, others


def product_swaps(others):
    return [(part, r) for r, part in enumerate(others, 1)]


def product_add(own, arrived):
    return own + sum(part.astype(F32) for part in arrived)


def product_sum(own, others):
    size = lax.axis_size("shard")
    for r in range(1, size):
        own = own + receive(others[r - 1], "shard", size - r).astype(F32)
    return own


def ahead_first(values, start, axis=0):
    return lax.dynamic_slice_in_dim(
        jnp.concatenate([values, values], axis=axis), start, values.shape[axis], axis=axis
    )


def gather_natural(values, axis_name, axis=0):
    return lax.all_gather(values, axis_name, axis=axis, tiled=True)


def gather_small(values, axis):
    size = lax.axis_size("shard")
    whole = jnp.concatenate([values] + [receive(values, "shard", r) for r in range(1, size)], axis=axis)
    return ahead_first(whole, lax.rem(size - lax.axis_index("shard"), size) * values.shape[axis], axis)


def corner(values):
    return values[(0,) * values.ndim]


def start_after(values):
    first = corner(values)
    return (first != first).astype(jnp.int32)


def tie(values, earlier):
    return values + (corner(earlier).astype(F32) * 0.0).astype(values.dtype)


def part_order(values):
    t = lax.axis_index("tp")
    return jnp.concatenate([lax.dynamic_index_in_dim(values, t ^ m, 1, False)[None] for m in masks("tp")], axis=0)


def natural_rows(values):
    t, order = lax.axis_index("tp"), masks("tp")
    part = values.shape[0] // len(order)
    found = []
    for q in range(len(order)):
        m, place = q ^ t, 0
        for i, bit in enumerate(reversed(bits("tp"))):
            place = place + jnp.where(m & bit, 1 << i, 0)
        found.append(lax.dynamic_slice_in_dim(values, place * part, part))
    return jnp.concatenate(found, axis=0)


def inverse_scale(values):
    return lax.rsqrt(jnp.mean(values * values, axis=-1, keepdims=True) + NORM_EPSILON)


def norm_back(grad, values, gain):
    scale = inverse_scale(values)
    weighted = grad * gain
    middle = jnp.mean(values * weighted, axis=-1, keepdims=True)
    return scale * weighted - values * (scale * scale * scale) * middle, grad * values * scale


def weights_kernel(ctxs, group, pieces, index, inward, outward, entry, *refs):
    exits, (first, others, head, leave) = refs[:ctxs], refs[ctxs:]
    c = index[0]
    tall = first.shape[0]
    deep = 16
    in_rows, out_rows = inward.shape[1], outward.shape[1]
    out_experts = 8
    half = lax.rem(c, out_experts // group) * group

    def picker(rows, kept, place):
        count = kept * deep
        to = lax.broadcasted_iota(jnp.int32, (count, rows * deep), 0)
        source = lax.broadcasted_iota(jnp.int32, (count, rows * deep), 1)
        return (source == to % deep * rows + place(to // deep)).astype(BF16)

    in_pick = picker(in_rows, in_rows, lambda row: row)
    kept = group * pieces
    out_pick = picker(out_rows, kept, lambda row: row // group * out_experts + half + row % group)

    def put(i, column, rows, value):
        if i:
            column = column + (i - 1) * 3 * pieces * 128
        (others if i else first)[rows, column : column + 128] = value

    def two(ref, step, rows):
        parts = [ref[slice((step + n) * deep, (step + n + 1) * deep)].reshape(deep * rows, 128) for n in range(2)]
        return jnp.concatenate(parts, axis=1)

    for step in range(0, tall // deep, 2):
        moved_in = matmul(in_pick, two(inward, step, in_rows)).astype(BF16)
        moved_out = matmul(out_pick, two(outward, step, out_rows)).astype(BF16)
        for n in range(2):
            rows, lanes = slice((step + n) * deep, (step + n + 1) * deep), slice(n * 128, (n + 1) * 128)
            for row in range(in_rows):
                i, piece, side = row // (2 * pieces), row // 2 % pieces, row % 2
                put(i, (side * pieces + piece) * 128, rows, moved_in[row * deep : (row + 1) * deep, lanes])
            for row in range(kept):
                i, piece = row % group, row // group
                put(i, (2 * pieces + piece) * 128, rows, moved_out[row * deep : (row + 1) * deep, lanes])
    for k in range(3):
        head[:, k * HEAD_DIM : (k + 1) * HEAD_DIM] = entry[k]
    for j in range(ctxs):
        leave[:, j * HEAD_DIM : (j + 1) * HEAD_DIM] = exits[j][...]


def own_weights(expert_in, expert_out, attention_in, attention_out):
    c, ctxs = lax.axis_index("ctx"), lax.axis_size("ctx")
    rows, experts, _, hidden = expert_in.shape
    group, pieces = experts // ctxs, hidden // 128
    assert group in (1, 2, 4, 8) and group * 2 * pieces % 16 == 0 and 8 * pieces % 16 == 0
    inward = expert_in.reshape(rows, experts, 2, pieces, 128).transpose(0, 1, 3, 2, 4).reshape(rows, -1, 128)
    outward = expert_out.reshape(rows, experts // 8, 8, pieces, 128).transpose(0, 1, 3, 2, 4).reshape(rows, -1, 128)
    entry = attention_in.transpose(1, 0, 2)
    tall = 64
    wide = 3 * hidden
    grid_spec = pltpu.PrefetchScalarGridSpec(
        num_scalar_prefetch=1,
        grid=(rows // tall,),
        in_specs=[
            pl.BlockSpec((tall, group * 2 * pieces, 128), lambda b, c: (b, c[0], 0)),
            pl.BlockSpec((tall, 8 * pieces, 128), lambda b, c: (b, c[0] * group // 8, 0)),
            pl.BlockSpec((3, tall, HEAD_DIM), lambda b, c: (0, b, c[0])),
        ]
        + [
            pl.BlockSpec((tall, HEAD_DIM), functools.partial(lambda j, b, c: (b, lax.rem(c[0] + j, ctxs)), j))
            for j in range(ctxs)
        ],
        out_specs=[
            pl.BlockSpec((tall, n), lambda b, c: (b, 0))
            for n in (wide, (group - 1) * wide, 3 * HEAD_DIM, ctxs * HEAD_DIM)
        ],
    )
    return pl.pallas_call(
        functools.partial(weights_kernel, ctxs, group, pieces),
        grid_spec=grid_spec,
        out_shape=[
            jax.ShapeDtypeStruct((rows, n), BF16)
            for n in (wide, (group - 1) * wide, 3 * HEAD_DIM, ctxs * HEAD_DIM)
        ],
        compiler_params=pltpu.CompilerParams(vmem_limit_bytes=48 * 1024 * 1024),
        name="own_weights",
        cost_estimate=COST,
    )(c.astype(jnp.int32)[None], inward, outward, entry, *([attention_out] * ctxs))


def matmul(left, right, over=(1, 0)):
    return lax.dot_general(left, right, (((over[0],), (over[1],)), ((), ())), preferred_element_type=F32)


def head_norm(values):
    return lax.rsqrt(jnp.mean(values * values, axis=-1, keepdims=True) + NORM_EPSILON)


def turned(values, cosine, sine):
    return values * cosine + pltpu.roll(values, values.shape[-1] // 2, 1) * sine


def shared_weights_kernel(ctxs, group, pieces, index, *refs):
    others = ctxs - 1
    inwards, outwards, outs = refs[:others], refs[others : 2 * others], refs[-others:]
    deep, hidden = 16, pieces * 128
    kinds, out_kinds = group * 2 * pieces, 8 * pieces

    def picker(rows, kept, place):
        to = lax.broadcasted_iota(jnp.int32, (kept * deep, rows * deep), 0)
        source = lax.broadcasted_iota(jnp.int32, (kept * deep, rows * deep), 1)
        return (source == to % deep * rows + place(to // deep)).astype(BF16)

    in_pick = picker(kinds, 2 * pieces, lambda r: (group - 1) * 2 * pieces + r)

    def two(ref, step, rows):
        parts = [ref[(step + n) * deep : (step + n + 1) * deep].reshape(deep * rows, 128) for n in range(2)]
        return jnp.concatenate(parts, axis=1)

    for k in range(others):
        inward, outward, out = inwards[k], outwards[k], outs[k]
        at = lax.rem(lax.rem(index[0] + k + 1, ctxs), 8 // group) * group + group - 1
        out_pick = picker(out_kinds, pieces, lambda r: r * 8 + at)

        def put(moved, step, r, column):
            for n in range(2):
                rows = slice((step + n) * deep, (step + n + 1) * deep)
                out[rows, column : column + 128] = moved[r * deep : (r + 1) * deep, n * 128 : (n + 1) * 128]

        for step in range(0, out.shape[0] // deep, 2):
            moved = matmul(in_pick, two(inward, step, kinds)).astype(BF16)
            for r in range(2 * pieces):
                put(moved, step, r, (r % 2 * pieces + r // 2) * 128)
            moved = matmul(out_pick, two(outward, step, out_kinds)).astype(BF16)
            for r in range(pieces):
                put(moved, step, r, (2 * pieces + r) * 128)


def shared_weights(expert_in, expert_out, *earlier):
    ctxs = lax.axis_size("ctx")
    rows, experts, _, hidden = expert_in.shape
    group, pieces = experts // ctxs, hidden // 128
    inward = expert_in.reshape(rows, experts, 2, pieces, 128).transpose(0, 1, 3, 2, 4).reshape(rows, -1, 128)
    outward = expert_out.reshape(rows, experts // 8, 8, pieces, 128).transpose(0, 1, 3, 2, 4).reshape(rows, -1, 128)
    tall, others = 64, ctxs - 1
    after = lambda k, c: lax.rem(c[0] + k + 1, ctxs)
    return pl.pallas_call(
        functools.partial(shared_weights_kernel, ctxs, group, pieces),
        grid_spec=pltpu.PrefetchScalarGridSpec(
            num_scalar_prefetch=1,
            grid=(rows // tall,),
            in_specs=[
                pl.BlockSpec(
                    (tall, group * 2 * pieces, 128), functools.partial(lambda k, b, c: (b, after(k, c), 0), k)
                )
                for k in range(others)
            ]
            + [
                pl.BlockSpec(
                    (tall, 8 * pieces, 128), functools.partial(lambda k, b, c: (b, after(k, c) * group // 8, 0), k)
                )
                for k in range(others)
            ]
            + [pl.BlockSpec(memory_space=pl.ANY)] * len(earlier),
            out_specs=[pl.BlockSpec((tall, 3 * hidden), lambda b, c: (b, 0))] * others,
        ),
        out_shape=[jax.ShapeDtypeStruct((rows, 3 * hidden), BF16)] * others,
        compiler_params=pltpu.CompilerParams(vmem_limit_bytes=48 * 1024 * 1024),
        name="shared_weights",
        cost_estimate=COST,
    )(lax.axis_index("ctx").astype(jnp.int32)[None], *([inward] * others), *([outward] * others), *earlier)


def project_kernel(tokens, gain, weight, gains, cosine, sine, normed, raw, query, key, value):
    values = tokens[...].astype(F32)
    low = (values * head_norm(values) * gain[...]).astype(BF16)
    normed[...] = low
    projected = matmul(low, weight[...])
    raw[...] = projected[:, : 2 * HEAD_DIM]
    for k, out in enumerate((query, key)):
        part = projected[:, k * HEAD_DIM : (k + 1) * HEAD_DIM]
        part = part * head_norm(part) * gains[k : k + 1, :]
        out[...] = turned(part, cosine[...], sine[...]).astype(BF16)
    value[...] = projected[:, 2 * HEAD_DIM :].astype(BF16)


def project(tokens, gain, weight, gains, cosine, sine):
    rows, width = tokens.shape
    tall = 256
    block = lambda n: pl.BlockSpec((tall, n), lambda b: (b, 0))
    whole = lambda v: pl.BlockSpec(v.shape, lambda b: (0, 0))
    head = jax.ShapeDtypeStruct((rows, HEAD_DIM), BF16)
    return pl.pallas_call(
        project_kernel,
        grid=(rows // tall,),
        in_specs=[block(width), whole(gain), whole(weight), whole(gains), block(HEAD_DIM), block(HEAD_DIM)],
        out_specs=[block(width), block(2 * HEAD_DIM)] + [block(HEAD_DIM)] * 3,
        out_shape=[
            jax.ShapeDtypeStruct((rows, width), BF16),
            jax.ShapeDtypeStruct((rows, 2 * HEAD_DIM), F32),
            head,
            head,
            head,
        ],
        compiler_params=pltpu.CompilerParams(vmem_limit_bytes=48 * 1024 * 1024),
        name="project",
        cost_estimate=COST,
    )(tokens, gain, weight, gains, cosine, sine)


def chances_of(query, key, row_doc, column_doc):
    scores = matmul(query, key, (1, 1)) * (HEAD_DIM**-0.5)
    scores = jnp.where(row_doc == column_doc, scores, MASKED)
    grown = jnp.exp(scores - jnp.max(scores, axis=-1, keepdims=True))
    return grown / jnp.sum(grown, axis=-1, keepdims=True)


def attend_kernel(query, key, value, row_doc, column_doc, mixed):
    chances = chances_of(query[...], key[...], row_doc[...], column_doc[...])
    mixed[...] = matmul(chances.astype(BF16), value[...]).astype(BF16)


def attend(query, key, value, row_doc, column_doc):
    rows = query.shape[0]
    tall = 256
    block = pl.BlockSpec((tall, HEAD_DIM), lambda b: (b, 0))
    whole = pl.BlockSpec((rows, HEAD_DIM), lambda b: (0, 0))
    return pl.pallas_call(
        attend_kernel,
        grid=(rows // tall,),
        in_specs=[
            block,
            whole,
            whole,
            pl.BlockSpec((tall, 1), lambda b: (b, 0)),
            pl.BlockSpec((1, rows), lambda b: (0, 0)),
        ],
        out_specs=block,
        out_shape=jax.ShapeDtypeStruct((rows, HEAD_DIM), BF16),
        compiler_params=pltpu.CompilerParams(vmem_limit_bytes=48 * 1024 * 1024),
        name="attend",
        cost_estimate=COST,
    )(query, key, value, row_doc, column_doc)


def attend_back_kernel(
    tall, query, key, value, raw, cosine, sine, gains, row_doc, column_doc, mixed_grad, *refs
):
    grad, gain_grad, key_grad, value_grad = refs[-4:]
    step = pl.program_id(0)
    rows = pl.ds(pl.multiple_of(step * tall, tall), tall)

    def projected_back(turned_grad, k, where):
        values = raw[where, k * HEAD_DIM : (k + 1) * HEAD_DIM]
        grown = turned(turned_grad, cosine[where], -sine[where])
        scale = head_norm(values)
        weighted = grown * gains[k : k + 1, :]
        middle = jnp.mean(values * weighted, axis=-1, keepdims=True)
        part = jnp.sum(grown * values * scale, axis=0, keepdims=True)
        return scale * weighted - values * (scale * scale * scale) * middle, part

    @pl.when(step == 0)
    def _():
        key_grad[...] = jnp.zeros_like(key_grad)
        value_grad[...] = jnp.zeros_like(value_grad)
        gain_grad[...] = jnp.zeros_like(gain_grad)

    here = query[...]
    chances = chances_of(here, key[...], row_doc[...], column_doc[...])
    upstream = mixed_grad[...]
    weight_grad = matmul(upstream, value[...], (1, 1))
    score_grad = chances * (weight_grad - jnp.sum(chances * weight_grad, axis=-1, keepdims=True))
    score_grad = score_grad.astype(BF16)
    scale = HEAD_DIM**-0.5
    query_grad, part = projected_back(matmul(score_grad, key[...]) * scale, 0, rows)
    grad[rows, :HEAD_DIM] = query_grad.astype(BF16)
    gain_grad[0:1, :] += part
    key_grad[...] += matmul(score_grad, here, (0, 0)) * scale
    value_grad[...] += matmul(chances.astype(BF16), upstream, (0, 0))

    @pl.when(step == pl.num_programs(0) - 1)
    def _():
        back, part = projected_back(key_grad[...], 1, slice(None))
        grad[:, HEAD_DIM : 2 * HEAD_DIM] = back.astype(BF16)
        gain_grad[1:2, :] += part
        grad[:, 2 * HEAD_DIM :] = value_grad[...].astype(BF16)


def attend_back(query, key, value, raw, cosine, sine, gains, row_doc, column_doc, mixed_grad, *earlier):
    rows = query.shape[0]
    tall = 256
    block = pl.BlockSpec((tall, HEAD_DIM), lambda b: (b, 0))
    whole = lambda v: pl.BlockSpec(v.shape, lambda b: (0, 0))
    return pl.pallas_call(
        functools.partial(attend_back_kernel, tall),
        grid=(rows // tall,),
        in_specs=[
            block,
            whole(key),
            whole(value),
            whole(raw),
            whole(cosine),
            whole(sine),
            whole(gains),
            pl.BlockSpec((tall, 1), lambda b: (b, 0)),
            whole(column_doc),
            block,
        ]
        + [pl.BlockSpec(memory_space=pl.ANY)] * len(earlier),
        out_specs=[
            pl.BlockSpec((rows, 3 * HEAD_DIM), lambda b: (0, 0)),
            pl.BlockSpec((8, HEAD_DIM), lambda b: (0, 0)),
        ],
        out_shape=[
            jax.ShapeDtypeStruct((rows, 3 * HEAD_DIM), BF16),
            jax.ShapeDtypeStruct((8, HEAD_DIM), F32),
        ],
        scratch_shapes=[pltpu.VMEM((rows, HEAD_DIM), F32)] * 2,
        compiler_params=pltpu.CompilerParams(vmem_limit_bytes=48 * 1024 * 1024),
        name="attend_back",
        cost_estimate=COST,
    )(query, key, value, raw, cosine, sine, gains, row_doc, column_doc, mixed_grad, *earlier)


def expert_step_kernel(index, count, earlier, shard, rows, upstream, *refs):
    gate_in, up_in, outward = [refs[k * count : (k + 1) * count] for k in range(3)]
    gates, lanes, scaled, inner_grad, gate_part = refs[3 * count], refs[3 * count + 1], *refs[3 * count + 2 + earlier :]
    hidden_size = outward[0].shape[1]
    deep = outward[0].shape[0]

    def product(left, parts):
        total = 0.0
        for r, part in enumerate(parts):
            start = pl.multiple_of(lax.rem(shard[0] + r, count) * deep, deep) if count > 1 else 0
            total = total + matmul(left[:, pl.ds(start, deep)], part[...])
        return total

    gate, up, back = product(rows, gate_in), product(rows, up_in), product(upstream, outward)
    sigmoid = 1.0 / (1.0 + jnp.exp(-gate))
    silu = gate * sigmoid
    hidden = (silu * up).astype(BF16).astype(F32)
    weight = gates[:, index : index + 1]
    scaled[...] = (hidden * weight).astype(BF16)
    gate_part[...] = jnp.sum(hidden * back, axis=1, keepdims=True) * lanes[index : index + 1, :]
    hidden_grad = back * weight
    inner_grad[:, :hidden_size] = (hidden_grad * up * sigmoid * (1.0 + gate * (1.0 - sigmoid))).astype(BF16)
    inner_grad[:, hidden_size:] = (hidden_grad * silu).astype(BF16)


def expert_step(index, place, rows, upstream, weights, hidden_size, gates, lanes, *earlier):
    count, width = rows.shape
    tall, parts = 256, len(weights)
    block = lambda n: pl.BlockSpec((tall, n), lambda b, s: (b, 0))
    whole = weights[0].shape[0] == width

    def column(k, r, b, s):
        return (lax.rem(s[0] + r, parts) if whole else 0, 3 * place + k)

    columns = [
        pl.BlockSpec((width // parts, hidden_size), functools.partial(column, k, r))
        for k in range(3)
        for r in range(parts)
    ]
    return pl.pallas_call(
        functools.partial(expert_step_kernel, index, parts, len(earlier)),
        grid_spec=pltpu.PrefetchScalarGridSpec(
            num_scalar_prefetch=1,
            grid=(count // tall,),
            in_specs=[block(width), block(width)]
            + columns
            + [block(gates.shape[1]), pl.BlockSpec(lanes.shape, lambda b, s: (0, 0))]
            + [pl.BlockSpec(memory_space=pl.ANY)] * len(earlier),
            out_specs=[block(hidden_size), block(2 * hidden_size), block(128)],
        ),
        out_shape=[
            jax.ShapeDtypeStruct((count, hidden_size), BF16),
            jax.ShapeDtypeStruct((count, 2 * hidden_size), BF16),
            jax.ShapeDtypeStruct((count, 128), F32),
        ],
        compiler_params=pltpu.CompilerParams(vmem_limit_bytes=48 * 1024 * 1024),
        name="expert_step",
        cost_estimate=COST,
    )(lax.axis_index("shard").astype(jnp.int32)[None], rows, upstream, *(list(weights) * 3), gates, lanes, *earlier)


def combine_kernel(count, extras, *refs):
    lefts, rights, lanes, out = refs[:count], refs[count : 2 * count], refs[2 * count : 2 * count + extras], refs[-1]
    width = rights[0].shape[0]
    total = matmul(lefts[0][...], rights[0][...], (1, 1))
    for left, right in zip(lefts[1:], rights[1:]):
        total = total + matmul(left[...], right[...], (1, 1))
    out[:, :width] = total.astype(BF16)
    if extras:
        out[:, width:] = sum(lane[...] for lane in lanes).astype(BF16)


def combine(lefts, rights, lanes, *earlier):
    (rows, _), (width, _) = lefts[0][0].shape, rights[0][0].shape
    tall, deep = 256, 256
    total = width + (lanes[0].shape[1] if lanes else 0)
    return pl.pallas_call(
        lambda *refs: combine_kernel(len(lefts), len(lanes), *refs[: len(refs) - 1 - len(earlier)], refs[-1]),
        grid=(rows // tall,),
        in_specs=[pl.BlockSpec((tall, deep), functools.partial(lambda k, b: (b, k), k)) for _, k in lefts]
        + [
            pl.BlockSpec((width, deep), functools.partial(lambda k, b: (0, k), k), pipeline_mode=pl.Buffered(1))
            for _, k in rights
        ]
        + [pl.BlockSpec((tall, lane.shape[1]), lambda b: (b, 0)) for lane in lanes]
        + [pl.BlockSpec(memory_space=pl.ANY)] * len(earlier),
        out_specs=pl.BlockSpec((tall, total), lambda b: (b, 0)),
        out_shape=jax.ShapeDtypeStruct((rows, total), BF16),
        compiler_params=pltpu.CompilerParams(vmem_limit_bytes=56 * 1024 * 1024),
        name="combine",
        cost_estimate=COST,
    )(*[v for v, _ in lefts], *[v for v, _ in rights], *lanes, *earlier)


def gradient_kernel(steps, index, rows, upstream, inner_grad, scaled, own, others):
    step = pl.program_id(0)
    wide = inner_grad.shape[1]

    def put(out):
        out[:, :wide] = matmul(rows[...], inner_grad[...], (0, 0)).astype(out.dtype)
        out[:, wide:] = matmul(upstream[...], scaled[...], (0, 0)).astype(out.dtype)

    @pl.when(step < steps)
    def _():
        put(own)

    @pl.when(step >= steps)
    def _():
        put(others)


def gradient_parts(rows, upstream, inner_grad, scaled):
    s, shards = lax.axis_index("shard"), lax.axis_size("shard")
    count, width = rows.shape
    deep = 256
    steps = width // shards // deep
    wide = inner_grad.shape[1] + scaled.shape[1]
    feature = pl.BlockSpec((count, deep), lambda b, s: (0, lax.rem(s[0] * steps + b, steps * shards)))
    whole = lambda v: pl.BlockSpec(v.shape, lambda b, s: (0, 0))
    return pl.pallas_call(
        functools.partial(gradient_kernel, steps),
        grid_spec=pltpu.PrefetchScalarGridSpec(
            num_scalar_prefetch=1,
            grid=(steps * shards,),
            in_specs=[feature, feature, whole(inner_grad), whole(scaled)],
            out_specs=[
                pl.BlockSpec((deep, wide), lambda b, s: (lax.min(b, steps - 1), 0)),
                pl.BlockSpec((deep, wide), lambda b, s: (lax.max(b - steps, 0), 0)),
            ],
        ),
        out_shape=[
            jax.ShapeDtypeStruct((steps * deep, wide), F32),
            jax.ShapeDtypeStruct((steps * deep * (shards - 1), wide), BF16),
        ],
        compiler_params=pltpu.CompilerParams(vmem_limit_bytes=48 * 1024 * 1024),
        name="gradient_parts",
        cost_estimate=COST,
    )(s.astype(jnp.int32)[None], rows, upstream, inner_grad, scaled)


def expert_kernel(group, ctxs, tall, hidden, index, *refs):
    gathered, shared, (up, down) = refs[: group - 1], refs[group - 1 : group - 1 + ctxs], refs[group - 1 + ctxs :]
    pieces = hidden // 128
    experts = group * ctxs
    deep = 16
    to = lax.broadcasted_iota(jnp.int32, (deep * deep, deep * deep), 0)
    source = lax.broadcasted_iota(jnp.int32, (deep * deep, deep * deep), 1)
    turn = (source == to % deep * deep + to // deep).astype(BF16)

    def tile(e, column, start):
        rows, columns = slice(start, start + deep), slice(column, column + 128)
        if e % group == group - 1:
            return shared[e // group][0, rows, columns]
        return gathered[e % group][e // group, rows, columns]

    def place(out, kinds, start):
        blocks = [jnp.concatenate([tile(e, column, start) for e, column in kinds[k : k + deep]], axis=0) for k in range(0, len(kinds), deep)]
        for k in range(0, len(blocks), 2):
            pair = blocks[k : k + 2]
            moved = matmul(turn, jnp.concatenate(pair, axis=1))
            for n in range(len(pair)):
                for d in range(deep):
                    row = (start + d) * len(kinds) + (k + n) * deep
                    out[row : row + deep, :] = moved[d * deep : (d + 1) * deep, n * 128 : (n + 1) * 128]

    ups = [(e, (side * pieces + piece) * 128) for e in range(experts) for piece in range(pieces) for side in range(2)]
    downs = [
        (part * 8 + e, (2 * pieces + piece) * 128)
        for part in range(experts // 8)
        for piece in range(pieces)
        for e in range(8)
    ]
    for start in range(0, tall, deep):
        place(up, ups, start)
        place(down, downs, start)


def expert_gradients(gathered, shared):
    (ctxs, rows, width), group = shared.shape, len(gathered) + 1
    hidden, experts = width // 3, group * ctxs
    pieces = hidden // 128
    assert experts % 8 == 0 and hidden % 128 == 0
    tall = 64
    up, down = pl.pallas_call(
        functools.partial(expert_kernel, group, ctxs, tall, hidden),
        grid_spec=pltpu.PrefetchScalarGridSpec(
            num_scalar_prefetch=1,
            grid=(rows // tall,),
            in_specs=[pl.BlockSpec((ctxs, tall, width), lambda b, c: (0, b, 0))] * len(gathered)
            + [
                pl.BlockSpec(
                    (1, tall, width), functools.partial(lambda j, b, c: (lax.rem(ctxs + j - c[0], ctxs), b, 0), j)
                )
                for j in range(ctxs)
            ],
            out_specs=[pl.BlockSpec((tall * experts * pieces * k, 128), lambda b, c: (b, 0)) for k in (2, 1)],
        ),
        out_shape=[jax.ShapeDtypeStruct((rows * experts * pieces * k, 128), F32) for k in (2, 1)],
        compiler_params=pltpu.CompilerParams(vmem_limit_bytes=48 * 1024 * 1024),
        name="expert_gradients",
        cost_estimate=COST,
    )(lax.axis_index("ctx").astype(jnp.int32)[None], *gathered, *([shared] * ctxs))
    up = up.reshape(rows, experts, pieces, 2, 128).transpose(0, 1, 3, 2, 4).reshape(rows, experts, 2, hidden)
    down = down.reshape(rows, experts // 8, pieces, 8, 128).transpose(0, 1, 3, 2, 4).reshape(rows, experts, hidden)
    return up, down


def attention_kernel(chunk, entry, exit_out):
    ctxs, _, width = chunk.shape
    head = width // 4
    for j in range(ctxs):
        for k in range(3):
            entry[k, :, j * head : (j + 1) * head] = chunk[j, :, k * head : (k + 1) * head].astype(F32)
        exit_out[:, j * head : (j + 1) * head] = chunk[j, :, 3 * head :].astype(F32)


def attention_gradients(chunk):
    ctxs, rows, width = chunk.shape
    wide = ctxs * width // 4
    tall = 128
    entry, exit_out = pl.pallas_call(
        attention_kernel,
        grid=(rows // tall,),
        in_specs=[pl.BlockSpec((ctxs, tall, width), lambda b: (0, b, 0))],
        out_specs=[pl.BlockSpec((3, tall, wide), lambda b: (0, b, 0)), pl.BlockSpec((tall, wide), lambda b: (b, 0))],
        out_shape=[jax.ShapeDtypeStruct((3, rows, wide), F32), jax.ShapeDtypeStruct((rows, wide), F32)],
        name="attention_gradients",
        cost_estimate=COST,
    )(chunk)
    return entry.transpose(1, 0, 2), exit_out


def local(
    tokens,
    segments,
    routes,
    cotangent,
    first_gain,
    head_gain,
    attention_in,
    attention_out,
    second_gain,
    router_weight,
    expert_in,
    expert_out,
):
    s, c, t = lax.axis_index("shard"), lax.axis_index("ctx"), lax.axis_index("tp")
    shards, ctxs, tps = lax.axis_size("shard"), lax.axis_size("ctx"), lax.axis_size("tp")
    rows, width = tokens.shape[1:]
    own = rows // tps
    block = width // shards
    every = rows * ctxs
    experts = router_weight.shape[1]
    hidden_size = expert_out.shape[2]
    local_width = attention_out.shape[1]
    head_size = local_width // ctxs

    group = experts // ctxs
    base = c * group

    gains = gather_small(jnp.stack([first_gain, second_gain]), 1).astype(F32)
    gain_one, gain_two = gains[0], gains[1]
    head_gains = gather_small(head_gain[None], 1)[0].astype(F32)
    first_weights, others, head_in, exit_weight = own_weights(expert_in, expert_out, attention_in, attention_out)
    tokens_all, cot_all = gather_rows([tokens[0], cotangent[0]], 3, head_in, shared=True)
    tokens_all, cot_all = tokens_all.reshape(every, width), cot_all.reshape(every, width)
    head_in = gather_natural(head_in, "shard")
    first_weights, others = gather_natural(first_weights, "shard"), gather_natural(others, "shard")
    exit_weight = gather_small(exit_weight, 0)
    first = t * own
    tokens_own = lax.dynamic_slice_in_dim(tokens[0], first, own)
    cot_own = lax.dynamic_slice_in_dim(cotangent[0], first, own)

    layer_in = tokens_own.astype(F32)
    upstream = cot_own.astype(F32)
    choices_all = gather_ctx(routes[0]).reshape(ctxs, tps, own, -1)
    picks_all = jnp.any(part_order(choices_all)[..., None] == jnp.arange(experts), axis=3)
    picks = lax.dynamic_index_in_dim(picks_all[0], c, 0, False)
    picks_all = picks_all.reshape(every, experts)
    router = gather_small(router_weight, 0)

    assert head_size == HEAD_DIM
    spot = part_order(jnp.arange(every, dtype=jnp.int32).reshape(ctxs, tps, own)).reshape(-1)
    documents = part_order(segments[0].reshape(ctxs, tps, own)).reshape(-1)
    row_doc, column_doc = documents[:, None], documents[None, :]
    steps = jnp.arange(HEAD_DIM // 2).astype(F32)
    frequency = ROTARY_BASE ** (-2.0 * steps / HEAD_DIM)
    angles = spot.astype(F32)[:, None] * frequency[None, :]
    cosine, sine = jnp.cos(angles), jnp.sin(angles)
    cosine, sine = jnp.concatenate([cosine, cosine], axis=1), jnp.concatenate([-sine, sine], axis=1)
    head_gains = head_gains.reshape(2, HEAD_DIM)
    normed_one_all, raw, queries, keys, values = project(
        tokens_all, gain_one[None], head_in, head_gains, cosine, sine
    )
    mixed_head = attend(queries, keys, values, row_doc, column_doc)
    blocks = ahead_first(mixed_head.reshape(tps, ctxs, own, head_size), c, 1)
    mixed = [blocks[:, 0]] + [receive(blocks[:, ctxs - j], "ctx", j) for j in range(1, ctxs)]
    mixed = jnp.concatenate([m.reshape(rows, head_size) for m in mixed], axis=1)
    residual = layer_in + scatter_tp(dot(mixed, exit_weight, (1, 1)))

    normed_two = lower(residual * inverse_scale(residual) * gain_two)
    normed_two_all = gather_rows([normed_two], 0)[0].reshape(every, width)
    chances_all = jax.nn.softmax(dot(normed_two_all, router, (1, 0)), axis=-1)
    gates_all = jnp.where(picks_all, chances_all, 0.0)
    gates = lax.dynamic_slice_in_dim(gates_all, base, group, axis=1)
    lanes = (jnp.arange(128)[None] == base + jnp.arange(group)[:, None]).astype(F32)
    scaled, gate_parts, inner_grads, products = [], [], [], []

    def gradient_blocks(inner_grad, gated):
        own_part, far = gradient_parts(normed_two_all, cot_all, inner_grad, gated)
        return own_part, tuple(far[r * block : (r + 1) * block] for r in range(shards - 1))

    last = group - 1
    before = []
    for i in range(group):
        weights = [others] * shards if i == last else [others] if i else [first_weights]
        step = expert_step(
            i, max(i - 1, 0), normed_two_all, cot_all, weights, hidden_size, gates, lanes, *before
        )
        scaled.append(step[0])
        inner_grads.append(step[1])
        gate_parts.append(step[2])
        products.append(gradient_blocks(inner_grads[i], scaled[i]))
        before = list(products[i][1])
        if i == 1:
            shared = shared_weights(expert_in, expert_out, *before)
            before += shared
    chunks, gathered = [], []
    for i in range(last):
        own_part, far = products[i]
        chunks.append(lower(product_sum(tie(own_part, inner_grads[last] if i else products[1][1][0]), far)))
        gathered.append(lax.all_gather(chunks[i], "ctx", axis=0, tiled=False))
    columns = lambda k: [(others if i else first_weights, 3 * max(i - 1, 0) + k) for i in range(group)]
    normed_part = combine(
        [(v, k) for k in range(2) for v in inner_grads], columns(0) + columns(1), gate_parts, *before
    )
    weight_swaps = lambda weights: [(w, shards - r) for w in weights for r in range(1, shards)]
    (normed_sum,), arrived = scatter_rows([normed_part.reshape(tps, ctxs, own, -1)], 1, weight_swaps(shared[:-1]))
    shared_all = [[w] + list(arrived[k * (shards - 1) : (k + 1) * (shards - 1)]) for k, w in enumerate(shared[:-1])]
    normed_sum = tie(normed_sum, gathered[0])
    normed_sum, gate_grad = normed_sum[:, :width], normed_sum[:, width : width + experts]

    router_chances = jax.nn.softmax(dot(normed_two, router, (1, 0)), axis=-1)
    chance_grad = jnp.where(picks, gate_grad, 0.0)
    logit_grad = lower(
        router_chances * (chance_grad - jnp.sum(router_chances * chance_grad, axis=-1, keepdims=True))
    )
    router_part = dot(logit_grad, normed_two, (0, 0))
    normed_grad = normed_sum + dot(logit_grad, router, (1, 1))
    residual_back, second_part = norm_back(normed_grad, residual, gain_two)
    residual_grad = upstream + residual_back

    attend_grad = gather_tp(lower(residual_grad))
    exit_parts = product_parts([([own_block(attend_grad, r, 1) for r in range(shards)], mixed)])
    mixed_grad = lower(dot(attend_grad, exit_weight, (1, 0))).reshape(tps, own, ctxs, head_size)
    parts = [mixed_grad[:, :, 0]] + [receive(mixed_grad[:, :, ctxs - j], "ctx", j) for j in range(1, ctxs)]
    mixed_grad = ahead_first(jnp.stack(parts, axis=1), lax.rem(ctxs - c, ctxs), 1)
    mixed_grad = mixed_grad.reshape(every, HEAD_DIM)
    projected_grad, gain_part = attend_back(
        queries, keys, values, raw, cosine, sine, head_gains, row_doc, column_doc, mixed_grad
    )
    entry_blocks = [own_block(normed_one_all, r, 1) for r in range(shards)]
    entry_parts = product_parts([(entry_blocks, projected_grad)])
    shared_gates = ahead_first(gates_all[:, last::group], c, 1)
    shared_all += [[w] + [receive(w, "shard", r) for r in range(1, shards)] for w in shared[len(shared_all) :]]
    exit_part = product_sum(*exit_parts)
    shared_products = [products[last]]
    shared_chunks = [lower(product_sum(*products[last]))]
    earlier = [exit_part, *entry_parts[1], *chunks]
    for j in range(1, ctxs):
        step = expert_step(
            j, 0, normed_two_all, cot_all, shared_all[j - 1], hidden_size, shared_gates, lanes, *earlier
        )
        parts = gradient_blocks(step[1], step[0])
        shared_products.append(parts)
        earlier = list(parts[1])
        if j == 1:
            exit_head = tie(exit_part[:, :head_size], parts[1][0])
            for r in range(1, ctxs):
                exit_head = exit_head + receive(
                    lower(exit_part[:, r * head_size : (r + 1) * head_size]), "ctx", ctxs - r
                ).astype(F32)
            earlier += [shared_chunks[0], gathered[1], *shared_all[-1][1:]]
        if j == 2:
            entry_head = product_sum(tie(entry_parts[0], parts[1][0]), entry_parts[1])
            attention_chunk = lower(jnp.concatenate([entry_head, exit_head], axis=1))
            attention_gathered = lax.all_gather(attention_chunk, "ctx", axis=0, tiled=False)

    result_part = combine([(v, 0) for v in scaled], columns(2), [], *earlier, attention_chunk)
    first_part = dot(projected_grad, head_in, (1, 1), BF16)
    tokens_wide = tokens_all.astype(F32)
    first_sum = jnp.sum(first_part.astype(F32) * tokens_wide * inverse_scale(tokens_wide), axis=0)
    head_part = gain_part[:2].reshape(1, -1)
    small_part = [jnp.sum(second_part, axis=0)[None], first_sum[None], jnp.pad(head_part, ((0, 0), (0, width - head_part.shape[1])))]
    small_part = jnp.concatenate([router_part] + small_part, axis=0)
    small_part = jnp.pad(small_part, ((0, -small_part.shape[0] % 8), (0, 0)))
    shared_chunks.append(lower(product_sum(*shared_products[1])))
    (first_normed_grad, result_sum), arrived = scatter_rows(
        [part.reshape(tps, ctxs, own, width) for part in (first_part, result_part)],
        2,
        sum([product_swaps(p[1]) for p in shared_products[2:]], []),
        shared_chunks[1],
        small=small_part,
    )
    head_gradient = sum_shard(arrived[-1][experts + 2 : experts + 3, : head_part.shape[1]], 1)[0]
    small_sum = sum_shard(arrived[-1][: experts + 2], 1)
    for k, p in enumerate(shared_products[2:]):
        shared_chunks.append(lower(product_add(p[0], arrived[k * (shards - 1) : (k + 1) * (shards - 1)])))
    layer_output = natural_rows(gather_tp(lower(residual + result_sum)))[None]
    input_back, _ = norm_back(first_normed_grad, layer_in, gain_one)
    input_gradient = natural_rows(gather_tp(lower(residual_grad + input_back))).astype(F32)[None]

    upward_gradient, downward_gradient = expert_gradients(
        gathered, jnp.stack(shared_chunks)
    )
    entry_gradient, exit_gradient = attention_gradients(attention_gathered)
    return (
        layer_output,
        input_gradient,
        small_sum[experts + 1],
        head_gradient,
        entry_gradient,
        exit_gradient,
        small_sum[experts],
        small_sum[:experts].T,
        upward_gradient,
        downward_gradient,
    )


def solution(mesh):
    return jax.shard_map(
        local,
        mesh=mesh,
        in_specs=(
            P("shard", "ctx", None),
            P("shard", None),
            P("shard", "ctx", None),
            P("shard", "ctx", None),
            P("shard"),
            P("shard"),
            P("shard", None, "tp"),
            P("shard", "tp"),
            P("shard"),
            P("shard", None),
            P("shard", None, None, "tp"),
            P("shard", None, "tp"),
        ),
        out_specs=(
            P("shard", "ctx", None),
            P("shard", "ctx", None),
            P("shard"),
            P("shard"),
            P("shard", None, "tp"),
            P("shard", "tp"),
            P("shard"),
            P("shard", None),
            P("shard", None, None, "tp"),
            P("shard", None, "tp"),
        ),
        check_vma=False,
    )
```

```python
import functools

import jax
import jax.numpy as jnp
from jax import lax
from jax.experimental import pallas as pl
from jax.experimental.pallas import tpu as pltpu
from jax.sharding import PartitionSpec as P

HEAD_DIM = 128
NORM_EPSILON = 1e-06
ROTARY_BASE = 50000.0
MASKED = -1e30
F32 = jnp.float32
BF16 = jnp.bfloat16
COST = pl.CostEstimate(flops=1024, bytes_accessed=1024, transcendentals=0)


def lower(values):
    return values.astype(BF16)


def dot(left, right, over, out=F32):
    result = lax.dot_general(left, right, (((over[0],), (over[1],)), ((), ())), preferred_element_type=F32)
    return result.astype(out)


def receive(values, axis, distance):
    size = lax.axis_size(axis)
    return lax.ppermute(values, axis, [((i + distance) % size, i) for i in range(size)])


def swap(values, axis, bit):
    size = lax.axis_size(axis)
    return lax.ppermute(values, axis, [(i, i ^ bit) for i in range(size)])


def bits(axis):
    size = lax.axis_size(axis)
    assert size & (size - 1) == 0
    found = [1 << i for i in range(size.bit_length() - 1)]
    return found


def masks(axis):
    order = [0]
    for bit in reversed(bits(axis)):
        order = order + [m ^ bit for m in order]
    return order


def gather_tp(values, beside=()):
    for k, bit in enumerate(reversed(bits("tp"))):
        far = swap(values, "tp", bit)
        values = jnp.concatenate([tie(values, beside[k]) if beside else values, far], axis=0)
    return values


def scatter_tp(values):
    for bit in bits("tp"):
        half = values.shape[0] // 2
        values = values[:half].astype(F32) + swap(lower(values[half:]), "tp", bit).astype(F32)
    return values


def gather_ctx(values):
    size = lax.axis_size("ctx")
    whole = jnp.concatenate([values] + [receive(values, "ctx", r) for r in range(1, size)], axis=0)
    return ahead_first(whole, lax.rem(size - lax.axis_index("ctx"), size) * values.shape[0])


def greet(peers, neighbours):
    barrier = pltpu.get_barrier_semaphore()
    for peer in peers:
        pl.semaphore_signal(barrier, inc=1, device_id=peer, device_id_type=pl.DeviceIdType.MESH)
    for there, peer in neighbours:

        @pl.when(there)
        def _():
            pl.semaphore_signal(barrier, inc=1, device_id=peer, device_id_type=pl.DeviceIdType.MESH)

    pl.semaphore_wait(barrier, len(peers) + sum(jnp.where(there, 1, 0) for there, _ in neighbours))


def remote(source, target, sent, arrived, place, peer):
    return pltpu.make_async_remote_copy(
        src_ref=source,
        dst_ref=target,
        send_sem=sent.at[place],
        recv_sem=arrived.at[place],
        device_id=peer,
        device_id_type=pl.DeviceIdType.MESH,
    )


def far_first(size):
    return sorted(range(1, size), key=lambda r: min(r, size - r))


def gather_kernel(size, pieces, arrays, shared, earlier, *refs):
    owns, outs = refs[:arrays], refs[arrays + earlier : 2 * arrays + earlier]
    held = refs[2 * arrays + earlier : 3 * arrays + earlier]
    local, z_sent, z_here, x_sent, x_here, core_sent, core_here = refs[3 * arrays + earlier :]
    c, t = lax.axis_index("ctx"), lax.axis_index("tp")
    x_peer, core_peer = {"tp": t ^ 2}, {"tp": t ^ 1}
    before, behind = {"ctx": lax.max(c - 1, 0)}, {"ctx": lax.min(c + 1, size - 1)}
    greet([x_peer, core_peer], ((c > 0, before), (c < size - 1, behind)))
    rows = outs[0].shape[2]
    step = rows // pieces
    cuts = [pl.ds(h * step, step) for h in range(pieces)]
    loads, keeps, z, x, core, places = [], [], {}, {}, {}, {}
    for n in range(arrays):
        loads.append(pltpu.make_async_copy(owns[n], held[n], local.at[n * 5 + 4]))
        for m in range(4 if shared else 1):
            part = held[n].at[pl.ds(pl.multiple_of((t ^ masks("tp")[m]) * rows, rows), rows)] if shared else held[n]
            keeps.append(pltpu.make_async_copy(part, outs[n].at[m, c], local.at[n * 5 + m]))
    for n in range(arrays):
        for r in range(size):
            for side in range(2 if r else 1):
                spot = lax.rem((c + r if side else c + size - r), size)
                for h in range(pieces):
                    key = (n, r, side, h)
                    place = (n * size + r) * pieces + h
                    if r:
                        source = outs[n].at[0, spot, cuts[h]]
                    else:
                        source = owns[n].at[pl.ds(pl.multiple_of(t * rows + h * step, step) if shared else h * step, step)]
                    there = [outs[n].at[m, spot, cuts[h]] for m in range(4)]
                    count = arrays * size * pieces
                    if r < size - 1:
                        for way in (0, 1) if r == 0 else (side,):
                            z[key + (way,)] = remote(
                                source, there[0], z_sent, z_here, way * count + place, before if way else behind
                            )
                    near = (n * size + spot) * pieces + h
                    if shared and not r:
                        continue
                    x[key] = remote(source, there[1], x_sent, x_here, near, x_peer)
                    core[(0,) + key] = remote(source, there[2], core_sent, core_here, near, core_peer)
                    core[(1,) + key] = remote(there[1], there[3], core_sent, core_here, count + near, core_peer)
                    if r:
                        places[key] = remote(
                            source, there[0], z_sent, z_here, side * count + place - pieces, before if side else behind
                        )

    def go_on(way):
        return c > 0 if way else c < size - 1

    pieces_of = [(n, h) for n in range(arrays) for h in range(pieces)]
    for n, h in pieces_of:
        for way in range(2):

            @pl.when(go_on(way))
            def _():
                z[n, 0, 0, h, way].start()

    for load in loads:
        load.start()
    if not shared:
        for n, h in pieces_of:
            x[n, 0, 0, h].start()
            core[0, n, 0, 0, h].start()
    for load in loads:
        load.wait()
    for keep in keeps:
        keep.start()
    arrivals = [(n, r, side, h) for r in range(1, size) for n in range(arrays) for side in range(2) for h in range(pieces)]

    def there_is(key):
        return c + key[1] < size if key[2] else c >= key[1]

    for key in arrivals:

        @pl.when(there_is(key))
        def _():
            places[key].wait_recv()
            if key[1] < size - 1:

                @pl.when(go_on(key[2]))
                def _():
                    z[key + (key[2],)].start()

            x[key].start()
            core[(0,) + key].start()

    if not shared:
        for n, h in pieces_of:
            x[n, 0, 0, h].wait_recv()
            core[1, n, 0, 0, h].start()
    for key in arrivals:

        @pl.when(there_is(key))
        def _():
            x[key].wait_recv()
            core[(1,) + key].start()

    if not shared:
        for n, h in pieces_of:
            x[n, 0, 0, h].wait_send()
            core[0, n, 0, 0, h].wait()
            core[1, n, 0, 0, h].wait()
    for key in arrivals:

        @pl.when(there_is(key))
        def _():
            x[key].wait_send()
            core[(0,) + key].wait()
            core[(1,) + key].wait()
            if key[1] < size - 1:

                @pl.when(go_on(key[2]))
                def _():
                    z[key + (key[2],)].wait_send()

    for n, h in pieces_of:
        for way in range(2):

            @pl.when(go_on(way))
            def _():
                z[n, 0, 0, h, way].wait_send()

    for keep in keeps:
        keep.wait()


def gather_rows(values, collective, *earlier, shared=False):
    size, tps = lax.axis_size("ctx"), lax.axis_size("tp")
    assert tps == 4
    pieces, arrays = 2, len(values)
    rows = values[0].shape[0] // (tps if shared else 1)
    count = arrays * size * pieces
    anywhere = pl.BlockSpec(memory_space=pl.ANY)
    return pl.pallas_call(
        functools.partial(gather_kernel, size, pieces, arrays, shared, len(earlier)),
        out_shape=[jax.ShapeDtypeStruct((tps, size, rows, v.shape[1]), v.dtype) for v in values],
        in_specs=[anywhere] * (arrays + len(earlier)),
        out_specs=[anywhere] * arrays,
        scratch_shapes=[pltpu.VMEM(v.shape, v.dtype) for v in values]
        + [
            pltpu.SemaphoreType.DMA((n,))
            for n in (5 * arrays, 2 * count, 2 * count, count, count, 2 * count, 2 * count)
        ],
        compiler_params=pltpu.CompilerParams(collective_id=collective, has_side_effects=True),
        name="gather_rows",
        cost_estimate=COST,
    )(*values, *earlier)


def scatter_kernel(size, arrays, aheads, small, earlier, *refs):
    parts, swaps = refs[:arrays], refs[arrays : arrays + len(aheads)]
    given, refs = refs[arrays + len(aheads) :][:small], refs[arrays + len(aheads) + small + earlier :]
    outs, swapped, refs = refs[:arrays], refs[arrays : arrays + len(aheads)], refs[arrays + len(aheads) :]
    summed, refs = refs[:small], refs[small:]
    if small:
        (given,), (summed,), (near, pair, blocks, small_sent, small_here) = given, summed, refs[-5:]
        refs = refs[:-5]
    helds, core_ins, x_ins, z_ins = [refs[k * arrays : (k + 1) * arrays] for k in range(4)]
    local, z_sent, z_here, x_sent, x_here, core_sent, core_here, y_sent, y_here = refs[4 * arrays :]
    c, t, s = lax.axis_index("ctx"), lax.axis_index("tp"), lax.axis_index("shard")
    shards = lax.axis_size("shard")
    rings = [{"shard": lax.rem(s + r, shards)} for r in range(1, shards)] if aheads else []
    x_peer, core_peer = {"tp": t ^ 2}, {"tp": t ^ 1}
    first, last = c == 0, c == size - 1
    upper = c // (size // 2)
    spot = [size - 1 - k + upper * (2 * k - size + 1) for k in range(size)]
    before, behind = {"ctx": lax.max(c - 1, 0)}, {"ctx": lax.min(c + 1, size - 1)}
    line = ((jnp.logical_not(first), before), (jnp.logical_not(last), behind))
    around = [{"ctx": lax.rem(c + r, size)} for r in range(1, size)] if small else []
    greet([x_peer, core_peer] + rings + around, () if small else line)
    if small:
        small_core = remote(given, near.at[0], small_sent, small_here, 0, core_peer)
        small_x = remote(pair, near.at[1], small_sent, small_here, 1, x_peer)
        small_ctx = [
            remote(blocks.at[c], blocks.at[c], small_sent, small_here, 1 + r, around[r - 1]) for r in range(1, size)
        ]
        small_from = [
            remote(blocks.at[b], blocks.at[b], small_sent, small_here, 1 + r, around[r - 1])
            for r, b in [(r, lax.rem(c + size - r, size)) for r in range(1, size)]
        ]
        small_core.start()
    keeps, core, x, rising, falling, finals = [], {}, {}, {}, {}, {}
    y = [remote(swaps[k], swapped[k], y_sent, y_here, k, rings[ahead - 1]) for k, ahead in enumerate(aheads)]
    for n in range(arrays):
        part, held, core_in, x_in, z_in = parts[n], helds[n], core_ins[n], x_ins[n], z_ins[n]
        keeps.append(pltpu.make_async_copy(part.at[pl.ds(0, 2)], held, local.at[n]))
        for m in (1, 0):
            for k in range(size):
                core[n, m, k] = remote(
                    part.at[2 + m, spot[k]], core_in.at[m, k], core_sent, core_here, (n * 2 + m) * size + k, core_peer
                )
        for k in range(size):
            a = spot[k]
            x[n, k] = remote(held.at[1, a], x_in.at[k], x_sent, x_here, n * size + k, x_peer)
            rising[n, k] = remote(held.at[0, a], z_in.at[0, a], z_sent, z_here, 2 * n * size + a, behind)
            falling[n, k] = remote(held.at[0, a], z_in.at[1, a], z_sent, z_here, (2 * n + 1) * size + a, before)
        finals[n] = [
            remote(held.at[0, c], z_in.at[0, c], z_sent, z_here, 2 * n * size + c, behind),
            remote(held.at[0, c], z_in.at[1, c], z_sent, z_here, (2 * n + 1) * size + c, before),
        ]
    for copy in list(core.values()) + y:
        copy.start()
    for keep in keeps:
        keep.start()
    for keep in keeps:
        keep.wait()
    tall = 16

    def each(body):
        @pl.loop(0, outs[0].shape[0] // tall)
        def _(i):
            body(pl.ds(pl.multiple_of(i * tall, tall), tall))

    order = [(n, k) for n in range(arrays) for k in range(size)]
    for n, k in order:
        a, held, core_in = spot[k], helds[n], core_ins[n]
        core[n, 1, k].wait_recv()

        def add_core(rows):
            held[1, a, rows] = (held[1, a, rows].astype(F32) + core_in[1, k, rows].astype(F32)).astype(BF16)

        each(add_core)
        x[n, k].start()
    if small:
        small_core.wait_recv()
        pair[...] = given[...] + near[0]
        small_x.start()
    for n, k in order:
        a, held, core_in, x_in, z_in, out = spot[k], helds[n], core_ins[n], x_ins[n], z_ins[n], outs[n]
        core[n, 0, k].wait_recv()
        x[n, k].wait_recv()

        def total(rows):
            return held[0, a, rows].astype(F32) + core_in[0, k, rows].astype(F32) + x_in[k, rows].astype(F32)

        def add(rows):
            held[0, a, rows] = total(rows).astype(BF16)

        def add_rising(rows):
            held[0, a, rows] = (total(rows) + z_in[0, a, rows].astype(F32)).astype(BF16)

        def add_falling(rows):
            held[0, a, rows] = (total(rows) + z_in[1, a, rows].astype(F32)).astype(BF16)

        def keep_total(rows):
            out[rows] = total(rows)

        @pl.when(a == c)
        def _():
            each(keep_total)

        @pl.when(a > c)
        def _():
            @pl.when(first)
            def _():
                each(add)

            @pl.when(jnp.logical_not(first))
            def _():
                rising[n, k].wait_recv()
                each(add_rising)

            rising[n, k].start()

        @pl.when(a < c)
        def _():
            @pl.when(last)
            def _():
                each(add)

            @pl.when(jnp.logical_not(last))
            def _():
                falling[n, k].wait_recv()
                each(add_falling)

            falling[n, k].start()

    if small:
        small_x.wait_recv()
        blocks[c] = pair[...] + near[1]
        for copy in small_ctx:
            copy.start()
    for n in range(arrays):
        for side, edge in enumerate((first, last)):
            z_in, out = z_ins[n], outs[n]

            @pl.when(jnp.logical_not(edge))
            def _():
                finals[n][side].wait_recv()

                def add_side(rows):
                    out[rows] = out[rows] + z_in[side, c, rows].astype(F32)

                each(add_side)

    for copy in y:
        copy.wait()
    if small:
        for copy in small_from:
            copy.wait_recv()
        summed[...] = sum(blocks[b] for b in range(1, size)) + blocks[0]
        for copy in [small_core, small_x] + small_ctx:
            copy.wait_send()
    for copy in list(core.values()) + list(x.values()):
        copy.wait_send()
    for n, k in order:

        @pl.when(spot[k] > c)
        def _():
            rising[n, k].wait_send()

        @pl.when(spot[k] < c)
        def _():
            falling[n, k].wait_send()


def scatter_rows(parts, collective, swaps, *earlier, small=None):
    size, arrays = lax.axis_size("ctx"), len(parts)
    rows, width = parts[0].shape[2:]
    moved = [v for v, _ in swaps]
    smalls = [] if small is None else [small]
    anywhere, held = pl.BlockSpec(memory_space=pl.ANY), pl.BlockSpec(memory_space=pltpu.VMEM)
    found = pl.pallas_call(
        functools.partial(
            scatter_kernel, size, arrays, tuple(ahead for _, ahead in swaps), len(smalls), len(earlier)
        ),
        out_shape=[jax.ShapeDtypeStruct((rows, width), F32)] * arrays
        + [jax.ShapeDtypeStruct(v.shape, v.dtype) for v in moved + smalls],
        in_specs=[anywhere] * (arrays + len(moved)) + [held] * len(smalls) + [anywhere] * len(earlier),
        out_specs=[held] * arrays + [anywhere] * len(moved) + [held] * len(smalls),
        scratch_shapes=[pltpu.VMEM((2, size, rows, width), BF16)] * (2 * arrays)
        + [pltpu.VMEM((size, rows, width), BF16)] * arrays
        + [pltpu.VMEM((2, size, rows, width), BF16)] * arrays
        + [
            pltpu.SemaphoreType.DMA((arrays * n,))
            for n in (1, 2 * size, 2 * size, size, size, 2 * size, 2 * size)
        ]
        + [pltpu.SemaphoreType.DMA((max(len(moved), 1),))] * 2
        + [pltpu.VMEM((n,) + v.shape, F32) if n else pltpu.VMEM(v.shape, F32) for v in smalls for n in (2, 0, size)]
        + [pltpu.SemaphoreType.DMA((1 + size,))] * (2 * len(smalls)),
        compiler_params=pltpu.CompilerParams(
            collective_id=collective, has_side_effects=True, vmem_limit_bytes=48 * 1024 * 1024
        ),
        name="scatter_rows",
        cost_estimate=COST,
    )(*parts, *moved, *smalls, *earlier)
    return found[:arrays], found[arrays:]


def own_block(values, ahead=0, axis=0):
    size = lax.axis_size("shard")
    block = values.shape[axis] // size
    spot = lax.rem(lax.axis_index("shard") + ahead, size)
    return lax.dynamic_slice_in_dim(values, spot * block, block, axis=axis)


def sum_shard(values, axis):
    size = lax.axis_size("shard")
    total = own_block(values, 0, axis)
    for r in range(1, size):
        total = total + receive(own_block(values, r, axis), "shard", size - r)
    return total


def product_parts(pairs):
    own = jnp.concatenate([dot(lefts[0], right, (0, 0)) for lefts, right in pairs], axis=1)
    others = tuple(
        jnp.concatenate([dot(lefts[r], right, (0, 0), BF16) for lefts, right in pairs], axis=1)
        for r in range(1, lax.axis_size("shard"))
    )
    return own, others


def product_swaps(others):
    return [(part, r) for r, part in enumerate(others, 1)]


def product_add(own, arrived):
    return own + sum(part.astype(F32) for part in arrived)


def product_sum(own, others):
    size = lax.axis_size("shard")
    for r in range(1, size):
        own = own + receive(others[r - 1], "shard", size - r).astype(F32)
    return own


def ahead_first(values, start, axis=0):
    return lax.dynamic_slice_in_dim(
        jnp.concatenate([values, values], axis=axis), start, values.shape[axis], axis=axis
    )


def gather_natural(values, axis_name, axis=0):
    return lax.all_gather(values, axis_name, axis=axis, tiled=True)


def gather_small(values, axis):
    size = lax.axis_size("shard")
    whole = jnp.concatenate([values] + [receive(values, "shard", r) for r in range(1, size)], axis=axis)
    return ahead_first(whole, lax.rem(size - lax.axis_index("shard"), size) * values.shape[axis], axis)


def corner(values):
    return values[(0,) * values.ndim]


def start_after(values):
    first = corner(values)
    return (first != first).astype(jnp.int32)


def tie(values, earlier):
    return values + (corner(earlier).astype(F32) * 0.0).astype(values.dtype)


def part_order(values):
    t = lax.axis_index("tp")
    return jnp.concatenate([lax.dynamic_index_in_dim(values, t ^ m, 1, False)[None] for m in masks("tp")], axis=0)


def natural_rows(values):
    t, order = lax.axis_index("tp"), masks("tp")
    part = values.shape[0] // len(order)
    found = []
    for q in range(len(order)):
        m, place = q ^ t, 0
        for i, bit in enumerate(reversed(bits("tp"))):
            place = place + jnp.where(m & bit, 1 << i, 0)
        found.append(lax.dynamic_slice_in_dim(values, place * part, part))
    return jnp.concatenate(found, axis=0)


def inverse_scale(values):
    return lax.rsqrt(jnp.mean(values * values, axis=-1, keepdims=True) + NORM_EPSILON)


def norm_back(grad, values, gain):
    scale = inverse_scale(values)
    weighted = grad * gain
    middle = jnp.mean(values * weighted, axis=-1, keepdims=True)
    return scale * weighted - values * (scale * scale * scale) * middle, grad * values * scale


def weights_kernel(ctxs, group, pieces, index, inward, outward, entry, *refs):
    exits, (first, others, head, leave) = refs[:ctxs], refs[ctxs:]
    c = index[0]
    tall = first.shape[0]
    deep = 16
    in_rows, out_rows = inward.shape[1], outward.shape[1]
    out_experts = 8
    half = lax.rem(c, out_experts // group) * group

    def picker(rows, kept, place):
        count = kept * deep
        to = lax.broadcasted_iota(jnp.int32, (count, rows * deep), 0)
        source = lax.broadcasted_iota(jnp.int32, (count, rows * deep), 1)
        return (source == to % deep * rows + place(to // deep)).astype(BF16)

    in_pick = picker(in_rows, in_rows, lambda row: row)
    kept = group * pieces
    out_pick = picker(out_rows, kept, lambda row: row // group * out_experts + half + row % group)

    def put(i, column, rows, value):
        if i:
            column = column + (i - 1) * 3 * pieces * 128
        (others if i else first)[rows, column : column + 128] = value

    def two(ref, step, rows):
        parts = [ref[slice((step + n) * deep, (step + n + 1) * deep)].reshape(deep * rows, 128) for n in range(2)]
        return jnp.concatenate(parts, axis=1)

    for step in range(0, tall // deep, 2):
        moved_in = matmul(in_pick, two(inward, step, in_rows)).astype(BF16)
        moved_out = matmul(out_pick, two(outward, step, out_rows)).astype(BF16)
        for n in range(2):
            rows, lanes = slice((step + n) * deep, (step + n + 1) * deep), slice(n * 128, (n + 1) * 128)
            for row in range(in_rows):
                i, piece, side = row // (2 * pieces), row // 2 % pieces, row % 2
                put(i, (side * pieces + piece) * 128, rows, moved_in[row * deep : (row + 1) * deep, lanes])
            for row in range(kept):
                i, piece = row % group, row // group
                put(i, (2 * pieces + piece) * 128, rows, moved_out[row * deep : (row + 1) * deep, lanes])
    for k in range(3):
        head[:, k * HEAD_DIM : (k + 1) * HEAD_DIM] = entry[k]
    for j in range(ctxs):
        leave[:, j * HEAD_DIM : (j + 1) * HEAD_DIM] = exits[j][...]


def own_weights(expert_in, expert_out, attention_in, attention_out):
    c, ctxs = lax.axis_index("ctx"), lax.axis_size("ctx")
    rows, experts, _, hidden = expert_in.shape
    group, pieces = experts // ctxs, hidden // 128
    assert group in (1, 2, 4, 8) and group * 2 * pieces % 16 == 0 and 8 * pieces % 16 == 0
    inward = expert_in.reshape(rows, experts, 2, pieces, 128).transpose(0, 1, 3, 2, 4).reshape(rows, -1, 128)
    outward = expert_out.reshape(rows, experts // 8, 8, pieces, 128).transpose(0, 1, 3, 2, 4).reshape(rows, -1, 128)
    entry = attention_in.transpose(1, 0, 2)
    tall = 64
    wide = 3 * hidden
    grid_spec = pltpu.PrefetchScalarGridSpec(
        num_scalar_prefetch=1,
        grid=(rows // tall,),
        in_specs=[
            pl.BlockSpec((tall, group * 2 * pieces, 128), lambda b, c: (b, c[0], 0)),
            pl.BlockSpec((tall, 8 * pieces, 128), lambda b, c: (b, c[0] * group // 8, 0)),
            pl.BlockSpec((3, tall, HEAD_DIM), lambda b, c: (0, b, c[0])),
        ]
        + [
            pl.BlockSpec((tall, HEAD_DIM), functools.partial(lambda j, b, c: (b, lax.rem(c[0] + j, ctxs)), j))
            for j in range(ctxs)
        ],
        out_specs=[
            pl.BlockSpec((tall, n), lambda b, c: (b, 0))
            for n in (wide, (group - 1) * wide, 3 * HEAD_DIM, ctxs * HEAD_DIM)
        ],
    )
    return pl.pallas_call(
        functools.partial(weights_kernel, ctxs, group, pieces),
        grid_spec=grid_spec,
        out_shape=[
            jax.ShapeDtypeStruct((rows, n), BF16)
            for n in (wide, (group - 1) * wide, 3 * HEAD_DIM, ctxs * HEAD_DIM)
        ],
        compiler_params=pltpu.CompilerParams(vmem_limit_bytes=48 * 1024 * 1024),
        name="own_weights",
        cost_estimate=COST,
    )(c.astype(jnp.int32)[None], inward, outward, entry, *([attention_out] * ctxs))


def matmul(left, right, over=(1, 0)):
    return lax.dot_general(left, right, (((over[0],), (over[1],)), ((), ())), preferred_element_type=F32)


def head_norm(values):
    return lax.rsqrt(jnp.mean(values * values, axis=-1, keepdims=True) + NORM_EPSILON)


def turned(values, cosine, sine):
    return values * cosine + pltpu.roll(values, values.shape[-1] // 2, 1) * sine


def shared_weights_kernel(ctxs, group, pieces, index, *refs):
    others = ctxs - 1
    inwards, outwards, outs = refs[:others], refs[others : 2 * others], refs[-others:]
    deep, hidden = 16, pieces * 128
    kinds, out_kinds = group * 2 * pieces, 8 * pieces

    def picker(rows, kept, place):
        to = lax.broadcasted_iota(jnp.int32, (kept * deep, rows * deep), 0)
        source = lax.broadcasted_iota(jnp.int32, (kept * deep, rows * deep), 1)
        return (source == to % deep * rows + place(to // deep)).astype(BF16)

    in_pick = picker(kinds, 2 * pieces, lambda r: (group - 1) * 2 * pieces + r)

    def two(ref, step, rows):
        parts = [ref[(step + n) * deep : (step + n + 1) * deep].reshape(deep * rows, 128) for n in range(2)]
        return jnp.concatenate(parts, axis=1)

    for k in range(others):
        inward, outward, out = inwards[k], outwards[k], outs[k]
        at = lax.rem(lax.rem(index[0] + k + 1, ctxs), 8 // group) * group + group - 1
        out_pick = picker(out_kinds, pieces, lambda r: r * 8 + at)

        def put(moved, step, r, column):
            for n in range(2):
                rows = slice((step + n) * deep, (step + n + 1) * deep)
                out[rows, column : column + 128] = moved[r * deep : (r + 1) * deep, n * 128 : (n + 1) * 128]

        for step in range(0, out.shape[0] // deep, 2):
            moved = matmul(in_pick, two(inward, step, kinds)).astype(BF16)
            for r in range(2 * pieces):
                put(moved, step, r, (r % 2 * pieces + r // 2) * 128)
            moved = matmul(out_pick, two(outward, step, out_kinds)).astype(BF16)
            for r in range(pieces):
                put(moved, step, r, (2 * pieces + r) * 128)


def shared_weights(expert_in, expert_out, *earlier):
    ctxs = lax.axis_size("ctx")
    rows, experts, _, hidden = expert_in.shape
    group, pieces = experts // ctxs, hidden // 128
    inward = expert_in.reshape(rows, experts, 2, pieces, 128).transpose(0, 1, 3, 2, 4).reshape(rows, -1, 128)
    outward = expert_out.reshape(rows, experts // 8, 8, pieces, 128).transpose(0, 1, 3, 2, 4).reshape(rows, -1, 128)
    tall, others = 64, ctxs - 1
    after = lambda k, c: lax.rem(c[0] + k + 1, ctxs)
    return pl.pallas_call(
        functools.partial(shared_weights_kernel, ctxs, group, pieces),
        grid_spec=pltpu.PrefetchScalarGridSpec(
            num_scalar_prefetch=1,
            grid=(rows // tall,),
            in_specs=[
                pl.BlockSpec(
                    (tall, group * 2 * pieces, 128), functools.partial(lambda k, b, c: (b, after(k, c), 0), k)
                )
                for k in range(others)
            ]
            + [
                pl.BlockSpec(
                    (tall, 8 * pieces, 128), functools.partial(lambda k, b, c: (b, after(k, c) * group // 8, 0), k)
                )
                for k in range(others)
            ]
            + [pl.BlockSpec(memory_space=pl.ANY)] * len(earlier),
            out_specs=[pl.BlockSpec((tall, 3 * hidden), lambda b, c: (b, 0))] * others,
        ),
        out_shape=[jax.ShapeDtypeStruct((rows, 3 * hidden), BF16)] * others,
        compiler_params=pltpu.CompilerParams(vmem_limit_bytes=48 * 1024 * 1024),
        name="shared_weights",
        cost_estimate=COST,
    )(lax.axis_index("ctx").astype(jnp.int32)[None], *([inward] * others), *([outward] * others), *earlier)


def project_kernel(tokens, gain, weight, gains, cosine, sine, normed, raw, query, key, value):
    values = tokens[...].astype(F32)
    low = (values * head_norm(values) * gain[...]).astype(BF16)
    normed[...] = low
    projected = matmul(low, weight[...])
    raw[...] = projected[:, : 2 * HEAD_DIM]
    for k, out in enumerate((query, key)):
        part = projected[:, k * HEAD_DIM : (k + 1) * HEAD_DIM]
        part = part * head_norm(part) * gains[k : k + 1, :]
        out[...] = turned(part, cosine[...], sine[...]).astype(BF16)
    value[...] = projected[:, 2 * HEAD_DIM :].astype(BF16)


def project(tokens, gain, weight, gains, cosine, sine):
    rows, width = tokens.shape
    tall = 256
    block = lambda n: pl.BlockSpec((tall, n), lambda b: (b, 0))
    whole = lambda v: pl.BlockSpec(v.shape, lambda b: (0, 0))
    head = jax.ShapeDtypeStruct((rows, HEAD_DIM), BF16)
    return pl.pallas_call(
        project_kernel,
        grid=(rows // tall,),
        in_specs=[block(width), whole(gain), whole(weight), whole(gains), block(HEAD_DIM), block(HEAD_DIM)],
        out_specs=[block(width), block(2 * HEAD_DIM)] + [block(HEAD_DIM)] * 3,
        out_shape=[
            jax.ShapeDtypeStruct((rows, width), BF16),
            jax.ShapeDtypeStruct((rows, 2 * HEAD_DIM), F32),
            head,
            head,
            head,
        ],
        compiler_params=pltpu.CompilerParams(vmem_limit_bytes=48 * 1024 * 1024),
        name="project",
        cost_estimate=COST,
    )(tokens, gain, weight, gains, cosine, sine)


def chances_of(query, key, row_doc, column_doc):
    scores = matmul(query, key, (1, 1)) * (HEAD_DIM**-0.5)
    scores = jnp.where(row_doc == column_doc, scores, MASKED)
    grown = jnp.exp(scores - jnp.max(scores, axis=-1, keepdims=True))
    return grown / jnp.sum(grown, axis=-1, keepdims=True)


def attend_kernel(query, key, value, row_doc, column_doc, mixed):
    chances = chances_of(query[...], key[...], row_doc[...], column_doc[...])
    mixed[...] = matmul(chances.astype(BF16), value[...]).astype(BF16)


def attend(query, key, value, row_doc, column_doc):
    rows = query.shape[0]
    tall = 256
    block = pl.BlockSpec((tall, HEAD_DIM), lambda b: (b, 0))
    whole = pl.BlockSpec((rows, HEAD_DIM), lambda b: (0, 0))
    return pl.pallas_call(
        attend_kernel,
        grid=(rows // tall,),
        in_specs=[
            block,
            whole,
            whole,
            pl.BlockSpec((tall, 1), lambda b: (b, 0)),
            pl.BlockSpec((1, rows), lambda b: (0, 0)),
        ],
        out_specs=block,
        out_shape=jax.ShapeDtypeStruct((rows, HEAD_DIM), BF16),
        compiler_params=pltpu.CompilerParams(vmem_limit_bytes=48 * 1024 * 1024),
        name="attend",
        cost_estimate=COST,
    )(query, key, value, row_doc, column_doc)


def attend_back_kernel(
    tall, query, key, value, raw, cosine, sine, gains, row_doc, column_doc, mixed_grad, *refs
):
    grad, gain_grad, key_grad, value_grad = refs[-4:]
    step = pl.program_id(0)
    rows = pl.ds(pl.multiple_of(step * tall, tall), tall)

    def projected_back(turned_grad, k, where):
        values = raw[where, k * HEAD_DIM : (k + 1) * HEAD_DIM]
        grown = turned(turned_grad, cosine[where], -sine[where])
        scale = head_norm(values)
        weighted = grown * gains[k : k + 1, :]
        middle = jnp.mean(values * weighted, axis=-1, keepdims=True)
        part = jnp.sum(grown * values * scale, axis=0, keepdims=True)
        return scale * weighted - values * (scale * scale * scale) * middle, part

    @pl.when(step == 0)
    def _():
        key_grad[...] = jnp.zeros_like(key_grad)
        value_grad[...] = jnp.zeros_like(value_grad)
        gain_grad[...] = jnp.zeros_like(gain_grad)

    here = query[...]
    chances = chances_of(here, key[...], row_doc[...], column_doc[...])
    upstream = mixed_grad[...]
    weight_grad = matmul(upstream, value[...], (1, 1))
    score_grad = chances * (weight_grad - jnp.sum(chances * weight_grad, axis=-1, keepdims=True))
    score_grad = score_grad.astype(BF16)
    scale = HEAD_DIM**-0.5
    query_grad, part = projected_back(matmul(score_grad, key[...]) * scale, 0, rows)
    grad[rows, :HEAD_DIM] = query_grad.astype(BF16)
    gain_grad[0:1, :] += part
    key_grad[...] += matmul(score_grad, here, (0, 0)) * scale
    value_grad[...] += matmul(chances.astype(BF16), upstream, (0, 0))

    @pl.when(step == pl.num_programs(0) - 1)
    def _():
        back, part = projected_back(key_grad[...], 1, slice(None))
        grad[:, HEAD_DIM : 2 * HEAD_DIM] = back.astype(BF16)
        gain_grad[1:2, :] += part
        grad[:, 2 * HEAD_DIM :] = value_grad[...].astype(BF16)


def attend_back(query, key, value, raw, cosine, sine, gains, row_doc, column_doc, mixed_grad, *earlier):
    rows = query.shape[0]
    tall = 256
    block = pl.BlockSpec((tall, HEAD_DIM), lambda b: (b, 0))
    whole = lambda v: pl.BlockSpec(v.shape, lambda b: (0, 0))
    return pl.pallas_call(
        functools.partial(attend_back_kernel, tall),
        grid=(rows // tall,),
        in_specs=[
            block,
            whole(key),
            whole(value),
            whole(raw),
            whole(cosine),
            whole(sine),
            whole(gains),
            pl.BlockSpec((tall, 1), lambda b: (b, 0)),
            whole(column_doc),
            block,
        ]
        + [pl.BlockSpec(memory_space=pl.ANY)] * len(earlier),
        out_specs=[
            pl.BlockSpec((rows, 3 * HEAD_DIM), lambda b: (0, 0)),
            pl.BlockSpec((8, HEAD_DIM), lambda b: (0, 0)),
        ],
        out_shape=[
            jax.ShapeDtypeStruct((rows, 3 * HEAD_DIM), BF16),
            jax.ShapeDtypeStruct((8, HEAD_DIM), F32),
        ],
        scratch_shapes=[pltpu.VMEM((rows, HEAD_DIM), F32)] * 2,
        compiler_params=pltpu.CompilerParams(vmem_limit_bytes=48 * 1024 * 1024),
        name="attend_back",
        cost_estimate=COST,
    )(query, key, value, raw, cosine, sine, gains, row_doc, column_doc, mixed_grad, *earlier)


def expert_step_kernel(index, count, earlier, shard, rows, upstream, *refs):
    gate_in, up_in, outward = [refs[k * count : (k + 1) * count] for k in range(3)]
    gates, lanes, scaled, inner_grad, gate_part = refs[3 * count], refs[3 * count + 1], *refs[3 * count + 2 + earlier :]
    hidden_size = outward[0].shape[1]
    deep = outward[0].shape[0]

    def product(left, parts):
        total = 0.0
        for r, part in enumerate(parts):
            start = pl.multiple_of(lax.rem(shard[0] + r, count) * deep, deep) if count > 1 else 0
            total = total + matmul(left[:, pl.ds(start, deep)], part[...])
        return total

    gate, up, back = product(rows, gate_in), product(rows, up_in), product(upstream, outward)
    sigmoid = 1.0 / (1.0 + jnp.exp(-gate))
    silu = gate * sigmoid
    hidden = (silu * up).astype(BF16).astype(F32)
    weight = gates[:, index : index + 1]
    scaled[...] = (hidden * weight).astype(BF16)
    gate_part[...] = jnp.sum(hidden * back, axis=1, keepdims=True) * lanes[index : index + 1, :]
    hidden_grad = back * weight
    inner_grad[:, :hidden_size] = (hidden_grad * up * sigmoid * (1.0 + gate * (1.0 - sigmoid))).astype(BF16)
    inner_grad[:, hidden_size:] = (hidden_grad * silu).astype(BF16)


def expert_step(index, place, rows, upstream, weights, hidden_size, gates, lanes, *earlier):
    count, width = rows.shape
    tall, parts = 256, len(weights)
    block = lambda n: pl.BlockSpec((tall, n), lambda b, s: (b, 0))
    whole = weights[0].shape[0] == width

    def column(k, r, b, s):
        return (lax.rem(s[0] + r, parts) if whole else 0, 3 * place + k)

    columns = [
        pl.BlockSpec((width // parts, hidden_size), functools.partial(column, k, r))
        for k in range(3)
        for r in range(parts)
    ]
    return pl.pallas_call(
        functools.partial(expert_step_kernel, index, parts, len(earlier)),
        grid_spec=pltpu.PrefetchScalarGridSpec(
            num_scalar_prefetch=1,
            grid=(count // tall,),
            in_specs=[block(width), block(width)]
            + columns
            + [block(gates.shape[1]), pl.BlockSpec(lanes.shape, lambda b, s: (0, 0))]
            + [pl.BlockSpec(memory_space=pl.ANY)] * len(earlier),
            out_specs=[block(hidden_size), block(2 * hidden_size), block(128)],
        ),
        out_shape=[
            jax.ShapeDtypeStruct((count, hidden_size), BF16),
            jax.ShapeDtypeStruct((count, 2 * hidden_size), BF16),
            jax.ShapeDtypeStruct((count, 128), F32),
        ],
        compiler_params=pltpu.CompilerParams(vmem_limit_bytes=48 * 1024 * 1024),
        name="expert_step",
        cost_estimate=COST,
    )(lax.axis_index("shard").astype(jnp.int32)[None], rows, upstream, *(list(weights) * 3), gates, lanes, *earlier)


def combine_kernel(count, extras, *refs):
    lefts, rights, lanes, out = refs[:count], refs[count : 2 * count], refs[2 * count : 2 * count + extras], refs[-1]
    width = rights[0].shape[0]
    total = matmul(lefts[0][...], rights[0][...], (1, 1))
    for left, right in zip(lefts[1:], rights[1:]):
        total = total + matmul(left[...], right[...], (1, 1))
    out[:, :width] = total.astype(BF16)
    if extras:
        out[:, width:] = sum(lane[...] for lane in lanes).astype(BF16)


def combine(lefts, rights, lanes, *earlier):
    (rows, _), (width, _) = lefts[0][0].shape, rights[0][0].shape
    tall, deep = 256, 256
    total = width + (lanes[0].shape[1] if lanes else 0)
    return pl.pallas_call(
        lambda *refs: combine_kernel(len(lefts), len(lanes), *refs[: len(refs) - 1 - len(earlier)], refs[-1]),
        grid=(rows // tall,),
        in_specs=[pl.BlockSpec((tall, deep), functools.partial(lambda k, b: (b, k), k)) for _, k in lefts]
        + [
            pl.BlockSpec((width, deep), functools.partial(lambda k, b: (0, k), k), pipeline_mode=pl.Buffered(1))
            for _, k in rights
        ]
        + [pl.BlockSpec((tall, lane.shape[1]), lambda b: (b, 0)) for lane in lanes]
        + [pl.BlockSpec(memory_space=pl.ANY)] * len(earlier),
        out_specs=pl.BlockSpec((tall, total), lambda b: (b, 0)),
        out_shape=jax.ShapeDtypeStruct((rows, total), BF16),
        compiler_params=pltpu.CompilerParams(vmem_limit_bytes=56 * 1024 * 1024),
        name="combine",
        cost_estimate=COST,
    )(*[v for v, _ in lefts], *[v for v, _ in rights], *lanes, *earlier)


def gradient_kernel(steps, index, rows, upstream, inner_grad, scaled, own, others):
    step = pl.program_id(0)
    wide = inner_grad.shape[1]

    def put(out):
        out[:, :wide] = matmul(rows[...], inner_grad[...], (0, 0)).astype(out.dtype)
        out[:, wide:] = matmul(upstream[...], scaled[...], (0, 0)).astype(out.dtype)

    @pl.when(step < steps)
    def _():
        put(own)

    @pl.when(step >= steps)
    def _():
        put(others)


def gradient_parts(rows, upstream, inner_grad, scaled):
    s, shards = lax.axis_index("shard"), lax.axis_size("shard")
    count, width = rows.shape
    deep = 256
    steps = width // shards // deep
    wide = inner_grad.shape[1] + scaled.shape[1]
    feature = pl.BlockSpec((count, deep), lambda b, s: (0, lax.rem(s[0] * steps + b, steps * shards)))
    whole = lambda v: pl.BlockSpec(v.shape, lambda b, s: (0, 0))
    return pl.pallas_call(
        functools.partial(gradient_kernel, steps),
        grid_spec=pltpu.PrefetchScalarGridSpec(
            num_scalar_prefetch=1,
            grid=(steps * shards,),
            in_specs=[feature, feature, whole(inner_grad), whole(scaled)],
            out_specs=[
                pl.BlockSpec((deep, wide), lambda b, s: (lax.min(b, steps - 1), 0)),
                pl.BlockSpec((deep, wide), lambda b, s: (lax.max(b - steps, 0), 0)),
            ],
        ),
        out_shape=[
            jax.ShapeDtypeStruct((steps * deep, wide), F32),
            jax.ShapeDtypeStruct((steps * deep * (shards - 1), wide), BF16),
        ],
        compiler_params=pltpu.CompilerParams(vmem_limit_bytes=48 * 1024 * 1024),
        name="gradient_parts",
        cost_estimate=COST,
    )(s.astype(jnp.int32)[None], rows, upstream, inner_grad, scaled)


def expert_kernel(group, ctxs, tall, hidden, index, *refs):
    gathered, shared, (up, down) = refs[: group - 1], refs[group - 1 : group - 1 + ctxs], refs[group - 1 + ctxs :]
    pieces = hidden // 128
    experts = group * ctxs
    deep = 16
    to = lax.broadcasted_iota(jnp.int32, (deep * deep, deep * deep), 0)
    source = lax.broadcasted_iota(jnp.int32, (deep * deep, deep * deep), 1)
    turn = (source == to % deep * deep + to // deep).astype(BF16)

    def tile(e, column, start):
        rows, columns = slice(start, start + deep), slice(column, column + 128)
        if e % group == group - 1:
            return shared[e // group][0, rows, columns]
        return gathered[e % group][e // group, rows, columns]

    def place(out, kinds, start):
        blocks = [jnp.concatenate([tile(e, column, start) for e, column in kinds[k : k + deep]], axis=0) for k in range(0, len(kinds), deep)]
        for k in range(0, len(blocks), 2):
            pair = blocks[k : k + 2]
            moved = matmul(turn, jnp.concatenate(pair, axis=1))
            for n in range(len(pair)):
                for d in range(deep):
                    row = (start + d) * len(kinds) + (k + n) * deep
                    out[row : row + deep, :] = moved[d * deep : (d + 1) * deep, n * 128 : (n + 1) * 128]

    ups = [(e, (side * pieces + piece) * 128) for e in range(experts) for piece in range(pieces) for side in range(2)]
    downs = [
        (part * 8 + e, (2 * pieces + piece) * 128)
        for part in range(experts // 8)
        for piece in range(pieces)
        for e in range(8)
    ]
    for start in range(0, tall, deep):
        place(up, ups, start)
        place(down, downs, start)


def expert_gradients(gathered, shared):
    (ctxs, rows, width), group = shared.shape, len(gathered) + 1
    hidden, experts = width // 3, group * ctxs
    pieces = hidden // 128
    assert experts % 8 == 0 and hidden % 128 == 0
    tall = 64
    up, down = pl.pallas_call(
        functools.partial(expert_kernel, group, ctxs, tall, hidden),
        grid_spec=pltpu.PrefetchScalarGridSpec(
            num_scalar_prefetch=1,
            grid=(rows // tall,),
            in_specs=[pl.BlockSpec((ctxs, tall, width), lambda b, c: (0, b, 0))] * len(gathered)
            + [
                pl.BlockSpec(
                    (1, tall, width), functools.partial(lambda j, b, c: (lax.rem(ctxs + j - c[0], ctxs), b, 0), j)
                )
                for j in range(ctxs)
            ],
            out_specs=[pl.BlockSpec((tall * experts * pieces * k, 128), lambda b, c: (b, 0)) for k in (2, 1)],
        ),
        out_shape=[jax.ShapeDtypeStruct((rows * experts * pieces * k, 128), F32) for k in (2, 1)],
        compiler_params=pltpu.CompilerParams(vmem_limit_bytes=48 * 1024 * 1024),
        name="expert_gradients",
        cost_estimate=COST,
    )(lax.axis_index("ctx").astype(jnp.int32)[None], *gathered, *([shared] * ctxs))
    up = up.reshape(rows, experts, pieces, 2, 128).transpose(0, 1, 3, 2, 4).reshape(rows, experts, 2, hidden)
    down = down.reshape(rows, experts // 8, pieces, 8, 128).transpose(0, 1, 3, 2, 4).reshape(rows, experts, hidden)
    return up, down


def attention_kernel(chunk, entry, exit_out):
    ctxs, _, width = chunk.shape
    head = width // 4
    for j in range(ctxs):
        for k in range(3):
            entry[k, :, j * head : (j + 1) * head] = chunk[j, :, k * head : (k + 1) * head].astype(F32)
        exit_out[:, j * head : (j + 1) * head] = chunk[j, :, 3 * head :].astype(F32)


def attention_gradients(chunk):
    ctxs, rows, width = chunk.shape
    wide = ctxs * width // 4
    tall = 128
    entry, exit_out = pl.pallas_call(
        attention_kernel,
        grid=(rows // tall,),
        in_specs=[pl.BlockSpec((ctxs, tall, width), lambda b: (0, b, 0))],
        out_specs=[pl.BlockSpec((3, tall, wide), lambda b: (0, b, 0)), pl.BlockSpec((tall, wide), lambda b: (b, 0))],
        out_shape=[jax.ShapeDtypeStruct((3, rows, wide), F32), jax.ShapeDtypeStruct((rows, wide), F32)],
        name="attention_gradients",
        cost_estimate=COST,
    )(chunk)
    return entry.transpose(1, 0, 2), exit_out


def local(
    tokens,
    segments,
    routes,
    cotangent,
    first_gain,
    head_gain,
    attention_in,
    attention_out,
    second_gain,
    router_weight,
    expert_in,
    expert_out,
):
    s, c, t = lax.axis_index("shard"), lax.axis_index("ctx"), lax.axis_index("tp")
    shards, ctxs, tps = lax.axis_size("shard"), lax.axis_size("ctx"), lax.axis_size("tp")
    rows, width = tokens.shape[1:]
    own = rows // tps
    block = width // shards
    every = rows * ctxs
    experts = router_weight.shape[1]
    hidden_size = expert_out.shape[2]
    local_width = attention_out.shape[1]
    head_size = local_width // ctxs

    group = experts // ctxs
    base = c * group

    gains = gather_small(jnp.stack([first_gain, second_gain]), 1).astype(F32)
    gain_one, gain_two = gains[0], gains[1]
    head_gains = gather_small(head_gain[None], 1)[0].astype(F32)
    first_weights, others, head_in, exit_weight = own_weights(expert_in, expert_out, attention_in, attention_out)
    tokens_all, cot_all = gather_rows([tokens[0], cotangent[0]], 3, head_in, shared=True)
    tokens_all, cot_all = tokens_all.reshape(every, width), cot_all.reshape(every, width)
    head_in = gather_natural(head_in, "shard")
    first_weights, others = gather_natural(first_weights, "shard"), gather_natural(others, "shard")
    exit_weights = [exit_weight] + [receive(exit_weight, "shard", r) for r in range(1, shards)]
    first = t * own
    tokens_own = lax.dynamic_slice_in_dim(tokens[0], first, own)
    cot_own = lax.dynamic_slice_in_dim(cotangent[0], first, own)

    layer_in = tokens_own.astype(F32)
    upstream = cot_own.astype(F32)
    choices_all = gather_ctx(routes[0]).reshape(ctxs, tps, own, -1)
    picks_all = jnp.any(part_order(choices_all)[..., None] == jnp.arange(experts), axis=3)
    picks = lax.dynamic_index_in_dim(picks_all[0], c, 0, False)
    picks_all = picks_all.reshape(every, experts)
    router = gather_small(router_weight, 0)

    assert head_size == HEAD_DIM
    spot = part_order(jnp.arange(every, dtype=jnp.int32).reshape(ctxs, tps, own)).reshape(-1)
    documents = part_order(segments[0].reshape(ctxs, tps, own)).reshape(-1)
    row_doc, column_doc = documents[:, None], documents[None, :]
    steps = jnp.arange(HEAD_DIM // 2).astype(F32)
    frequency = ROTARY_BASE ** (-2.0 * steps / HEAD_DIM)
    angles = spot.astype(F32)[:, None] * frequency[None, :]
    cosine, sine = jnp.cos(angles), jnp.sin(angles)
    cosine, sine = jnp.concatenate([cosine, cosine], axis=1), jnp.concatenate([-sine, sine], axis=1)
    head_gains = head_gains.reshape(2, HEAD_DIM)
    normed_one_all, raw, queries, keys, values = project(
        tokens_all, gain_one[None], head_in, head_gains, cosine, sine
    )
    mixed_head = attend(queries, keys, values, row_doc, column_doc)
    blocks = ahead_first(mixed_head.reshape(tps, ctxs, own, head_size), c, 1)
    mixed = [blocks[:, 0]] + [receive(blocks[:, ctxs - j], "ctx", j) for j in range(1, ctxs)]
    mixed = jnp.concatenate([m.reshape(rows, head_size) for m in mixed], axis=1)
    attended = scatter_tp(jnp.concatenate([dot(mixed, w, (1, 1)) for w in exit_weights], axis=1))
    residual = layer_in + ahead_first(attended, lax.rem(shards - s, shards) * block, 1)

    normed_two = lower(residual * inverse_scale(residual) * gain_two)
    normed_two_all = gather_rows([normed_two], 0)[0].reshape(every, width)
    chances_all = jax.nn.softmax(dot(normed_two_all, router, (1, 0)), axis=-1)
    gates_all = jnp.where(picks_all, chances_all, 0.0)
    gates = lax.dynamic_slice_in_dim(gates_all, base, group, axis=1)
    lanes = (jnp.arange(128)[None] == base + jnp.arange(group)[:, None]).astype(F32)
    scaled, gate_parts, inner_grads, products = [], [], [], []

    def gradient_blocks(inner_grad, gated):
        own_part, far = gradient_parts(normed_two_all, cot_all, inner_grad, gated)
        return own_part, tuple(far[r * block : (r + 1) * block] for r in range(shards - 1))

    last = group - 1
    before = []
    for i in range(group):
        weights = [others] * shards if i == last else [others] if i else [first_weights]
        step = expert_step(
            i, max(i - 1, 0), normed_two_all, cot_all, weights, hidden_size, gates, lanes, *before
        )
        scaled.append(step[0])
        inner_grads.append(step[1])
        gate_parts.append(step[2])
        products.append(gradient_blocks(inner_grads[i], scaled[i]))
        before = list(products[i][1])
        if i == 1:
            shared = shared_weights(expert_in, expert_out, *before)
            before += shared
    chunks, gathered = [], []
    for i in range(last):
        own_part, far = products[i]
        chunks.append(lower(product_sum(tie(own_part, inner_grads[i + 1] if i else products[1][1][0]), far)))
        gathered.append(lax.all_gather(chunks[i], "ctx", axis=0, tiled=False))
    columns = lambda k: [(others if i else first_weights, 3 * max(i - 1, 0) + k) for i in range(group)]
    normed_part = combine(
        [(v, k) for k in range(2) for v in inner_grads], columns(0) + columns(1), gate_parts, *before
    )
    weight_swaps = lambda weights: [(w, shards - r) for w in weights for r in range(1, shards)]
    (normed_sum,), arrived = scatter_rows([normed_part.reshape(tps, ctxs, own, -1)], 1, weight_swaps(shared[:-1]))
    shared_all = [[w] + list(arrived[k * (shards - 1) : (k + 1) * (shards - 1)]) for k, w in enumerate(shared[:-1])]
    normed_sum = tie(normed_sum, gathered[0])
    normed_sum, gate_grad = normed_sum[:, :width], normed_sum[:, width : width + experts]

    router_chances = jax.nn.softmax(dot(normed_two, router, (1, 0)), axis=-1)
    chance_grad = jnp.where(picks, gate_grad, 0.0)
    logit_grad = lower(
        router_chances * (chance_grad - jnp.sum(router_chances * chance_grad, axis=-1, keepdims=True))
    )
    router_part = dot(logit_grad, normed_two, (0, 0))
    normed_grad = normed_sum + dot(logit_grad, router, (1, 1))
    residual_back, second_part = norm_back(normed_grad, residual, gain_two)
    residual_grad = upstream + residual_back

    attend_grad = gather_tp(lower(residual_grad))
    attend_blocks = [own_block(attend_grad, r, 1) for r in range(shards)]
    exit_parts = product_parts([(attend_blocks, mixed)])
    mixed_grad = lower(sum(dot(v, w, (1, 0)) for v, w in zip(attend_blocks, exit_weights)))
    mixed_grad = mixed_grad.reshape(tps, own, ctxs, head_size)
    parts = [mixed_grad[:, :, 0]] + [receive(mixed_grad[:, :, ctxs - j], "ctx", j) for j in range(1, ctxs)]
    mixed_grad = ahead_first(jnp.stack(parts, axis=1), lax.rem(ctxs - c, ctxs), 1)
    mixed_grad = mixed_grad.reshape(every, HEAD_DIM)
    projected_grad, gain_part = attend_back(
        queries, keys, values, raw, cosine, sine, head_gains, row_doc, column_doc, mixed_grad
    )
    entry_blocks = [own_block(normed_one_all, r, 1) for r in range(shards)]
    entry_parts = product_parts([(entry_blocks, projected_grad)])
    shared_gates = ahead_first(gates_all[:, last::group], c, 1)
    shared_all += [[w] + [receive(w, "shard", r) for r in range(1, shards)] for w in shared[len(shared_all) :]]
    exit_part = product_sum(*exit_parts)
    shared_products = [products[last]]
    shared_chunks = [lower(product_sum(*products[last]))]
    earlier = [exit_part, *entry_parts[1], *chunks]
    for j in range(1, ctxs):
        step = expert_step(
            j, 0, normed_two_all, cot_all, shared_all[j - 1], hidden_size, shared_gates, lanes, *earlier
        )
        parts = gradient_blocks(step[1], step[0])
        shared_products.append(parts)
        earlier = list(parts[1])
        if j == 1:
            exit_head = tie(exit_part[:, :head_size], parts[1][0])
            for r in range(1, ctxs):
                exit_head = exit_head + receive(
                    lower(exit_part[:, r * head_size : (r + 1) * head_size]), "ctx", ctxs - r
                ).astype(F32)
            earlier += [shared_chunks[0], gathered[1], *shared_all[-1][1:]]
        if j == 2:
            entry_head = product_sum(tie(entry_parts[0], parts[1][0]), entry_parts[1])
            attention_chunk = lower(jnp.concatenate([entry_head, exit_head], axis=1))
            attention_gathered = lax.all_gather(attention_chunk, "ctx", axis=0, tiled=False)

    result_part = combine([(v, 0) for v in scaled], columns(2), [], *earlier, attention_chunk)
    first_part = dot(projected_grad, head_in, (1, 1), BF16)
    tokens_wide = tokens_all.astype(F32)
    first_sum = jnp.sum(first_part.astype(F32) * tokens_wide * inverse_scale(tokens_wide), axis=0)
    head_part = gain_part[:2].reshape(1, -1)
    small_part = [jnp.sum(second_part, axis=0)[None], first_sum[None], jnp.pad(head_part, ((0, 0), (0, width - head_part.shape[1])))]
    small_part = jnp.concatenate([router_part] + small_part, axis=0)
    small_part = jnp.pad(small_part, ((0, -small_part.shape[0] % 8), (0, 0)))
    shared_chunks.append(lower(product_sum(*shared_products[1])))
    (first_normed_grad, result_sum), arrived = scatter_rows(
        [part.reshape(tps, ctxs, own, width) for part in (first_part, result_part)],
        2,
        sum([product_swaps(p[1]) for p in shared_products[2:]], []),
        shared_chunks[1],
        small=small_part,
    )
    head_gradient = sum_shard(arrived[-1][experts + 2 : experts + 3, : head_part.shape[1]], 1)[0]
    small_sum = sum_shard(arrived[-1][: experts + 2], 1)
    for k, p in enumerate(shared_products[2:]):
        shared_chunks.append(lower(product_add(p[0], arrived[k * (shards - 1) : (k + 1) * (shards - 1)])))
    layer_output = natural_rows(gather_tp(lower(residual + result_sum)))[None]
    input_back, _ = norm_back(first_normed_grad, layer_in, gain_one)
    input_gradient = natural_rows(gather_tp(lower(residual_grad + input_back))).astype(F32)[None]

    upward_gradient, downward_gradient = expert_gradients(
        gathered, jnp.stack(shared_chunks)
    )
    entry_gradient, exit_gradient = attention_gradients(attention_gathered)
    return (
        layer_output,
        input_gradient,
        small_sum[experts + 1],
        head_gradient,
        entry_gradient,
        exit_gradient,
        small_sum[experts],
        small_sum[:experts].T,
        upward_gradient,
        downward_gradient,
    )


def solution(mesh):
    return jax.shard_map(
        local,
        mesh=mesh,
        in_specs=(
            P("shard", "ctx", None),
            P("shard", None),
            P("shard", "ctx", None),
            P("shard", "ctx", None),
            P("shard"),
            P("shard"),
            P("shard", None, "tp"),
            P("shard", "tp"),
            P("shard"),
            P("shard", None),
            P("shard", None, None, "tp"),
            P("shard", None, "tp"),
        ),
        out_specs=(
            P("shard", "ctx", None),
            P("shard", "ctx", None),
            P("shard"),
            P("shard"),
            P("shard", None, "tp"),
            P("shard", "tp"),
            P("shard"),
            P("shard", None),
            P("shard", None, None, "tp"),
            P("shard", None, "tp"),
        ),
        check_vma=False,
    )
```

```python
import functools

import jax
import jax.numpy as jnp
from jax import lax
from jax.experimental import pallas as pl
from jax.experimental.pallas import tpu as pltpu
from jax.sharding import PartitionSpec as P

HEAD_DIM = 128
NORM_EPSILON = 1e-06
ROTARY_BASE = 50000.0
MASKED = -1e30
F32 = jnp.float32
BF16 = jnp.bfloat16
COST = pl.CostEstimate(flops=1024, bytes_accessed=1024, transcendentals=0)


def lower(values):
    return values.astype(BF16)


def dot(left, right, over, out=F32):
    result = lax.dot_general(left, right, (((over[0],), (over[1],)), ((), ())), preferred_element_type=F32)
    return result.astype(out)


def receive(values, axis, distance):
    size = lax.axis_size(axis)
    return lax.ppermute(values, axis, [((i + distance) % size, i) for i in range(size)])


def swap(values, axis, bit):
    size = lax.axis_size(axis)
    return lax.ppermute(values, axis, [(i, i ^ bit) for i in range(size)])


def bits(axis):
    size = lax.axis_size(axis)
    assert size & (size - 1) == 0
    found = [1 << i for i in range(size.bit_length() - 1)]
    return found


def masks(axis):
    order = [0]
    for bit in reversed(bits(axis)):
        order = order + [m ^ bit for m in order]
    return order


def gather_tp(values, beside=()):
    for k, bit in enumerate(reversed(bits("tp"))):
        far = swap(values, "tp", bit)
        values = jnp.concatenate([tie(values, beside[k]) if beside else values, far], axis=0)
    return values


def scatter_tp(values):
    for bit in bits("tp"):
        half = values.shape[0] // 2
        values = values[:half].astype(F32) + swap(lower(values[half:]), "tp", bit).astype(F32)
    return values


def gather_ctx(values):
    size = lax.axis_size("ctx")
    whole = jnp.concatenate([values] + [receive(values, "ctx", r) for r in range(1, size)], axis=0)
    return ahead_first(whole, lax.rem(size - lax.axis_index("ctx"), size) * values.shape[0])


def greet(peers, neighbours):
    barrier = pltpu.get_barrier_semaphore()
    for peer in peers:
        pl.semaphore_signal(barrier, inc=1, device_id=peer, device_id_type=pl.DeviceIdType.MESH)
    for there, peer in neighbours:

        @pl.when(there)
        def _():
            pl.semaphore_signal(barrier, inc=1, device_id=peer, device_id_type=pl.DeviceIdType.MESH)

    pl.semaphore_wait(barrier, len(peers) + sum(jnp.where(there, 1, 0) for there, _ in neighbours))


def remote(source, target, sent, arrived, place, peer):
    return pltpu.make_async_remote_copy(
        src_ref=source,
        dst_ref=target,
        send_sem=sent.at[place],
        recv_sem=arrived.at[place],
        device_id=peer,
        device_id_type=pl.DeviceIdType.MESH,
    )


def far_first(size):
    return sorted(range(1, size), key=lambda r: min(r, size - r))


def gather_kernel(size, pieces, arrays, shared, earlier, *refs):
    owns, outs = refs[:arrays], refs[arrays + earlier : 2 * arrays + earlier]
    held = refs[2 * arrays + earlier : 3 * arrays + earlier]
    local, z_sent, z_here, x_sent, x_here, core_sent, core_here = refs[3 * arrays + earlier :]
    c, t = lax.axis_index("ctx"), lax.axis_index("tp")
    x_peer, core_peer = {"tp": t ^ 2}, {"tp": t ^ 1}
    before, behind = {"ctx": lax.max(c - 1, 0)}, {"ctx": lax.min(c + 1, size - 1)}
    greet([x_peer, core_peer], ((c > 0, before), (c < size - 1, behind)))
    rows = outs[0].shape[2]
    step = rows // pieces
    cuts = [pl.ds(h * step, step) for h in range(pieces)]
    loads, keeps, z, x, core, places = [], [], {}, {}, {}, {}
    for n in range(arrays):
        loads.append(pltpu.make_async_copy(owns[n], held[n], local.at[n * 5 + 4]))
        for m in range(4 if shared else 1):
            part = held[n].at[pl.ds(pl.multiple_of((t ^ masks("tp")[m]) * rows, rows), rows)] if shared else held[n]
            keeps.append(pltpu.make_async_copy(part, outs[n].at[m, c], local.at[n * 5 + m]))
    for n in range(arrays):
        for r in range(size):
            for side in range(2 if r else 1):
                spot = lax.rem((c + r if side else c + size - r), size)
                for h in range(pieces):
                    key = (n, r, side, h)
                    place = (n * size + r) * pieces + h
                    if r:
                        source = outs[n].at[0, spot, cuts[h]]
                    else:
                        source = owns[n].at[pl.ds(pl.multiple_of(t * rows + h * step, step) if shared else h * step, step)]
                    there = [outs[n].at[m, spot, cuts[h]] for m in range(4)]
                    count = arrays * size * pieces
                    if r < size - 1:
                        for way in (0, 1) if r == 0 else (side,):
                            z[key + (way,)] = remote(
                                source, there[0], z_sent, z_here, way * count + place, before if way else behind
                            )
                    near = (n * size + spot) * pieces + h
                    if shared and not r:
                        continue
                    x[key] = remote(source, there[1], x_sent, x_here, near, x_peer)
                    core[(0,) + key] = remote(source, there[2], core_sent, core_here, near, core_peer)
                    core[(1,) + key] = remote(there[1], there[3], core_sent, core_here, count + near, core_peer)
                    if r:
                        places[key] = remote(
                            source, there[0], z_sent, z_here, side * count + place - pieces, before if side else behind
                        )

    def go_on(way):
        return c > 0 if way else c < size - 1

    pieces_of = [(n, h) for n in range(arrays) for h in range(pieces)]
    for n, h in pieces_of:
        for way in range(2):

            @pl.when(go_on(way))
            def _():
                z[n, 0, 0, h, way].start()

    for load in loads:
        load.start()
    if not shared:
        for n, h in pieces_of:
            x[n, 0, 0, h].start()
            core[0, n, 0, 0, h].start()
    for load in loads:
        load.wait()
    for keep in keeps:
        keep.start()
    arrivals = [(n, r, side, h) for r in range(1, size) for n in range(arrays) for side in range(2) for h in range(pieces)]

    def there_is(key):
        return c + key[1] < size if key[2] else c >= key[1]

    for key in arrivals:

        @pl.when(there_is(key))
        def _():
            places[key].wait_recv()
            if key[1] < size - 1:

                @pl.when(go_on(key[2]))
                def _():
                    z[key + (key[2],)].start()

            x[key].start()
            core[(0,) + key].start()

    if not shared:
        for n, h in pieces_of:
            x[n, 0, 0, h].wait_recv()
            core[1, n, 0, 0, h].start()
    for key in arrivals:

        @pl.when(there_is(key))
        def _():
            x[key].wait_recv()
            core[(1,) + key].start()

    if not shared:
        for n, h in pieces_of:
            x[n, 0, 0, h].wait_send()
            core[0, n, 0, 0, h].wait()
            core[1, n, 0, 0, h].wait()
    for key in arrivals:

        @pl.when(there_is(key))
        def _():
            x[key].wait_send()
            core[(0,) + key].wait()
            core[(1,) + key].wait()
            if key[1] < size - 1:

                @pl.when(go_on(key[2]))
                def _():
                    z[key + (key[2],)].wait_send()

    for n, h in pieces_of:
        for way in range(2):

            @pl.when(go_on(way))
            def _():
                z[n, 0, 0, h, way].wait_send()

    for keep in keeps:
        keep.wait()


def gather_rows(values, collective, *earlier, shared=False):
    size, tps = lax.axis_size("ctx"), lax.axis_size("tp")
    assert tps == 4
    pieces, arrays = 2, len(values)
    rows = values[0].shape[0] // (tps if shared else 1)
    count = arrays * size * pieces
    anywhere = pl.BlockSpec(memory_space=pl.ANY)
    return pl.pallas_call(
        functools.partial(gather_kernel, size, pieces, arrays, shared, len(earlier)),
        out_shape=[jax.ShapeDtypeStruct((tps, size, rows, v.shape[1]), v.dtype) for v in values],
        in_specs=[anywhere] * (arrays + len(earlier)),
        out_specs=[anywhere] * arrays,
        scratch_shapes=[pltpu.VMEM(v.shape, v.dtype) for v in values]
        + [
            pltpu.SemaphoreType.DMA((n,))
            for n in (5 * arrays, 2 * count, 2 * count, count, count, 2 * count, 2 * count)
        ],
        compiler_params=pltpu.CompilerParams(collective_id=collective, has_side_effects=True),
        name="gather_rows",
        cost_estimate=COST,
    )(*values, *earlier)


def scatter_kernel(size, arrays, aheads, small, earlier, *refs):
    parts, swaps = refs[:arrays], refs[arrays : arrays + len(aheads)]
    given, refs = refs[arrays + len(aheads) :][:small], refs[arrays + len(aheads) + small + earlier :]
    outs, swapped, refs = refs[:arrays], refs[arrays : arrays + len(aheads)], refs[arrays + len(aheads) :]
    summed, refs = refs[:small], refs[small:]
    if small:
        (given,), (summed,), (near, pair, blocks, small_sent, small_here) = given, summed, refs[-5:]
        refs = refs[:-5]
    helds, core_ins, x_ins, z_ins = [refs[k * arrays : (k + 1) * arrays] for k in range(4)]
    local, z_sent, z_here, x_sent, x_here, core_sent, core_here, y_sent, y_here = refs[4 * arrays :]
    c, t, s = lax.axis_index("ctx"), lax.axis_index("tp"), lax.axis_index("shard")
    shards = lax.axis_size("shard")
    rings = [{"shard": lax.rem(s + r, shards)} for r in range(1, shards)] if aheads else []
    x_peer, core_peer = {"tp": t ^ 2}, {"tp": t ^ 1}
    first, last = c == 0, c == size - 1
    upper = c // (size // 2)
    spot = [size - 1 - k + upper * (2 * k - size + 1) for k in range(size)]
    before, behind = {"ctx": lax.max(c - 1, 0)}, {"ctx": lax.min(c + 1, size - 1)}
    line = ((jnp.logical_not(first), before), (jnp.logical_not(last), behind))
    around = [{"ctx": lax.rem(c + r, size)} for r in range(1, size)] if small else []
    greet([x_peer, core_peer] + rings + around, () if small else line)
    if small:
        small_core = remote(given, near.at[0], small_sent, small_here, 0, core_peer)
        small_x = remote(pair, near.at[1], small_sent, small_here, 1, x_peer)
        small_ctx = [
            remote(blocks.at[c], blocks.at[c], small_sent, small_here, 1 + r, around[r - 1]) for r in range(1, size)
        ]
        small_from = [
            remote(blocks.at[b], blocks.at[b], small_sent, small_here, 1 + r, around[r - 1])
            for r, b in [(r, lax.rem(c + size - r, size)) for r in range(1, size)]
        ]
        small_core.start()
    keeps, core, x, rising, falling, finals = [], {}, {}, {}, {}, {}
    y = [remote(swaps[k], swapped[k], y_sent, y_here, k, rings[ahead - 1]) for k, ahead in enumerate(aheads)]
    for n in range(arrays):
        part, held, core_in, x_in, z_in = parts[n], helds[n], core_ins[n], x_ins[n], z_ins[n]
        keeps.append(pltpu.make_async_copy(part.at[pl.ds(0, 2)], held, local.at[n]))
        for m in (1, 0):
            for k in range(size):
                core[n, m, k] = remote(
                    part.at[2 + m, spot[k]], core_in.at[m, k], core_sent, core_here, (n * 2 + m) * size + k, core_peer
                )
        for k in range(size):
            a = spot[k]
            x[n, k] = remote(held.at[1, a], x_in.at[k], x_sent, x_here, n * size + k, x_peer)
            rising[n, k] = remote(held.at[0, a], z_in.at[0, a], z_sent, z_here, 2 * n * size + a, behind)
            falling[n, k] = remote(held.at[0, a], z_in.at[1, a], z_sent, z_here, (2 * n + 1) * size + a, before)
        finals[n] = [
            remote(held.at[0, c], z_in.at[0, c], z_sent, z_here, 2 * n * size + c, behind),
            remote(held.at[0, c], z_in.at[1, c], z_sent, z_here, (2 * n + 1) * size + c, before),
        ]
    for copy in list(core.values()) + y:
        copy.start()
    for keep in keeps:
        keep.start()
    for keep in keeps:
        keep.wait()
    tall = 16

    def each(body):
        @pl.loop(0, outs[0].shape[0] // tall)
        def _(i):
            body(pl.ds(pl.multiple_of(i * tall, tall), tall))

    order = [(n, k) for n in range(arrays) for k in range(size)]
    for n, k in order:
        a, held, core_in = spot[k], helds[n], core_ins[n]
        core[n, 1, k].wait_recv()

        def add_core(rows):
            held[1, a, rows] = (held[1, a, rows].astype(F32) + core_in[1, k, rows].astype(F32)).astype(BF16)

        each(add_core)
        x[n, k].start()
    if small:
        small_core.wait_recv()
        pair[...] = given[...] + near[0]
        small_x.start()
    for n, k in order:
        a, held, core_in, x_in, z_in, out = spot[k], helds[n], core_ins[n], x_ins[n], z_ins[n], outs[n]
        core[n, 0, k].wait_recv()
        x[n, k].wait_recv()

        def total(rows):
            return held[0, a, rows].astype(F32) + core_in[0, k, rows].astype(F32) + x_in[k, rows].astype(F32)

        def add(rows):
            held[0, a, rows] = total(rows).astype(BF16)

        def add_rising(rows):
            held[0, a, rows] = (total(rows) + z_in[0, a, rows].astype(F32)).astype(BF16)

        def add_falling(rows):
            held[0, a, rows] = (total(rows) + z_in[1, a, rows].astype(F32)).astype(BF16)

        def keep_total(rows):
            out[rows] = total(rows)

        @pl.when(a == c)
        def _():
            each(keep_total)

        @pl.when(a > c)
        def _():
            @pl.when(first)
            def _():
                each(add)

            @pl.when(jnp.logical_not(first))
            def _():
                rising[n, k].wait_recv()
                each(add_rising)

            rising[n, k].start()

        @pl.when(a < c)
        def _():
            @pl.when(last)
            def _():
                each(add)

            @pl.when(jnp.logical_not(last))
            def _():
                falling[n, k].wait_recv()
                each(add_falling)

            falling[n, k].start()

    if small:
        small_x.wait_recv()
        blocks[c] = pair[...] + near[1]
        for copy in small_ctx:
            copy.start()
    for n in range(arrays):
        for side, edge in enumerate((first, last)):
            z_in, out = z_ins[n], outs[n]

            @pl.when(jnp.logical_not(edge))
            def _():
                finals[n][side].wait_recv()

                def add_side(rows):
                    out[rows] = out[rows] + z_in[side, c, rows].astype(F32)

                each(add_side)

    for copy in y:
        copy.wait()
    if small:
        for copy in small_from:
            copy.wait_recv()
        summed[...] = sum(blocks[b] for b in range(1, size)) + blocks[0]
        for copy in [small_core, small_x] + small_ctx:
            copy.wait_send()
    for copy in list(core.values()) + list(x.values()):
        copy.wait_send()
    for n, k in order:

        @pl.when(spot[k] > c)
        def _():
            rising[n, k].wait_send()

        @pl.when(spot[k] < c)
        def _():
            falling[n, k].wait_send()


def scatter_rows(parts, collective, swaps, *earlier, small=None):
    size, arrays = lax.axis_size("ctx"), len(parts)
    rows, width = parts[0].shape[2:]
    moved = [v for v, _ in swaps]
    smalls = [] if small is None else [small]
    anywhere, held = pl.BlockSpec(memory_space=pl.ANY), pl.BlockSpec(memory_space=pltpu.VMEM)
    found = pl.pallas_call(
        functools.partial(
            scatter_kernel, size, arrays, tuple(ahead for _, ahead in swaps), len(smalls), len(earlier)
        ),
        out_shape=[jax.ShapeDtypeStruct((rows, width), F32)] * arrays
        + [jax.ShapeDtypeStruct(v.shape, v.dtype) for v in moved + smalls],
        in_specs=[anywhere] * (arrays + len(moved)) + [held] * len(smalls) + [anywhere] * len(earlier),
        out_specs=[held] * arrays + [anywhere] * len(moved) + [held] * len(smalls),
        scratch_shapes=[pltpu.VMEM((2, size, rows, width), BF16)] * (2 * arrays)
        + [pltpu.VMEM((size, rows, width), BF16)] * arrays
        + [pltpu.VMEM((2, size, rows, width), BF16)] * arrays
        + [
            pltpu.SemaphoreType.DMA((arrays * n,))
            for n in (1, 2 * size, 2 * size, size, size, 2 * size, 2 * size)
        ]
        + [pltpu.SemaphoreType.DMA((max(len(moved), 1),))] * 2
        + [pltpu.VMEM((n,) + v.shape, F32) if n else pltpu.VMEM(v.shape, F32) for v in smalls for n in (2, 0, size)]
        + [pltpu.SemaphoreType.DMA((1 + size,))] * (2 * len(smalls)),
        compiler_params=pltpu.CompilerParams(
            collective_id=collective, has_side_effects=True, vmem_limit_bytes=48 * 1024 * 1024
        ),
        name="scatter_rows",
        cost_estimate=COST,
    )(*parts, *moved, *smalls, *earlier)
    return found[:arrays], found[arrays:]


def own_block(values, ahead=0, axis=0):
    size = lax.axis_size("shard")
    block = values.shape[axis] // size
    spot = lax.rem(lax.axis_index("shard") + ahead, size)
    return lax.dynamic_slice_in_dim(values, spot * block, block, axis=axis)


def sum_shard(values, axis):
    size = lax.axis_size("shard")
    total = own_block(values, 0, axis)
    for r in range(1, size):
        total = total + receive(own_block(values, r, axis), "shard", size - r)
    return total


def product_parts(pairs):
    own = jnp.concatenate([dot(lefts[0], right, (0, 0)) for lefts, right in pairs], axis=1)
    others = tuple(
        jnp.concatenate([dot(lefts[r], right, (0, 0), BF16) for lefts, right in pairs], axis=1)
        for r in range(1, lax.axis_size("shard"))
    )
    return own, others


def product_swaps(others):
    return [(part, r) for r, part in enumerate(others, 1)]


def product_add(own, arrived):
    return own + sum(part.astype(F32) for part in arrived)


def product_sum(own, others):
    size = lax.axis_size("shard")
    for r in range(1, size):
        own = own + receive(others[r - 1], "shard", size - r).astype(F32)
    return own


def ahead_first(values, start, axis=0):
    return lax.dynamic_slice_in_dim(
        jnp.concatenate([values, values], axis=axis), start, values.shape[axis], axis=axis
    )


def gather_natural(values, axis_name, axis=0):
    return lax.all_gather(values, axis_name, axis=axis, tiled=True)


def gather_small(values, axis):
    size = lax.axis_size("shard")
    whole = jnp.concatenate([values] + [receive(values, "shard", r) for r in range(1, size)], axis=axis)
    return ahead_first(whole, lax.rem(size - lax.axis_index("shard"), size) * values.shape[axis], axis)


def corner(values):
    return values[(0,) * values.ndim]


def start_after(values):
    first = corner(values)
    return (first != first).astype(jnp.int32)


def tie(values, earlier):
    return values + (corner(earlier).astype(F32) * 0.0).astype(values.dtype)


def part_order(values):
    t = lax.axis_index("tp")
    return jnp.concatenate([lax.dynamic_index_in_dim(values, t ^ m, 1, False)[None] for m in masks("tp")], axis=0)


def natural_rows(values):
    t, order = lax.axis_index("tp"), masks("tp")
    part = values.shape[0] // len(order)
    found = []
    for q in range(len(order)):
        m, place = q ^ t, 0
        for i, bit in enumerate(reversed(bits("tp"))):
            place = place + jnp.where(m & bit, 1 << i, 0)
        found.append(lax.dynamic_slice_in_dim(values, place * part, part))
    return jnp.concatenate(found, axis=0)


def inverse_scale(values):
    return lax.rsqrt(jnp.mean(values * values, axis=-1, keepdims=True) + NORM_EPSILON)


def norm_back(grad, values, gain):
    scale = inverse_scale(values)
    weighted = grad * gain
    middle = jnp.mean(values * weighted, axis=-1, keepdims=True)
    return scale * weighted - values * (scale * scale * scale) * middle, grad * values * scale


def weights_kernel(ctxs, group, pieces, index, inward, outward, entry, *refs):
    exits, (first, others, head, leave) = refs[:ctxs], refs[ctxs:]
    c = index[0]
    tall = first.shape[0]
    deep = 16
    in_rows, out_rows = inward.shape[1], outward.shape[1]
    out_experts = 8
    half = lax.rem(c, out_experts // group) * group

    def picker(rows, kept, place):
        count = kept * deep
        to = lax.broadcasted_iota(jnp.int32, (count, rows * deep), 0)
        source = lax.broadcasted_iota(jnp.int32, (count, rows * deep), 1)
        return (source == to % deep * rows + place(to // deep)).astype(BF16)

    in_pick = picker(in_rows, in_rows, lambda row: row)
    kept = group * pieces
    out_pick = picker(out_rows, kept, lambda row: row // group * out_experts + half + row % group)

    def put(i, column, rows, value):
        if i:
            column = column + (i - 1) * 3 * pieces * 128
        (others if i else first)[rows, column : column + 128] = value

    def two(ref, step, rows):
        parts = [ref[slice((step + n) * deep, (step + n + 1) * deep)].reshape(deep * rows, 128) for n in range(2)]
        return jnp.concatenate(parts, axis=1)

    for step in range(0, tall // deep, 2):
        moved_in = matmul(in_pick, two(inward, step, in_rows)).astype(BF16)
        moved_out = matmul(out_pick, two(outward, step, out_rows)).astype(BF16)
        for n in range(2):
            rows, lanes = slice((step + n) * deep, (step + n + 1) * deep), slice(n * 128, (n + 1) * 128)
            for row in range(in_rows):
                i, piece, side = row // (2 * pieces), row // 2 % pieces, row % 2
                put(i, (side * pieces + piece) * 128, rows, moved_in[row * deep : (row + 1) * deep, lanes])
            for row in range(kept):
                i, piece = row % group, row // group
                put(i, (2 * pieces + piece) * 128, rows, moved_out[row * deep : (row + 1) * deep, lanes])
    for k in range(3):
        head[:, k * HEAD_DIM : (k + 1) * HEAD_DIM] = entry[k]
    for j in range(ctxs):
        leave[:, j * HEAD_DIM : (j + 1) * HEAD_DIM] = exits[j][...]


def own_weights(expert_in, expert_out, attention_in, attention_out):
    c, ctxs = lax.axis_index("ctx"), lax.axis_size("ctx")
    rows, experts, _, hidden = expert_in.shape
    group, pieces = experts // ctxs, hidden // 128
    assert group in (1, 2, 4, 8) and group * 2 * pieces % 16 == 0 and 8 * pieces % 16 == 0
    inward = expert_in.reshape(rows, experts, 2, pieces, 128).transpose(0, 1, 3, 2, 4).reshape(rows, -1, 128)
    outward = expert_out.reshape(rows, experts // 8, 8, pieces, 128).transpose(0, 1, 3, 2, 4).reshape(rows, -1, 128)
    entry = attention_in.transpose(1, 0, 2)
    tall = 64
    wide = 3 * hidden
    grid_spec = pltpu.PrefetchScalarGridSpec(
        num_scalar_prefetch=1,
        grid=(rows // tall,),
        in_specs=[
            pl.BlockSpec((tall, group * 2 * pieces, 128), lambda b, c: (b, c[0], 0)),
            pl.BlockSpec((tall, 8 * pieces, 128), lambda b, c: (b, c[0] * group // 8, 0)),
            pl.BlockSpec((3, tall, HEAD_DIM), lambda b, c: (0, b, c[0])),
        ]
        + [
            pl.BlockSpec((tall, HEAD_DIM), functools.partial(lambda j, b, c: (b, lax.rem(c[0] + j, ctxs)), j))
            for j in range(ctxs)
        ],
        out_specs=[
            pl.BlockSpec((tall, n), lambda b, c: (b, 0))
            for n in (wide, (group - 1) * wide, 3 * HEAD_DIM, ctxs * HEAD_DIM)
        ],
    )
    return pl.pallas_call(
        functools.partial(weights_kernel, ctxs, group, pieces),
        grid_spec=grid_spec,
        out_shape=[
            jax.ShapeDtypeStruct((rows, n), BF16)
            for n in (wide, (group - 1) * wide, 3 * HEAD_DIM, ctxs * HEAD_DIM)
        ],
        compiler_params=pltpu.CompilerParams(vmem_limit_bytes=48 * 1024 * 1024),
        name="own_weights",
        cost_estimate=COST,
    )(c.astype(jnp.int32)[None], inward, outward, entry, *([attention_out] * ctxs))


def matmul(left, right, over=(1, 0)):
    return lax.dot_general(left, right, (((over[0],), (over[1],)), ((), ())), preferred_element_type=F32)


def head_norm(values):
    return lax.rsqrt(jnp.mean(values * values, axis=-1, keepdims=True) + NORM_EPSILON)


def turned(values, cosine, sine):
    return values * cosine + pltpu.roll(values, values.shape[-1] // 2, 1) * sine


def shared_weights_kernel(ctxs, group, pieces, index, *refs):
    others = ctxs - 1
    inwards, outwards, outs = refs[:others], refs[others : 2 * others], refs[-others:]
    deep, hidden = 16, pieces * 128
    kinds, out_kinds = group * 2 * pieces, 8 * pieces

    def picker(rows, kept, place):
        to = lax.broadcasted_iota(jnp.int32, (kept * deep, rows * deep), 0)
        source = lax.broadcasted_iota(jnp.int32, (kept * deep, rows * deep), 1)
        return (source == to % deep * rows + place(to // deep)).astype(BF16)

    in_pick = picker(kinds, 2 * pieces, lambda r: (group - 1) * 2 * pieces + r)

    def two(ref, step, rows):
        parts = [ref[(step + n) * deep : (step + n + 1) * deep].reshape(deep * rows, 128) for n in range(2)]
        return jnp.concatenate(parts, axis=1)

    for k in range(others):
        inward, outward, out = inwards[k], outwards[k], outs[k]
        at = lax.rem(lax.rem(index[0] + k + 1, ctxs), 8 // group) * group + group - 1
        out_pick = picker(out_kinds, pieces, lambda r: r * 8 + at)

        def put(moved, step, r, column):
            for n in range(2):
                rows = slice((step + n) * deep, (step + n + 1) * deep)
                out[rows, column : column + 128] = moved[r * deep : (r + 1) * deep, n * 128 : (n + 1) * 128]

        for step in range(0, out.shape[0] // deep, 2):
            moved = matmul(in_pick, two(inward, step, kinds)).astype(BF16)
            for r in range(2 * pieces):
                put(moved, step, r, (r % 2 * pieces + r // 2) * 128)
            moved = matmul(out_pick, two(outward, step, out_kinds)).astype(BF16)
            for r in range(pieces):
                put(moved, step, r, (2 * pieces + r) * 128)


def shared_weights(expert_in, expert_out, *earlier):
    ctxs = lax.axis_size("ctx")
    rows, experts, _, hidden = expert_in.shape
    group, pieces = experts // ctxs, hidden // 128
    inward = expert_in.reshape(rows, experts, 2, pieces, 128).transpose(0, 1, 3, 2, 4).reshape(rows, -1, 128)
    outward = expert_out.reshape(rows, experts // 8, 8, pieces, 128).transpose(0, 1, 3, 2, 4).reshape(rows, -1, 128)
    tall, others = 64, ctxs - 1
    after = lambda k, c: lax.rem(c[0] + k + 1, ctxs)
    return pl.pallas_call(
        functools.partial(shared_weights_kernel, ctxs, group, pieces),
        grid_spec=pltpu.PrefetchScalarGridSpec(
            num_scalar_prefetch=1,
            grid=(rows // tall,),
            in_specs=[
                pl.BlockSpec(
                    (tall, group * 2 * pieces, 128), functools.partial(lambda k, b, c: (b, after(k, c), 0), k)
                )
                for k in range(others)
            ]
            + [
                pl.BlockSpec(
                    (tall, 8 * pieces, 128), functools.partial(lambda k, b, c: (b, after(k, c) * group // 8, 0), k)
                )
                for k in range(others)
            ]
            + [pl.BlockSpec(memory_space=pl.ANY)] * len(earlier),
            out_specs=[pl.BlockSpec((tall, 3 * hidden), lambda b, c: (b, 0))] * others,
        ),
        out_shape=[jax.ShapeDtypeStruct((rows, 3 * hidden), BF16)] * others,
        compiler_params=pltpu.CompilerParams(vmem_limit_bytes=48 * 1024 * 1024),
        name="shared_weights",
        cost_estimate=COST,
    )(lax.axis_index("ctx").astype(jnp.int32)[None], *([inward] * others), *([outward] * others), *earlier)


def project_kernel(tokens, gain, weight, gains, cosine, sine, normed, raw, query, key, value):
    values = tokens[...].astype(F32)
    low = (values * head_norm(values) * gain[...]).astype(BF16)
    normed[...] = low
    projected = matmul(low, weight[...])
    raw[...] = projected[:, : 2 * HEAD_DIM]
    for k, out in enumerate((query, key)):
        part = projected[:, k * HEAD_DIM : (k + 1) * HEAD_DIM]
        part = part * head_norm(part) * gains[k : k + 1, :]
        out[...] = turned(part, cosine[...], sine[...]).astype(BF16)
    value[...] = projected[:, 2 * HEAD_DIM :].astype(BF16)


def project(tokens, gain, weight, gains, cosine, sine):
    rows, width = tokens.shape
    tall = 256
    block = lambda n: pl.BlockSpec((tall, n), lambda b: (b, 0))
    whole = lambda v: pl.BlockSpec(v.shape, lambda b: (0, 0))
    head = jax.ShapeDtypeStruct((rows, HEAD_DIM), BF16)
    return pl.pallas_call(
        project_kernel,
        grid=(rows // tall,),
        in_specs=[block(width), whole(gain), whole(weight), whole(gains), block(HEAD_DIM), block(HEAD_DIM)],
        out_specs=[block(width), block(2 * HEAD_DIM)] + [block(HEAD_DIM)] * 3,
        out_shape=[
            jax.ShapeDtypeStruct((rows, width), BF16),
            jax.ShapeDtypeStruct((rows, 2 * HEAD_DIM), F32),
            head,
            head,
            head,
        ],
        compiler_params=pltpu.CompilerParams(vmem_limit_bytes=48 * 1024 * 1024),
        name="project",
        cost_estimate=COST,
    )(tokens, gain, weight, gains, cosine, sine)


def chances_of(query, key, row_doc, column_doc):
    scores = matmul(query, key, (1, 1)) * (HEAD_DIM**-0.5)
    scores = jnp.where(row_doc == column_doc, scores, MASKED)
    grown = jnp.exp(scores - jnp.max(scores, axis=-1, keepdims=True))
    return grown / jnp.sum(grown, axis=-1, keepdims=True)


def attend_kernel(query, key, value, row_doc, column_doc, mixed):
    chances = chances_of(query[...], key[...], row_doc[...], column_doc[...])
    mixed[...] = matmul(chances.astype(BF16), value[...]).astype(BF16)


def attend(query, key, value, row_doc, column_doc):
    rows = query.shape[0]
    tall = 256
    block = pl.BlockSpec((tall, HEAD_DIM), lambda b: (b, 0))
    whole = pl.BlockSpec((rows, HEAD_DIM), lambda b: (0, 0))
    return pl.pallas_call(
        attend_kernel,
        grid=(rows // tall,),
        in_specs=[
            block,
            whole,
            whole,
            pl.BlockSpec((tall, 1), lambda b: (b, 0)),
            pl.BlockSpec((1, rows), lambda b: (0, 0)),
        ],
        out_specs=block,
        out_shape=jax.ShapeDtypeStruct((rows, HEAD_DIM), BF16),
        compiler_params=pltpu.CompilerParams(vmem_limit_bytes=48 * 1024 * 1024),
        name="attend",
        cost_estimate=COST,
    )(query, key, value, row_doc, column_doc)


def attend_back_kernel(
    tall, query, key, value, raw, cosine, sine, gains, row_doc, column_doc, mixed_grad, *refs
):
    grad, gain_grad, key_grad, value_grad = refs[-4:]
    step = pl.program_id(0)
    rows = pl.ds(pl.multiple_of(step * tall, tall), tall)

    def projected_back(turned_grad, k, where):
        values = raw[where, k * HEAD_DIM : (k + 1) * HEAD_DIM]
        grown = turned(turned_grad, cosine[where], -sine[where])
        scale = head_norm(values)
        weighted = grown * gains[k : k + 1, :]
        middle = jnp.mean(values * weighted, axis=-1, keepdims=True)
        part = jnp.sum(grown * values * scale, axis=0, keepdims=True)
        return scale * weighted - values * (scale * scale * scale) * middle, part

    @pl.when(step == 0)
    def _():
        key_grad[...] = jnp.zeros_like(key_grad)
        value_grad[...] = jnp.zeros_like(value_grad)
        gain_grad[...] = jnp.zeros_like(gain_grad)

    here = query[...]
    chances = chances_of(here, key[...], row_doc[...], column_doc[...])
    upstream = mixed_grad[...]
    weight_grad = matmul(upstream, value[...], (1, 1))
    score_grad = chances * (weight_grad - jnp.sum(chances * weight_grad, axis=-1, keepdims=True))
    score_grad = score_grad.astype(BF16)
    scale = HEAD_DIM**-0.5
    query_grad, part = projected_back(matmul(score_grad, key[...]) * scale, 0, rows)
    grad[rows, :HEAD_DIM] = query_grad.astype(BF16)
    gain_grad[0:1, :] += part
    key_grad[...] += matmul(score_grad, here, (0, 0)) * scale
    value_grad[...] += matmul(chances.astype(BF16), upstream, (0, 0))

    @pl.when(step == pl.num_programs(0) - 1)
    def _():
        back, part = projected_back(key_grad[...], 1, slice(None))
        grad[:, HEAD_DIM : 2 * HEAD_DIM] = back.astype(BF16)
        gain_grad[1:2, :] += part
        grad[:, 2 * HEAD_DIM :] = value_grad[...].astype(BF16)


def attend_back(query, key, value, raw, cosine, sine, gains, row_doc, column_doc, mixed_grad, *earlier):
    rows = query.shape[0]
    tall = 256
    block = pl.BlockSpec((tall, HEAD_DIM), lambda b: (b, 0))
    whole = lambda v: pl.BlockSpec(v.shape, lambda b: (0, 0))
    return pl.pallas_call(
        functools.partial(attend_back_kernel, tall),
        grid=(rows // tall,),
        in_specs=[
            block,
            whole(key),
            whole(value),
            whole(raw),
            whole(cosine),
            whole(sine),
            whole(gains),
            pl.BlockSpec((tall, 1), lambda b: (b, 0)),
            whole(column_doc),
            block,
        ]
        + [pl.BlockSpec(memory_space=pl.ANY)] * len(earlier),
        out_specs=[
            pl.BlockSpec((rows, 3 * HEAD_DIM), lambda b: (0, 0)),
            pl.BlockSpec((8, HEAD_DIM), lambda b: (0, 0)),
        ],
        out_shape=[
            jax.ShapeDtypeStruct((rows, 3 * HEAD_DIM), BF16),
            jax.ShapeDtypeStruct((8, HEAD_DIM), F32),
        ],
        scratch_shapes=[pltpu.VMEM((rows, HEAD_DIM), F32)] * 2,
        compiler_params=pltpu.CompilerParams(vmem_limit_bytes=48 * 1024 * 1024),
        name="attend_back",
        cost_estimate=COST,
    )(query, key, value, raw, cosine, sine, gains, row_doc, column_doc, mixed_grad, *earlier)


def expert_step_kernel(index, count, earlier, shard, rows, upstream, *refs):
    gate_in, up_in, outward = [refs[k * count : (k + 1) * count] for k in range(3)]
    gates, lanes, scaled, inner_grad, gate_part = refs[3 * count], refs[3 * count + 1], *refs[3 * count + 2 + earlier :]
    hidden_size = outward[0].shape[1]
    deep = outward[0].shape[0]

    def product(left, parts):
        total = 0.0
        for r, part in enumerate(parts):
            start = pl.multiple_of(lax.rem(shard[0] + r, count) * deep, deep) if count > 1 else 0
            total = total + matmul(left[:, pl.ds(start, deep)], part[...])
        return total

    gate, up, back = product(rows, gate_in), product(rows, up_in), product(upstream, outward)
    sigmoid = 1.0 / (1.0 + jnp.exp(-gate))
    silu = gate * sigmoid
    hidden = (silu * up).astype(BF16).astype(F32)
    weight = gates[:, index : index + 1]
    scaled[...] = (hidden * weight).astype(BF16)
    gate_part[...] = jnp.sum(hidden * back, axis=1, keepdims=True) * lanes[index : index + 1, :]
    hidden_grad = back * weight
    inner_grad[:, :hidden_size] = (hidden_grad * up * sigmoid * (1.0 + gate * (1.0 - sigmoid))).astype(BF16)
    inner_grad[:, hidden_size:] = (hidden_grad * silu).astype(BF16)


def expert_step(index, place, rows, upstream, weights, hidden_size, gates, lanes, *earlier):
    count, width = rows.shape
    tall, parts = 256, len(weights)
    block = lambda n: pl.BlockSpec((tall, n), lambda b, s: (b, 0))
    whole = weights[0].shape[0] == width

    def column(k, r, b, s):
        return (lax.rem(s[0] + r, parts) if whole else 0, 3 * place + k)

    columns = [
        pl.BlockSpec((width // parts, hidden_size), functools.partial(column, k, r))
        for k in range(3)
        for r in range(parts)
    ]
    return pl.pallas_call(
        functools.partial(expert_step_kernel, index, parts, len(earlier)),
        grid_spec=pltpu.PrefetchScalarGridSpec(
            num_scalar_prefetch=1,
            grid=(count // tall,),
            in_specs=[block(width), block(width)]
            + columns
            + [block(gates.shape[1]), pl.BlockSpec(lanes.shape, lambda b, s: (0, 0))]
            + [pl.BlockSpec(memory_space=pl.ANY)] * len(earlier),
            out_specs=[block(hidden_size), block(2 * hidden_size), block(128)],
        ),
        out_shape=[
            jax.ShapeDtypeStruct((count, hidden_size), BF16),
            jax.ShapeDtypeStruct((count, 2 * hidden_size), BF16),
            jax.ShapeDtypeStruct((count, 128), F32),
        ],
        compiler_params=pltpu.CompilerParams(vmem_limit_bytes=48 * 1024 * 1024),
        name="expert_step",
        cost_estimate=COST,
    )(lax.axis_index("shard").astype(jnp.int32)[None], rows, upstream, *(list(weights) * 3), gates, lanes, *earlier)


def combine_kernel(count, extras, *refs):
    lefts, rights, lanes, out = refs[:count], refs[count : 2 * count], refs[2 * count : 2 * count + extras], refs[-1]
    width = rights[0].shape[0]
    total = matmul(lefts[0][...], rights[0][...], (1, 1))
    for left, right in zip(lefts[1:], rights[1:]):
        total = total + matmul(left[...], right[...], (1, 1))
    out[:, :width] = total.astype(BF16)
    if extras:
        out[:, width:] = sum(lane[...] for lane in lanes).astype(BF16)


def combine(lefts, rights, lanes, *earlier):
    (rows, _), (width, _) = lefts[0][0].shape, rights[0][0].shape
    tall, deep = 256, 256
    total = width + (lanes[0].shape[1] if lanes else 0)
    return pl.pallas_call(
        lambda *refs: combine_kernel(len(lefts), len(lanes), *refs[: len(refs) - 1 - len(earlier)], refs[-1]),
        grid=(rows // tall,),
        in_specs=[pl.BlockSpec((tall, deep), functools.partial(lambda k, b: (b, k), k)) for _, k in lefts]
        + [
            pl.BlockSpec((width, deep), functools.partial(lambda k, b: (0, k), k), pipeline_mode=pl.Buffered(1))
            for _, k in rights
        ]
        + [pl.BlockSpec((tall, lane.shape[1]), lambda b: (b, 0)) for lane in lanes]
        + [pl.BlockSpec(memory_space=pl.ANY)] * len(earlier),
        out_specs=pl.BlockSpec((tall, total), lambda b: (b, 0)),
        out_shape=jax.ShapeDtypeStruct((rows, total), BF16),
        compiler_params=pltpu.CompilerParams(vmem_limit_bytes=56 * 1024 * 1024),
        name="combine",
        cost_estimate=COST,
    )(*[v for v, _ in lefts], *[v for v, _ in rights], *lanes, *earlier)


def gradient_kernel(steps, index, rows, upstream, inner_grad, scaled, own, others):
    step = pl.program_id(0)
    wide = inner_grad.shape[1]

    def put(out):
        out[:, :wide] = matmul(rows[...], inner_grad[...], (0, 0)).astype(out.dtype)
        out[:, wide:] = matmul(upstream[...], scaled[...], (0, 0)).astype(out.dtype)

    @pl.when(step < steps)
    def _():
        put(own)

    @pl.when(step >= steps)
    def _():
        put(others)


def gradient_parts(rows, upstream, inner_grad, scaled):
    s, shards = lax.axis_index("shard"), lax.axis_size("shard")
    count, width = rows.shape
    deep = 256
    steps = width // shards // deep
    wide = inner_grad.shape[1] + scaled.shape[1]
    feature = pl.BlockSpec((count, deep), lambda b, s: (0, lax.rem(s[0] * steps + b, steps * shards)))
    whole = lambda v: pl.BlockSpec(v.shape, lambda b, s: (0, 0))
    return pl.pallas_call(
        functools.partial(gradient_kernel, steps),
        grid_spec=pltpu.PrefetchScalarGridSpec(
            num_scalar_prefetch=1,
            grid=(steps * shards,),
            in_specs=[feature, feature, whole(inner_grad), whole(scaled)],
            out_specs=[
                pl.BlockSpec((deep, wide), lambda b, s: (lax.min(b, steps - 1), 0)),
                pl.BlockSpec((deep, wide), lambda b, s: (lax.max(b - steps, 0), 0)),
            ],
        ),
        out_shape=[
            jax.ShapeDtypeStruct((steps * deep, wide), F32),
            jax.ShapeDtypeStruct((steps * deep * (shards - 1), wide), BF16),
        ],
        compiler_params=pltpu.CompilerParams(vmem_limit_bytes=48 * 1024 * 1024),
        name="gradient_parts",
        cost_estimate=COST,
    )(s.astype(jnp.int32)[None], rows, upstream, inner_grad, scaled)


def attention_kernel(chunk, entry, exit_out):
    ctxs, _, width = chunk.shape
    head = width // 4
    for j in range(ctxs):
        for k in range(3):
            entry[k, :, j * head : (j + 1) * head] = chunk[j, :, k * head : (k + 1) * head].astype(F32)
        exit_out[:, j * head : (j + 1) * head] = chunk[j, :, 3 * head :].astype(F32)


def expert_kernel(group, ctxs, tall, hidden, index, *refs):
    gathered, shared = refs[: group - 1], refs[group - 1 : group - 1 + ctxs]
    chunk, up, down, entry, exit_out = refs[group - 1 + ctxs :]
    attention_kernel(chunk, entry, exit_out)
    pieces = hidden // 128
    experts = group * ctxs
    deep = 16
    to = lax.broadcasted_iota(jnp.int32, (deep * deep, deep * deep), 0)
    source = lax.broadcasted_iota(jnp.int32, (deep * deep, deep * deep), 1)
    turn = (source == to % deep * deep + to // deep).astype(BF16)

    def tile(e, column, start):
        rows, columns = slice(start, start + deep), slice(column, column + 128)
        if e % group == group - 1:
            return shared[e // group][0, rows, columns]
        return gathered[e % group][e // group, rows, columns]

    def place(out, kinds, start):
        blocks = [jnp.concatenate([tile(e, column, start) for e, column in kinds[k : k + deep]], axis=0) for k in range(0, len(kinds), deep)]
        for k in range(0, len(blocks), 2):
            pair = blocks[k : k + 2]
            moved = matmul(turn, jnp.concatenate(pair, axis=1))
            for n in range(len(pair)):
                for d in range(deep):
                    row = (start + d) * len(kinds) + (k + n) * deep
                    out[row : row + deep, :] = moved[d * deep : (d + 1) * deep, n * 128 : (n + 1) * 128]

    ups = [(e, (side * pieces + piece) * 128) for e in range(experts) for piece in range(pieces) for side in range(2)]
    downs = [
        (part * 8 + e, (2 * pieces + piece) * 128)
        for part in range(experts // 8)
        for piece in range(pieces)
        for e in range(8)
    ]
    for start in range(0, tall, deep):
        place(up, ups, start)
        place(down, downs, start)


def weight_gradients(gathered, shared, chunk):
    (ctxs, rows, width), group = shared.shape, len(gathered) + 1
    hidden, experts = width // 3, group * ctxs
    pieces = hidden // 128
    assert experts % 8 == 0 and hidden % 128 == 0
    tall = 64
    wide = ctxs * chunk.shape[2] // 4
    up, down, entry, exit_out = pl.pallas_call(
        functools.partial(expert_kernel, group, ctxs, tall, hidden),
        grid_spec=pltpu.PrefetchScalarGridSpec(
            num_scalar_prefetch=1,
            grid=(rows // tall,),
            in_specs=[pl.BlockSpec((ctxs, tall, width), lambda b, c: (0, b, 0))] * len(gathered)
            + [
                pl.BlockSpec(
                    (1, tall, width), functools.partial(lambda j, b, c: (lax.rem(ctxs + j - c[0], ctxs), b, 0), j)
                )
                for j in range(ctxs)
            ]
            + [pl.BlockSpec((ctxs, tall, chunk.shape[2]), lambda b, c: (0, b, 0))],
            out_specs=[pl.BlockSpec((tall * experts * pieces * k, 128), lambda b, c: (b, 0)) for k in (2, 1)]
            + [
                pl.BlockSpec((3, tall, wide), lambda b, c: (0, b, 0)),
                pl.BlockSpec((tall, wide), lambda b, c: (b, 0)),
            ],
        ),
        out_shape=[jax.ShapeDtypeStruct((rows * experts * pieces * k, 128), F32) for k in (2, 1)]
        + [jax.ShapeDtypeStruct((3, rows, wide), F32), jax.ShapeDtypeStruct((rows, wide), F32)],
        compiler_params=pltpu.CompilerParams(vmem_limit_bytes=48 * 1024 * 1024),
        name="weight_gradients",
        cost_estimate=COST,
    )(lax.axis_index("ctx").astype(jnp.int32)[None], *gathered, *([shared] * ctxs), chunk)
    up = up.reshape(rows, experts, pieces, 2, 128).transpose(0, 1, 3, 2, 4).reshape(rows, experts, 2, hidden)
    down = down.reshape(rows, experts // 8, pieces, 8, 128).transpose(0, 1, 3, 2, 4).reshape(rows, experts, hidden)
    return up, down, entry.transpose(1, 0, 2), exit_out


def local(
    tokens,
    segments,
    routes,
    cotangent,
    first_gain,
    head_gain,
    attention_in,
    attention_out,
    second_gain,
    router_weight,
    expert_in,
    expert_out,
):
    s, c, t = lax.axis_index("shard"), lax.axis_index("ctx"), lax.axis_index("tp")
    shards, ctxs, tps = lax.axis_size("shard"), lax.axis_size("ctx"), lax.axis_size("tp")
    rows, width = tokens.shape[1:]
    own = rows // tps
    block = width // shards
    every = rows * ctxs
    experts = router_weight.shape[1]
    hidden_size = expert_out.shape[2]
    local_width = attention_out.shape[1]
    head_size = local_width // ctxs

    group = experts // ctxs
    base = c * group

    gains = gather_small(jnp.stack([first_gain, second_gain]), 1).astype(F32)
    gain_one, gain_two = gains[0], gains[1]
    head_gains = gather_small(head_gain[None], 1)[0].astype(F32)
    first_weights, others, head_in, exit_weight = own_weights(expert_in, expert_out, attention_in, attention_out)
    tokens_all, cot_all = gather_rows([tokens[0], cotangent[0]], 3, head_in, shared=True)
    tokens_all, cot_all = tokens_all.reshape(every, width), cot_all.reshape(every, width)
    head_in = gather_natural(head_in, "shard")
    first_weights, others = gather_natural(first_weights, "shard"), gather_natural(others, "shard")
    exit_weights = [exit_weight] + [receive(exit_weight, "shard", r) for r in range(1, shards)]
    first = t * own
    tokens_own = lax.dynamic_slice_in_dim(tokens[0], first, own)
    cot_own = lax.dynamic_slice_in_dim(cotangent[0], first, own)

    layer_in = tokens_own.astype(F32)
    upstream = cot_own.astype(F32)
    choices_all = gather_ctx(routes[0]).reshape(ctxs, tps, own, -1)
    picks_all = jnp.any(part_order(choices_all)[..., None] == jnp.arange(experts), axis=3)
    picks = lax.dynamic_index_in_dim(picks_all[0], c, 0, False)
    picks_all = picks_all.reshape(every, experts)
    router = gather_small(router_weight, 0)

    assert head_size == HEAD_DIM
    spot = part_order(jnp.arange(every, dtype=jnp.int32).reshape(ctxs, tps, own)).reshape(-1)
    documents = part_order(segments[0].reshape(ctxs, tps, own)).reshape(-1)
    row_doc, column_doc = documents[:, None], documents[None, :]
    steps = jnp.arange(HEAD_DIM // 2).astype(F32)
    frequency = ROTARY_BASE ** (-2.0 * steps / HEAD_DIM)
    angles = spot.astype(F32)[:, None] * frequency[None, :]
    cosine, sine = jnp.cos(angles), jnp.sin(angles)
    cosine, sine = jnp.concatenate([cosine, cosine], axis=1), jnp.concatenate([-sine, sine], axis=1)
    head_gains = head_gains.reshape(2, HEAD_DIM)
    normed_one_all, raw, queries, keys, values = project(
        tokens_all, gain_one[None], head_in, head_gains, cosine, sine
    )
    mixed_head = attend(queries, keys, values, row_doc, column_doc)
    blocks = ahead_first(mixed_head.reshape(tps, ctxs, own, head_size), c, 1)
    mixed = [blocks[:, 0]] + [receive(blocks[:, ctxs - j], "ctx", j) for j in range(1, ctxs)]
    mixed = jnp.concatenate([m.reshape(rows, head_size) for m in mixed], axis=1)
    attended = scatter_tp(jnp.concatenate([dot(mixed, w, (1, 1)) for w in exit_weights], axis=1))
    residual = layer_in + ahead_first(attended, lax.rem(shards - s, shards) * block, 1)

    normed_two = lower(residual * inverse_scale(residual) * gain_two)
    normed_two_all = gather_rows([normed_two], 0)[0].reshape(every, width)
    chances_all = jax.nn.softmax(dot(normed_two_all, router, (1, 0)), axis=-1)
    gates_all = jnp.where(picks_all, chances_all, 0.0)
    gates = lax.dynamic_slice_in_dim(gates_all, base, group, axis=1)
    lanes = (jnp.arange(128)[None] == base + jnp.arange(group)[:, None]).astype(F32)
    scaled, gate_parts, inner_grads, products = [], [], [], []

    def gradient_blocks(inner_grad, gated):
        own_part, far = gradient_parts(normed_two_all, cot_all, inner_grad, gated)
        return own_part, tuple(far[r * block : (r + 1) * block] for r in range(shards - 1))

    last = group - 1
    before = []
    for i in range(group):
        weights = [others] * shards if i == last else [others] if i else [first_weights]
        step = expert_step(
            i, max(i - 1, 0), normed_two_all, cot_all, weights, hidden_size, gates, lanes, *before
        )
        scaled.append(step[0])
        inner_grads.append(step[1])
        gate_parts.append(step[2])
        products.append(gradient_blocks(inner_grads[i], scaled[i]))
        before = list(products[i][1])
        if i == 1:
            shared = shared_weights(expert_in, expert_out, *before)
            before += shared
    chunks, gathered = [], []
    for i in range(last):
        own_part, far = products[i]
        chunks.append(lower(product_sum(tie(own_part, inner_grads[i + 1] if i else products[1][1][0]), far)))
        gathered.append(lax.all_gather(chunks[i], "ctx", axis=0, tiled=False))
    columns = lambda k: [(others if i else first_weights, 3 * max(i - 1, 0) + k) for i in range(group)]
    normed_part = combine(
        [(v, k) for k in range(2) for v in inner_grads], columns(0) + columns(1), gate_parts, *before
    )
    weight_swaps = lambda weights: [(w, shards - r) for w in weights for r in range(1, shards)]
    (normed_sum,), arrived = scatter_rows([normed_part.reshape(tps, ctxs, own, -1)], 1, weight_swaps(shared[:-1]))
    shared_all = [[w] + list(arrived[k * (shards - 1) : (k + 1) * (shards - 1)]) for k, w in enumerate(shared[:-1])]
    normed_sum = tie(normed_sum, gathered[0])
    normed_sum, gate_grad = normed_sum[:, :width], normed_sum[:, width : width + experts]

    router_chances = jax.nn.softmax(dot(normed_two, router, (1, 0)), axis=-1)
    chance_grad = jnp.where(picks, gate_grad, 0.0)
    logit_grad = lower(
        router_chances * (chance_grad - jnp.sum(router_chances * chance_grad, axis=-1, keepdims=True))
    )
    router_part = dot(logit_grad, normed_two, (0, 0))
    normed_grad = normed_sum + dot(logit_grad, router, (1, 1))
    residual_back, second_part = norm_back(normed_grad, residual, gain_two)
    residual_grad = upstream + residual_back

    attend_grad = gather_tp(lower(residual_grad))
    attend_blocks = [own_block(attend_grad, r, 1) for r in range(shards)]
    exit_parts = product_parts([(attend_blocks, mixed)])
    mixed_grad = lower(sum(dot(v, w, (1, 0)) for v, w in zip(attend_blocks, exit_weights)))
    mixed_grad = mixed_grad.reshape(tps, own, ctxs, head_size)
    parts = [mixed_grad[:, :, 0]] + [receive(mixed_grad[:, :, ctxs - j], "ctx", j) for j in range(1, ctxs)]
    mixed_grad = ahead_first(jnp.stack(parts, axis=1), lax.rem(ctxs - c, ctxs), 1)
    mixed_grad = mixed_grad.reshape(every, HEAD_DIM)
    projected_grad, gain_part = attend_back(
        queries, keys, values, raw, cosine, sine, head_gains, row_doc, column_doc, mixed_grad
    )
    entry_blocks = [own_block(normed_one_all, r, 1) for r in range(shards)]
    entry_parts = product_parts([(entry_blocks, projected_grad)])
    shared_gates = ahead_first(gates_all[:, last::group], c, 1)
    shared_all += [[w] + [receive(w, "shard", r) for r in range(1, shards)] for w in shared[len(shared_all) :]]
    exit_part = product_sum(*exit_parts)
    shared_products = [products[last]]
    shared_chunks = [lower(product_sum(*products[last]))]
    earlier = [exit_part, *entry_parts[1], *chunks]
    for j in range(1, ctxs):
        step = expert_step(
            j, 0, normed_two_all, cot_all, shared_all[j - 1], hidden_size, shared_gates, lanes, *earlier
        )
        parts = gradient_blocks(step[1], step[0])
        shared_products.append(parts)
        earlier = list(parts[1])
        if j == 1:
            exit_head = tie(exit_part[:, :head_size], parts[1][0])
            for r in range(1, ctxs):
                exit_head = exit_head + receive(
                    lower(exit_part[:, r * head_size : (r + 1) * head_size]), "ctx", ctxs - r
                ).astype(F32)
            earlier += [shared_chunks[0], gathered[1], *shared_all[-1][1:]]
        if j == 2:
            entry_head = product_sum(tie(entry_parts[0], parts[1][0]), entry_parts[1])
            attention_chunk = lower(jnp.concatenate([entry_head, exit_head], axis=1))
            attention_gathered = lax.all_gather(attention_chunk, "ctx", axis=0, tiled=False)

    result_part = combine([(v, 0) for v in scaled], columns(2), [], *earlier, attention_chunk)
    first_part = dot(projected_grad, head_in, (1, 1), BF16)
    tokens_wide = tokens_all.astype(F32)
    first_sum = jnp.sum(first_part.astype(F32) * tokens_wide * inverse_scale(tokens_wide), axis=0)
    head_part = gain_part[:2].reshape(1, -1)
    small_part = [jnp.sum(second_part, axis=0)[None], first_sum[None], jnp.pad(head_part, ((0, 0), (0, width - head_part.shape[1])))]
    small_part = jnp.concatenate([router_part] + small_part, axis=0)
    small_part = jnp.pad(small_part, ((0, -small_part.shape[0] % 8), (0, 0)))
    shared_chunks.append(lower(product_sum(*shared_products[1])))
    (first_normed_grad, result_sum), arrived = scatter_rows(
        [part.reshape(tps, ctxs, own, width) for part in (first_part, result_part)],
        2,
        sum([product_swaps(p[1]) for p in shared_products[2:]], []),
        shared_chunks[1],
        small=small_part,
    )
    head_gradient = sum_shard(arrived[-1][experts + 2 : experts + 3, : head_part.shape[1]], 1)[0]
    small_sum = sum_shard(arrived[-1][: experts + 2], 1)
    for k, p in enumerate(shared_products[2:]):
        shared_chunks.append(lower(product_add(p[0], arrived[k * (shards - 1) : (k + 1) * (shards - 1)])))
    layer_output = natural_rows(gather_tp(lower(residual + result_sum)))[None]
    input_back, _ = norm_back(first_normed_grad, layer_in, gain_one)
    input_gradient = natural_rows(gather_tp(lower(residual_grad + input_back))).astype(F32)[None]

    upward_gradient, downward_gradient, entry_gradient, exit_gradient = weight_gradients(
        gathered, jnp.stack(shared_chunks), attention_gathered
    )
    return (
        layer_output,
        input_gradient,
        small_sum[experts + 1],
        head_gradient,
        entry_gradient,
        exit_gradient,
        small_sum[experts],
        small_sum[:experts].T,
        upward_gradient,
        downward_gradient,
    )


def solution(mesh):
    return jax.shard_map(
        local,
        mesh=mesh,
        in_specs=(
            P("shard", "ctx", None),
            P("shard", None),
            P("shard", "ctx", None),
            P("shard", "ctx", None),
            P("shard"),
            P("shard"),
            P("shard", None, "tp"),
            P("shard", "tp"),
            P("shard"),
            P("shard", None),
            P("shard", None, None, "tp"),
            P("shard", None, "tp"),
        ),
        out_specs=(
            P("shard", "ctx", None),
            P("shard", "ctx", None),
            P("shard"),
            P("shard"),
            P("shard", None, "tp"),
            P("shard", "tp"),
            P("shard"),
            P("shard", None),
            P("shard", None, None, "tp"),
            P("shard", None, "tp"),
        ),
        check_vma=False,
    )
```
